256 devices in a mesh: outer: 64 (over y, x_lo, z), inner: 4 (over x_hi, core).
Axes of the slice: x: 4 (x_hi: 2, x_lo: 2; x = x_hi * 2 + x_lo), y: 4, z: 8, core: 2. Of those that a mesh axis runs over, the one named last changes fastest.
Arguments:
- queries: bfloat16 [4, 8192, 1024], P('inner', 'outer'), may hold values from -120 to 120
- keys: bfloat16 [4, 8192, 128], P('inner', 'outer'), may hold values from -4.5 to 4.5
- values: bfloat16 [4, 8192, 128], P('inner', 'outer'), may hold values from -5 to 5
- grad_out: bfloat16 [4, 8192, 1024], P('inner', 'outer'), may hold values from -5 to 5
- block_pos: int32 [4, 128], replicated, may hold values from 0 to 255, as said below
Outputs:
- attended: bfloat16 [4, 8192, 1024], P('inner', 'outer')
- query_grad: bfloat16 [4, 8192, 1024], P('inner', 'outer')
- key_grad: bfloat16 [4, 8192, 128], P('inner', 'outer')
- value_grad: bfloat16 [4, 8192, 128], P('inner', 'outer')
The draws below stay inside these ranges and needn't reach their ends.
Inputs may be any that keep to these rules, and one draw needn't show every extreme that they name: `block_pos`: for each sequence s, rows 2s and 2s+1 together hold each block number once. In each column pair 2o, 2o+1 of a row the first entry b is below 128 and the second is 255 - b.
All inputs are finite; a program needn't handle non-finite values.
Results may differ from the reference program's by a relative error of at most 0.035.
Values may be sent and summed in bfloat16 or wider, within the bound.
A program may use at most 128 MiB of HBM per device.

```python
import jax
import jax.numpy as jnp
from jax import lax

HEAD_DIM = 128
HEADS = 8
TOK_DEV = 128
BLK = 64
SEQS = 2
HALVES = 4
ROWS = 8192
SEQ_LEN = 16384
NBLOCKS = 256


def shared_draws(key):
    normal_part = jax.random.truncated_normal(jax.random.fold_in(key, 11), -4.5, 4.5, (HALVES * ROWS, HEAD_DIM), jnp.float32)
    return normal_part


def draw_keys(key, part):
    normal_part = shared_draws(key)
    result = normal_part
    return result.reshape(HALVES, ROWS, HEAD_DIM).astype(jnp.bfloat16)


def draw_queries(key, part):
    key = jax.random.fold_in(key, 5)
    result = 2.5 * jax.random.truncated_normal(key, -4.5, 4.5, (HALVES * ROWS, HEADS * HEAD_DIM), jnp.float32)
    return result.reshape(HALVES, ROWS, HEADS * HEAD_DIM).astype(jnp.bfloat16)


def draw_block_pos(key, part):
    key = jax.random.fold_in(key, 7)
    tables = []
    for seq_index in range(HALVES // 2):
        order = jax.random.permutation(jax.random.fold_in(key, seq_index), NBLOCKS // 2).astype(jnp.int32)
        early = order.reshape(2, NBLOCKS // 4)
        paired = jnp.stack([early, NBLOCKS - 1 - early], axis=-1)
        tables.append(paired.reshape(2, NBLOCKS // 2))
    return jnp.concatenate(tables, axis=0).astype(jnp.int32)


def block_levels(rng, shape, shards, least, high):
    level = 1.0
    for axis_at, blocks in shards:
        steps = jax.random.uniform(jax.random.fold_in(jax.random.fold_in(rng, 6), axis_at), (blocks,), jnp.float32, least / len(shards), high / len(shards))
        level = level * jnp.repeat(jnp.exp(steps), shape[axis_at] // blocks).reshape((-1,) + (1,) * (len(shape) - 1 - axis_at))
    return level


def centred(rng, extent, deviation, most, split=(), held_as=jnp.bfloat16):
    values = deviation * jax.random.normal(rng, extent, jnp.float32)
    if split:
        values = values * block_levels(rng, extent, split, -0.22, 0.18)
    return jnp.clip(values, -most, most).astype(held_as)


def setup_inputs(seed: int = 0) -> dict:
    key_of = jax.random.split(jax.random.key(seed), 6)
    return {
        "queries": draw_queries(jax.random.fold_in(key_of[5], 71), 0),
        "keys": draw_keys(jax.random.fold_in(key_of[5], 71), 0),
        "values": centred(key_of[2], (HALVES, ROWS, HEAD_DIM), 1.0, 5.0, ((0, 4), (1, 64))),
        "grad_out": centred(key_of[3], (HALVES, ROWS, HEADS * HEAD_DIM), 1.0, 5.0, ((0, 4), (1, 64))),
        "block_pos": draw_block_pos(jax.random.fold_in(key_of[5], 71), 0),
    }


NEG_FILL = -1e30


def reference(queries, keys, values, grad_out, block_pos):
    score_scale = HEAD_DIM ** -0.5
    offsets = jnp.arange(BLK, dtype=jnp.int32)
    key_places = jnp.arange(SEQ_LEN, dtype=jnp.int32)
    block_total = SEQ_LEN // TOK_DEV
    outs_attended = []
    outs_qgrad = []
    outs_kgrad = []
    outs_vgrad = []
    for seq_index in range(SEQS):
        first = 2 * seq_index
        query_all = queries[first:first + 2].reshape(SEQ_LEN, HEADS * HEAD_DIM)
        grad_all = grad_out[first:first + 2].reshape(SEQ_LEN, HEADS * HEAD_DIM)
        key_all = keys[first:first + 2].reshape(SEQ_LEN, HEAD_DIM)
        value_all = values[first:first + 2].reshape(SEQ_LEN, HEAD_DIM)
        places = (block_pos[first:first + 2][..., None] * BLK + offsets).reshape(SEQ_LEN).astype(jnp.int32)
        inverse = jnp.zeros((SEQ_LEN,), jnp.int32).at[places].set(jnp.arange(SEQ_LEN, dtype=jnp.int32))
        key_sorted = key_all[inverse]
        value_sorted = value_all[inverse]
        query_blocks = query_all[inverse].reshape(block_total, TOK_DEV * HEADS, HEAD_DIM)
        grad_blocks = grad_all[inverse].reshape(block_total, TOK_DEV * HEADS, HEAD_DIM)
        place_blocks = jnp.repeat(key_places, HEADS).reshape(block_total, TOK_DEV * HEADS)

        def one_block(carried, inputs):
            key_grad, value_grad = carried
            query_rows, grad_rows, query_places = inputs
            scores = jnp.dot(query_rows, key_sorted.T, preferred_element_type=jnp.float32) * score_scale
            visible = key_places[None, :] <= query_places[:, None]
            scores = jnp.where(visible, scores, NEG_FILL)
            maxima = jnp.max(scores, axis=1)
            weights = jnp.where(visible, jnp.exp(scores - maxima[:, None]), 0.0)
            totals = jnp.sum(weights, axis=1)
            attended = (jnp.dot(weights.astype(jnp.bfloat16), value_sorted, preferred_element_type=jnp.float32) / totals[:, None]).astype(jnp.bfloat16)
            log_totals = maxima + jnp.log(totals)
            deltas = jnp.sum(grad_rows.astype(jnp.float32) * attended.astype(jnp.float32), axis=1)
            probs = jnp.where(visible, jnp.exp(scores - log_totals[:, None]), 0.0)
            grad_probs = jnp.dot(grad_rows, value_sorted.T, preferred_element_type=jnp.float32)
            grad_scores = (probs * (grad_probs - deltas[:, None])).astype(jnp.bfloat16)
            query_grad = (jnp.dot(grad_scores, key_sorted, preferred_element_type=jnp.float32) * score_scale).astype(jnp.bfloat16)
            key_grad = key_grad + jnp.dot(grad_scores.T, query_rows, preferred_element_type=jnp.float32)
            value_grad = value_grad + jnp.dot(probs.astype(jnp.bfloat16).T, grad_rows, preferred_element_type=jnp.float32)
            return (key_grad, value_grad), (attended, query_grad)

        initial = (jnp.zeros((SEQ_LEN, HEAD_DIM), jnp.float32), jnp.zeros((SEQ_LEN, HEAD_DIM), jnp.float32))
        (key_grad, value_grad), (attended, query_grad) = lax.scan(one_block, initial, (query_blocks, grad_blocks, place_blocks))
        attended = attended.reshape(SEQ_LEN, HEADS * HEAD_DIM)[places]
        query_grad = query_grad.reshape(SEQ_LEN, HEADS * HEAD_DIM)[places]
        key_grad = (key_grad * score_scale).astype(jnp.bfloat16)[places]
        value_grad = value_grad.astype(jnp.bfloat16)[places]
        outs_attended.append(attended.reshape(2, ROWS, HEADS * HEAD_DIM))
        outs_qgrad.append(query_grad.reshape(2, ROWS, HEADS * HEAD_DIM))
        outs_kgrad.append(key_grad.reshape(2, ROWS, HEAD_DIM))
        outs_vgrad.append(value_grad.reshape(2, ROWS, HEAD_DIM))
    return (jnp.concatenate(outs_attended, axis=0), jnp.concatenate(outs_qgrad, axis=0), jnp.concatenate(outs_kgrad, axis=0), jnp.concatenate(outs_vgrad, axis=0))
```

```python
import jax
import jax.numpy as jnp
from jax import lax
from jax.experimental import pallas as pl
from jax.experimental.pallas import tpu as pltpu
from jax.sharding import PartitionSpec as P

MESH = pl.DeviceIdType.MESH
NEG = -1e30
BIG = 1e30
BLK = 64
DIM = 128
HEADS = 8
ROWS = BLK * HEADS
CHUNKS = 16
SCALE = DIM**-0.5
C2 = SCALE * 1.4426950408889634

YORDER = (0, -1, 1, 2)
NEAR = (0, -1, 1, -2)
FAR = (2, -3, 3, 4)


def a_chunk(dz):
    return [(0, dy, dz) for dy in YORDER]


def b_chunk(dy, part):
    return [(1, dy, dz) for dz in part]


TABLE = [
    a_chunk(0),
    a_chunk(-1),
    a_chunk(1),
    b_chunk(0, NEAR),
    b_chunk(0, FAR),
    b_chunk(-1, NEAR),
    b_chunk(1, NEAR),
    a_chunk(-2),
    a_chunk(2),
    b_chunk(-1, FAR),
    b_chunk(1, FAR),
    a_chunk(-3),
    a_chunk(3),
    b_chunk(2, NEAR),
    b_chunk(2, FAR),
    a_chunk(4),
]


def nt(a, b):
    return lax.dot_general(a, b, (((1,), (0,)), ((), ())), preferred_element_type=jnp.float32)


def tn(a, b):
    return lax.dot_general(a, b, (((0,), (0,)), ((), ())), preferred_element_type=jnp.float32)


def row_sum(x):
    return jnp.sum(x, axis=0, keepdims=True)


def row_max(x):
    return jnp.max(x, axis=0, keepdims=True)


def kernel(
    pos,
    q_ref,
    k_ref,
    v_ref,
    g_ref,
    att_ref,
    dq_ref,
    dk_ref,
    dv_ref,
    buf,
    own,
    pq,
    pg,
    qn,
    gn,
    qt,
    gt,
    ot,
    dqt,
    stat,
    pstat,
    lse,
    pot,
    pdq,
    tf,
    snd,
    r1,
    r2,
    sy,
    ry,
    sz,
    rz,
    xs,
    rx,
    dg,
    kt,
    lsem,
    ssem,
    rsem,
):
    outer = lax.axis_index("outer")
    inner = lax.axis_index("inner")
    yy = outer // 16
    xx = (outer // 8) % 2
    zz = outer % 8
    mate = inner + 1 - 2 * (inner % 2)

    def at(x, dy, dz):
        return (((yy + dy + 4) % 4) * 2 + x) * 8 + (zz + dz + 8) % 8

    yp, ym = (at(xx, 1, 0), inner), (at(xx, -1, 0), inner)
    zp, zm = (at(xx, 0, 1), inner), (at(xx, 0, -1), inner)
    xp = (at(1 - xx, 0, 0), inner)
    cp = (outer, mate)

    barrier = pltpu.get_barrier_semaphore()
    for dev in (yp, ym, zp, zm, xp, cp):
        pl.semaphore_signal(barrier, inc=1, device_id=dev, device_id_type=MESH)

    for w, k in enumerate((k_ref, v_ref)):
        own[2 * w] = k[0:BLK, :]
        own[2 * w + 1] = k[BLK : 2 * BLK, :]
    pl.semaphore_wait(barrier, 6)

    msgs = {}

    def msg(name, src, dst, dev):
        at_sem = len(msgs)
        msgs[name] = pltpu.make_async_remote_copy(
            src_ref=src,
            dst_ref=dst,
            send_sem=ssem.at[at_sem],
            recv_sem=rsem.at[at_sem],
            device_id=dev,
            device_id_type=MESH,
        )

    def go(*names):
        for name in names:
            msgs[name].start()

    def got(*names):
        for name in names:
            msgs[name].wait_recv()

    msg("x", own, buf.at[3 * xx, 0], xp)
    msg("q", q_ref, pq, cp)
    msg("g", g_ref, pg, cp)
    msg("ay1", buf.at[0, 0], buf.at[0, 1], yp)
    msg("ay2", buf.at[0, 0], buf.at[0, 2], ym)
    msg("ay3", buf.at[0, 1], buf.at[0, 3], yp)
    for w in range(4):
        msg("azp%d" % w, buf.at[0, w], buf.at[1, w], zp)
        msg("azm%d" % w, buf.at[0, w], buf.at[2, w], zm)
        msg("byp%d" % w, buf.at[3, w], buf.at[5, w], yp)
        msg("bym%d" % w, buf.at[3, w], buf.at[6, w], ym)
    msg("a7", buf.at[1], buf.at[7], zp)
    msg("a8", buf.at[2], buf.at[8], zm)
    msg("a11", buf.at[7], buf.at[11], zp)
    msg("a12", buf.at[8], buf.at[12], zm)
    msg("a15p", buf.at[11, pl.ds(0, 2)], buf.at[15, pl.ds(0, 2)], zp)
    msg("a15m", buf.at[12, pl.ds(2, 2)], buf.at[15, pl.ds(2, 2)], zm)
    msg("bz1", buf.at[3, 0], buf.at[3, 1], zp)
    msg("bz2", buf.at[3, 0], buf.at[3, 2], zm)
    msg("bz3", buf.at[3, 1], buf.at[3, 3], zp)
    msg("bz4", buf.at[3, 2], buf.at[4, 0], zm)
    msg("bz5", buf.at[3, 3], buf.at[4, 1], zp)
    msg("bz6", buf.at[4, 0], buf.at[4, 2], zm)
    msg("bz7", buf.at[4, 1], buf.at[4, 3], zp)
    msg("b9", buf.at[4], buf.at[9], yp)
    msg("b10", buf.at[4], buf.at[10], ym)
    msg("b13", buf.at[5], buf.at[13], yp)
    msg("b14", buf.at[10], buf.at[14], ym)
    msg("stat", stat, pstat, cp)
    msg("ot", ot.at[1], pot, cp)
    msg("dq", dqt.at[1], pdq, cp)
    msg("r15m", snd.at[15, pl.ds(0, 2)], r1.at[11, pl.ds(0, 2)], zm)
    msg("r15p", snd.at[15, pl.ds(2, 2)], r1.at[12, pl.ds(2, 2)], zp)
    msg("r11", snd.at[11], r1.at[7], zm)
    msg("r12", snd.at[12], r1.at[8], zp)
    msg("r7", snd.at[7], r1.at[1], zm)
    msg("r8", snd.at[8], r1.at[2], zp)
    msg("r1", snd.at[1], r1.at[0], zm)
    msg("r2", snd.at[2], r2.at[0], zp)
    msg("r13", snd.at[13], r1.at[5], ym)
    msg("r14", snd.at[14], r1.at[10], yp)
    msg("r5", snd.at[5], r1.at[3], ym)
    msg("r9", snd.at[9], r1.at[4], ym)
    msg("r6", snd.at[6], r2.at[1], yp)
    msg("r10", snd.at[10], r2.at[2], yp)
    for n, dev in enumerate((ym, ym, yp)):
        msg("ry%d" % n, sy.at[n], ry.at[n], dev)
    for n, dev in enumerate((zm, zm, zm, zm, zp, zp, zp)):
        msg("rz%d" % n, sz.at[n], rz.at[n], dev)
    msg("rx", xs, rx, xp)

    go("x", "q", "g")
    local = pltpu.make_async_copy(own, buf.at[3 * xx, 0], lsem)
    local.start()

    ql = [pos[inner, 2 * outer], pos[mate, 2 * outer]]
    for c in range(CHUNKS):
        for w in range(4):
            t, dy, dz = TABLE[c][w]
            kt[4 * c + w] = pos[inner, 2 * at(t, dy, dz)]

    def spread(p, src, rows, cols):
        for h in range(HEADS):
            lanes = slice(h * DIM, (h + 1) * DIM)
            rows[p, h * BLK : (h + 1) * BLK, 0:DIM] = src[0:BLK, lanes]
            rows[p, h * BLK : (h + 1) * BLK, DIM : 2 * DIM] = src[BLK : 2 * BLK, lanes]
        cols[p] = rows[p].T

    spread(0, q_ref, qn, qt)
    local.wait()
    pltpu.make_async_remote_copy(
        src_ref=own,
        dst_ref=buf.at[3 - 3 * xx, 0],
        send_sem=ssem.at[0],
        recv_sem=rsem.at[0],
        device_id=xp,
        device_id_type=MESH,
    ).wait_recv()
    go("azp0", "azm0", "ay1", "ay2", "bz1", "bz2", "byp0", "bym0")

    got("q")
    spread(1, pq, qn, qt)
    got("ay1", "ay2", "bz1", "bz2")
    go("ay3", "azp1", "azm1", "azp2", "azm2", "bz3", "bz4", "byp1", "bym1", "byp2", "bym2")

    tok_k = lax.broadcasted_iota(jnp.int32, (BLK, ROWS), 0)
    tok_q = lax.broadcasted_iota(jnp.int32, (BLK, ROWS), 1) % BLK
    diag = tok_k <= tok_q
    for lh in range(2):
        s = jnp.where(diag, nt(own[lh], qt[0, lh * DIM : (lh + 1) * DIM]), NEG)
        m = row_max(s)
        p = jnp.exp2((s - m) * C2)
        stat[lh : lh + 1] = m
        stat[4 + lh : 5 + lh] = row_sum(p)
        ot[0, lh * DIM : (lh + 1) * DIM] = tn(own[2 + lh], p.astype(jnp.bfloat16))
    stat[2:4] = jnp.full((2, ROWS), NEG, jnp.float32)
    stat[6:8] = jnp.zeros((2, ROWS), jnp.float32)
    stat[12:16] = jnp.zeros((4, ROWS), jnp.float32)
    ot[1] = jnp.zeros((2 * DIM, ROWS), jnp.float32)

    got("ay3", "bz3", "bz4")
    go("azp3", "azm3", "bz5", "bz6", "byp3", "bym3")
    for c in (6, 9, 13, 14, 15):
        r1[c] = jnp.zeros((4, 4, BLK, DIM), jnp.bfloat16)
    r1[11, 2:4] = jnp.zeros((2, 4, BLK, DIM), jnp.bfloat16)
    r1[12, 0:2] = jnp.zeros((2, 4, BLK, DIM), jnp.bfloat16)

    def take(c):
        return [buf[c, :, kind].reshape(4 * BLK, DIM) for kind in range(4)]

    def picks(c, p):
        number = [kt[4 * c + w] for w in range(4)]
        return [n < ql[p] for n in number], [n == ql[p] for n in number]

    def cat(low, high, chosen):
        zero = jnp.zeros((BLK, DIM), jnp.bfloat16)
        rows = []
        for w in range(4):
            a, b = low[w * BLK : (w + 1) * BLK], high[w * BLK : (w + 1) * BLK]
            rows.append(
                jnp.concatenate(
                    [lax.select(chosen[w], a, zero), lax.select(chosen[w], zero, b)], axis=1
                )
            )
        return jnp.concatenate(rows, axis=0)

    neg_row = jnp.full((1, ROWS), NEG, jnp.float32)
    big_row = jnp.full((1, ROWS), BIG, jnp.float32)

    def windows(x):
        return [x[w * BLK : (w + 1) * BLK] for w in range(4)]

    def arrive(c):
        def do(at_chunk, *steps):
            @pl.when(c == at_chunk)
            def _():
                for step, names in steps:
                    step(*names)

        do(1, (got, ["azp%d" % w for w in range(4)]), (go, ["a7"]), (got, ["bz5", "bz6"]), (go, ["bz7"]))
        do(2, (got, ["azm%d" % w for w in range(4)]), (go, ["a8"]))
        do(4, (got, ["bz7"]), (go, ["b9", "b10"]))
        do(5, (got, ["byp%d" % w for w in range(4)]), (go, ["b13"]))
        do(6, (got, ["bym%d" % w for w in range(4)]))
        do(7, (got, ["a7"]), (go, ["a11"]))
        do(8, (got, ["a8"]), (go, ["a12"]))
        do(9, (got, ["b9"]))
        do(10, (got, ["b10"]), (go, ["b14"]))
        do(11, (got, ["a11"]), (go, ["a15p"]))
        do(12, (got, ["a12"]), (go, ["a15m"]))
        do(13, (got, ["b13"]))
        do(14, (got, ["b14"]))
        do(15, (got, ["a15p", "a15m"]))

    def forward(c, carry):
        arrive(c)
        kl, kh, vl, vh = take(c)
        for p in range(2):
            low, same = picks(c, p)
            kcat, vcat = cat(kl, kh, low), cat(vl, vh, low)
            s1 = nt(kl, qt[p, DIM : 2 * DIM])
            s2 = windows(nt(kcat, qt[p]))
            rl, rh = 2 * p, 2 * p + 1
            ml, mh = stat[rl : rl + 1], stat[rh : rh + 1]
            nl, nh = ml, jnp.maximum(mh, row_max(s1))
            for w in range(4):
                top = row_max(s2[w])
                nl = jnp.maximum(nl, lax.select(low[w], top, neg_row))
                nh = jnp.maximum(nh, lax.select(low[w] | same[w], neg_row, top))
            fl, fh = jnp.exp2((ml - nl) * C2), jnp.exp2((mh - nh) * C2)
            p1 = jnp.exp2((s1 - nh) * C2)
            tl, th = stat[4 + rl : 5 + rl] * fl, stat[4 + rh : 5 + rh] * fh + row_sum(p1)
            parts = []
            for w in range(4):
                ref = lax.select(same[w], big_row, lax.select(low[w], nl, nh))
                part = jnp.exp2((s2[w] - ref) * C2)
                total = row_sum(part)
                zero = jnp.zeros_like(total)
                tl = tl + lax.select(low[w], total, zero)
                th = th + lax.select(low[w], zero, total)
                parts.append(part.astype(jnp.bfloat16))
            stat[rl : rl + 1], stat[rh : rh + 1] = nl, nh
            stat[4 + rl : 5 + rl], stat[4 + rh : 5 + rh] = tl, th
            o1 = tn(vl, p1.astype(jnp.bfloat16))
            o2 = tn(vcat, jnp.concatenate(parts, axis=0))
            ot[p, 0:DIM] = ot[p, 0:DIM] * fl + o2[0:DIM]
            ot[p, DIM : 2 * DIM] = ot[p, DIM : 2 * DIM] * fh + (o1 + o2[DIM : 2 * DIM])
        return carry

    lax.fori_loop(0, CHUNKS, forward, 0)

    go("ot")
    spread(0, g_ref, gn, gt)
    got("g")
    spread(1, pg, gn, gt)
    for p in range(2):
        for lh in range(2):
            r = 2 * p + lh
            rows = slice(lh * DIM, (lh + 1) * DIM)
            stat[8 + r : 9 + r] = row_sum(ot[p, rows] * gt[p, rows].astype(jnp.float32))
    go("stat")
    got("stat")
    scale_mine, scale_other = [], []
    for p in range(2):
        for lh in range(2):
            r, other = 2 * p + lh, 2 * (1 - p) + lh
            ma, mb = stat[r : r + 1], pstat[other : other + 1]
            top = jnp.maximum(ma, mb)
            fa, fb = jnp.exp2((ma - top) * C2), jnp.exp2((mb - top) * C2)
            total = stat[4 + r : 5 + r] * fa + pstat[4 + other : 5 + other] * fb
            delta = stat[8 + r : 9 + r] * fa + pstat[8 + other : 9 + other] * fb
            lse[r : r + 1] = top + jnp.log(total) * (1.0 / SCALE)
            lse[4 + r : 5 + r] = delta / total
            if p == 0:
                scale_mine.append(fa / total)
                scale_other.append(fb / total)
    for lh in range(2):
        lse[8 + 2 * lh : 9 + 2 * lh] = scale_mine[lh]
        lse[9 + 2 * lh : 10 + 2 * lh] = scale_other[lh]

    dqt[1] = jnp.zeros((2 * DIM, ROWS), jnp.float32)
    for lh in range(2):
        rows = slice(lh * DIM, (lh + 1) * DIM)
        s = jnp.where(diag, nt(own[lh], qt[0, rows]), NEG)
        p = jnp.exp2((s - lse[lh : lh + 1]) * C2)
        ds = (p * (nt(own[2 + lh], gt[0, rows]) - lse[4 + lh : 5 + lh])).astype(jnp.bfloat16)
        dg[lh] = nt(ds, qn[0, :, rows])
        dg[2 + lh] = nt(p.astype(jnp.bfloat16), gn[0, :, rows])
        dqt[0, rows] = tn(own[lh], ds)

    def backward(step, carry):
        c = CHUNKS - 1 - step
        kl, kh, vl, vh = take(c)
        sums = None
        for p in range(2):
            low, same = picks(c, p)
            kcat, vcat = cat(kl, kh, low), cat(vl, vh, low)
            rl, rh = 2 * p, 2 * p + 1
            high = slice(DIM, 2 * DIM)
            p1 = jnp.exp2((nt(kl, qt[p, high]) - lse[rh : rh + 1]) * C2)
            ds1 = (p1 * (nt(vl, gt[p, high]) - lse[4 + rh : 5 + rh])).astype(jnp.bfloat16)
            s2 = windows(nt(kcat, qt[p]))
            g2 = windows(nt(vcat, gt[p]))
            ps, ds = [], []
            for w in range(4):
                ref = lax.select(
                    same[w], big_row, lax.select(low[w], lse[rl : rl + 1], lse[rh : rh + 1])
                )
                delta = lax.select(low[w], lse[4 + rl : 5 + rl], lse[4 + rh : 5 + rh])
                part = jnp.exp2((s2[w] - ref) * C2)
                ps.append(part.astype(jnp.bfloat16))
                ds.append((part * (g2[w] - delta)).astype(jnp.bfloat16))
            p2, ds2 = jnp.concatenate(ps, axis=0), jnp.concatenate(ds, axis=0)
            dqt[p, high] = dqt[p, high] + tn(kl, ds1)
            dqt[p] = dqt[p] + tn(kcat, ds2)
            ones = [nt(ds1, qn[p, :, high]), nt(p1.astype(jnp.bfloat16), gn[p, :, high])]
            twos = [nt(ds2, qn[p]), nt(p2, gn[p])]
            new = []
            for one, two in zip(ones, twos):
                zero = jnp.zeros((BLK, DIM), jnp.float32)
                lows, highs = [], []
                for w in range(4):
                    rows = slice(w * BLK, (w + 1) * BLK)
                    lows.append(one[rows] + lax.select(low[w], two[rows, 0:DIM], zero))
                    highs.append(lax.select(low[w], zero, two[rows, DIM : 2 * DIM]))
                new += [lows, highs]
            if sums is None:
                sums = new
            else:
                sums = [[a + b for a, b in zip(x, y)] for x, y in zip(sums, new)]
        for kind in range(4):
            for w in range(4):
                tf[c, w, kind] = sums[kind][w]

        def before(at_chunk, *names):
            @pl.when(c == at_chunk)
            def _():
                got(*names)

        before(11, "r15m")
        before(12, "r15p")
        before(7, "r11")
        before(8, "r12")
        before(1, "r7")
        before(2, "r8")
        before(5, "r13")
        before(10, "r14")

        @pl.when((c != 0) & (c != 3) & (c != 4))
        def _():
            snd[c] = (tf[c] + r1[c].astype(jnp.float32)).astype(jnp.bfloat16)

        def after(at_chunk, *names):
            @pl.when(c == at_chunk)
            def _():
                go(*names)

        after(15, "r15m", "r15p")
        for at_chunk in (11, 12, 7, 8, 1, 2, 13, 14, 5, 9, 6, 10):
            after(at_chunk, "r%d" % at_chunk)

        @pl.when(c == 2)
        def _():
            got("r9", "r10", "r5", "r6")
            chain(4, None, 0)
            chain(3, None, 4)

        @pl.when(c == 1)
        def _():
            chain(-3, 0, 1)
            chain(2, 4, 5)

        return carry

    def b_total(dz, *arrived):
        for c in (3, 4):
            for w in range(4):
                if TABLE[c][w][2] == dz:
                    total = tf[c, w] + r1[c, w].astype(jnp.float32)
                    total = total + r2[c - 2, w].astype(jnp.float32)
        for n in arrived:
            got("rz%d" % n)
            total = total + rz[n].astype(jnp.float32)
        return total

    def chain(dz, arrived, leaving):
        total = b_total(dz) if arrived is None else b_total(dz, arrived)
        sz[leaving] = total.astype(jnp.bfloat16)
        go("rz%d" % leaving)

    def a_total(w, *arrived):
        total = tf[0, w] + r1[0, w].astype(jnp.float32) + r2[0, w].astype(jnp.float32)
        for n in arrived:
            got("ry%d" % n)
            total = total + ry[n].astype(jnp.float32)
        return total

    def a_send(w, leaving, *arrived):
        sy[leaving] = a_total(w, *arrived).astype(jnp.bfloat16)
        go("ry%d" % leaving)

    lax.fori_loop(0, CHUNKS, backward, 0)

    go("dq")
    chain(-2, 1, 2)
    chain(1, 5, 6)
    got("r1", "r2")
    a_send(3, 0)
    a_send(2, 2)

    def store(ref, rows):
        for h in range(HEADS):
            lanes = slice(h * DIM, (h + 1) * DIM)
            ref[0:BLK, lanes] = rows[h * BLK : (h + 1) * BLK, 0:DIM]
            ref[BLK : 2 * BLK, lanes] = rows[h * BLK : (h + 1) * BLK, DIM : 2 * DIM]

    got("ot")
    halves = []
    for lh in range(2):
        rows = slice(lh * DIM, (lh + 1) * DIM)
        halves.append(
            ot[0, rows] * lse[8 + 2 * lh : 9 + 2 * lh] + pot[rows] * lse[9 + 2 * lh : 10 + 2 * lh]
        )
    store(att_ref, jnp.concatenate(halves, axis=0).T.astype(jnp.bfloat16))

    chain(-1, 2, 3)
    a_send(1, 1, 0)
    got("dq")
    store(dq_ref, ((dqt[0] + pdq[...]) * SCALE).T.astype(jnp.bfloat16))

    total_b = b_total(0, 3, 6)
    total_a = a_total(0, 1, 2)
    first = xx == 0
    xs[...] = lax.select(first, total_b, total_a).astype(jnp.bfloat16)
    go("rx")
    mine = lax.select(first, total_a, total_b) + dg[...]
    got("rx")
    mine = mine + rx[...].astype(jnp.float32)
    for lh in range(2):
        rows = slice(lh * BLK, (lh + 1) * BLK)
        dk_ref[rows, :] = (mine[lh] * SCALE).astype(jnp.bfloat16)
        dv_ref[rows, :] = mine[2 + lh].astype(jnp.bfloat16)
    for copy in msgs.values():
        copy.wait_send()


def body(queries, keys, values, grad_out, block_pos):
    vmem = pl.BlockSpec(memory_space=pltpu.VMEM)
    bf, f32 = jnp.bfloat16, jnp.float32
    window = (4, BLK, DIM)
    count = 80
    outs = pl.pallas_call(
        kernel,
        out_shape=[
            jax.ShapeDtypeStruct((2 * BLK, HEADS * DIM), bf),
            jax.ShapeDtypeStruct((2 * BLK, HEADS * DIM), bf),
            jax.ShapeDtypeStruct((2 * BLK, DIM), bf),
            jax.ShapeDtypeStruct((2 * BLK, DIM), bf),
        ],
        in_specs=[pl.BlockSpec(memory_space=pltpu.SMEM)] + [vmem] * 4,
        out_specs=[vmem] * 4,
        scratch_shapes=[
            pltpu.VMEM((CHUNKS, 4) + window, bf),
            pltpu.VMEM(window, bf),
            pltpu.VMEM((2 * BLK, HEADS * DIM), bf),
            pltpu.VMEM((2 * BLK, HEADS * DIM), bf),
            pltpu.VMEM((2, ROWS, 2 * DIM), bf),
            pltpu.VMEM((2, ROWS, 2 * DIM), bf),
            pltpu.VMEM((2, 2 * DIM, ROWS), bf),
            pltpu.VMEM((2, 2 * DIM, ROWS), bf),
            pltpu.VMEM((2, 2 * DIM, ROWS), f32),
            pltpu.VMEM((2, 2 * DIM, ROWS), f32),
            pltpu.VMEM((16, ROWS), f32),
            pltpu.VMEM((16, ROWS), f32),
            pltpu.VMEM((16, ROWS), f32),
            pltpu.VMEM((2 * DIM, ROWS), f32),
            pltpu.VMEM((2 * DIM, ROWS), f32),
            pltpu.VMEM((CHUNKS, 4) + window, f32),
            pltpu.VMEM((CHUNKS, 4) + window, bf),
            pltpu.VMEM((CHUNKS, 4) + window, bf),
            pltpu.VMEM((3, 4) + window, bf),
            pltpu.VMEM((3,) + window, bf),
            pltpu.VMEM((3,) + window, bf),
            pltpu.VMEM((7,) + window, bf),
            pltpu.VMEM((7,) + window, bf),
            pltpu.VMEM(window, bf),
            pltpu.VMEM(window, bf),
            pltpu.VMEM(window, f32),
            pltpu.SMEM((4 * CHUNKS,), jnp.int32),
            pltpu.SemaphoreType.DMA,
            pltpu.SemaphoreType.DMA((count,)),
            pltpu.SemaphoreType.DMA((count,)),
        ],
        compiler_params=pltpu.CompilerParams(
            collective_id=0, has_side_effects=True, vmem_limit_bytes=52 * 1024 * 1024
        ),
        name="attention",
    )(block_pos, queries[0], keys[0], values[0], grad_out[0])
    return tuple(out[None] for out in outs)


def solution(mesh):
    spec = P("inner", "outer", None)
    return jax.shard_map(
        body,
        mesh=mesh,
        in_specs=(spec, spec, spec, spec, P()),
        out_specs=(spec, spec, spec, spec),
        check_vma=False,
    )
```

```python
import jax
import jax.numpy as jnp
from jax import lax
from jax.experimental import pallas as pl
from jax.experimental.pallas import tpu as pltpu
from jax.sharding import PartitionSpec as P

MESH = pl.DeviceIdType.MESH
NEG = -1e30
BIG = 1e30
BLK = 64
HALF = 32
DIM = 128
HEADS = 8
ROWS = BLK * HEADS
CHUNKS = 16
STEPS = 8
KEYS = 8 * HALF
SCALE = DIM**-0.5
C2 = SCALE * 1.4426950408889634

YORDER = (0, -1, 1, 2)
NEAR = (0, -1, 1, -2)
FAR = (2, -3, 3, 4)


def a_chunk(dz):
    return [(dy, dz) for dy in YORDER]


def b_chunk(dy, part):
    return [(dy, dz) for dz in part]


TABLE = [
    a_chunk(0),
    b_chunk(0, NEAR),
    a_chunk(-1),
    a_chunk(1),
    b_chunk(0, FAR),
    b_chunk(-1, NEAR),
    b_chunk(1, NEAR),
    a_chunk(-2),
    a_chunk(2),
    b_chunk(-1, FAR),
    b_chunk(1, FAR),
    a_chunk(-3),
    a_chunk(3),
    b_chunk(2, NEAR),
    b_chunk(2, FAR),
    a_chunk(4),
]


def nt(a, b):
    return lax.dot_general(a, b, (((1,), (0,)), ((), ())), preferred_element_type=jnp.float32)


def tn(a, b):
    return lax.dot_general(a, b, (((0,), (0,)), ((), ())), preferred_element_type=jnp.float32)


def fold(x, op):
    rows, lanes = x.shape
    return op(x.reshape(rows // 8, 8, lanes), axis=0)


def row_sum(x):
    return jnp.sum(x, axis=0, keepdims=True)


def row_max(x):
    return jnp.max(x, axis=0, keepdims=True)


def kernel(
    pos_ref,
    q_ref,
    k_ref,
    v_ref,
    g_ref,
    att_ref,
    dq_ref,
    dk_ref,
    dv_ref,
    buf,
    mq,
    mg,
    pq,
    pg,
    qn,
    gn,
    qt,
    gt,
    ot,
    dqt,
    stat,
    ls,
    pstat,
    lse,
    mc,
    wt,
    pot,
    pd,
    xd,
    px,
    tf,
    snd,
    r1,
    r2,
    sy,
    ry,
    sz,
    rz,
    dg,
    pos,
    kt,
    lsem,
    ssem,
    rsem,
):
    outer = lax.axis_index("outer")
    inner = lax.axis_index("inner")
    yy = outer // 16
    xx = (outer // 8) % 2
    zz = outer % 8
    mate = inner + 1 - 2 * (inner % 2)

    def at(x, dy, dz):
        return (((yy + dy + 4) % 4) * 2 + x) * 8 + (zz + dz + 8) % 8

    beside = at(1 - xx, 0, 0)
    yp, ym = (at(xx, 1, 0), inner), (at(xx, -1, 0), inner)
    zp, zm = (at(xx, 0, 1), inner), (at(xx, 0, -1), inner)
    cp, xp, dp = (outer, mate), (beside, inner), (beside, mate)

    barrier = pltpu.get_barrier_semaphore()
    for dev in (yp, ym, zp, zm, cp, xp, dp):
        pl.semaphore_signal(barrier, inc=1, device_id=dev, device_id_type=MESH)

    fetch = [
        pltpu.make_async_copy(pos_ref, pos, lsem.at[0]),
        pltpu.make_async_copy(q_ref, mq, lsem.at[1]),
        pltpu.make_async_copy(g_ref, mg, lsem.at[2]),
    ]
    pieces = []
    for n, ref in enumerate((k_ref, v_ref)):
        for lh in range(2):
            for half in range(2):
                pieces.append(
                    pltpu.make_async_copy(
                        ref.at[pl.ds(lh * BLK + half * HALF, HALF)],
                        buf.at[half, 0, 2 * n + lh],
                        lsem.at[3 + len(pieces)],
                    )
                )
    for copy in pieces + fetch:
        copy.start()
    pl.semaphore_wait(barrier, 7)

    msgs = {}

    def msg(name, src, dst, dev):
        at_sem = len(msgs)
        msgs[name] = pltpu.make_async_remote_copy(
            src_ref=src,
            dst_ref=dst,
            send_sem=ssem.at[at_sem],
            recv_sem=rsem.at[at_sem],
            device_id=dev,
            device_id_type=MESH,
        )

    def go(*names):
        for name in names:
            msgs[name].start()

    def got(*names):
        for name in names:
            msgs[name].wait_recv()

    for name, src, dst in (("q", q_ref, pq), ("g", g_ref, pg)):
        msg(name + "1", src, dst.at[0], cp)
        msg(name + "2", src, dst.at[1], xp)
        msg(name + "3", dst.at[1], dst.at[2], cp)
    msg("ay1", buf.at[0, 0], buf.at[0, 1], yp)
    msg("ay2", buf.at[0, 0], buf.at[0, 2], ym)
    msg("ay3", buf.at[0, 1], buf.at[0, 3], yp)
    for w in range(4):
        msg("azp%d" % w, buf.at[0, w], buf.at[2, w], zp)
        msg("azm%d" % w, buf.at[0, w], buf.at[3, w], zm)
        msg("byp%d" % w, buf.at[1, w], buf.at[5, w], yp)
        msg("bym%d" % w, buf.at[1, w], buf.at[6, w], ym)
    msg("a7", buf.at[2], buf.at[7], zp)
    msg("a8", buf.at[3], buf.at[8], zm)
    msg("a11", buf.at[7], buf.at[11], zp)
    msg("a12", buf.at[8], buf.at[12], zm)
    msg("a15p", buf.at[11, pl.ds(0, 2)], buf.at[15, pl.ds(0, 2)], zp)
    msg("a15m", buf.at[12, pl.ds(2, 2)], buf.at[15, pl.ds(2, 2)], zm)
    msg("bz1", buf.at[1, 0], buf.at[1, 1], zp)
    msg("bz2", buf.at[1, 0], buf.at[1, 2], zm)
    msg("bz3", buf.at[1, 1], buf.at[1, 3], zp)
    msg("bz4", buf.at[1, 2], buf.at[4, 0], zm)
    msg("bz5", buf.at[1, 3], buf.at[4, 1], zp)
    msg("bz6", buf.at[4, 0], buf.at[4, 2], zm)
    msg("bz7", buf.at[4, 1], buf.at[4, 3], zp)
    msg("b9", buf.at[4], buf.at[9], yp)
    msg("b10", buf.at[4], buf.at[10], ym)
    msg("b13", buf.at[5], buf.at[13], yp)
    msg("b14", buf.at[10], buf.at[14], ym)
    for n, dev in enumerate((cp, xp, dp)):
        msg("stat%d" % n, stat, pstat.at[n], dev)
    for n, dev in enumerate((cp, xp, dp)):
        msg("ot%d" % n, ot.at[n + 1], pot.at[n], dev)
    msg("dq3", dqt.at[3], pd.at[0], cp)
    msg("dq2", xd, px, xp)
    msg("dq1", dqt.at[1], pd.at[1], cp)
    msg("r15m", snd.at[15, pl.ds(0, 2)], r1.at[11, pl.ds(0, 2)], zm)
    msg("r15p", snd.at[15, pl.ds(2, 2)], r1.at[12, pl.ds(2, 2)], zp)
    msg("r11", snd.at[11], r1.at[7], zm)
    msg("r12", snd.at[12], r1.at[8], zp)
    msg("r7", snd.at[7], r1.at[2], zm)
    msg("r8", snd.at[8], r1.at[3], zp)
    msg("r2", snd.at[2], r1.at[0], zm)
    msg("r3", snd.at[3], r2.at[0], zp)
    msg("r13", snd.at[13], r1.at[5], ym)
    msg("r14", snd.at[14], r1.at[10], yp)
    msg("r5", snd.at[5], r1.at[1], ym)
    msg("r9", snd.at[9], r1.at[4], ym)
    msg("r6", snd.at[6], r2.at[1], yp)
    msg("r10", snd.at[10], r2.at[2], yp)
    for n, dev in enumerate((ym, ym, yp)):
        msg("ry%d" % n, sy.at[n], ry.at[n], dev)
    for n, dev in enumerate((zm, zm, zm, zm, zp, zp, zp)):
        msg("rz%d" % n, sz.at[n], rz.at[n], dev)

    go("q2", "q1")
    for copy in pieces:
        copy.wait()
    go("ay1", "ay2", "bz1", "bz2", "azp0", "azm0", "byp0", "bym0", "g2", "g1")
    fetch[0].wait()

    for p, (row, column) in enumerate(
        ((inner, outer), (mate, outer), (inner, beside), (mate, beside))
    ):
        kt[4 * CHUNKS + p] = pos[row, 2 * column]
    for c in range(CHUNKS):
        for w in range(4):
            dy, dz = TABLE[c][w]
            kt[4 * c + w] = pos[inner, 2 * at(xx, dy, dz)]

    def spread(p, src, rows, cols):
        for h in range(HEADS):
            lanes = slice(h * DIM, (h + 1) * DIM)
            rows[p, h * BLK : (h + 1) * BLK, 0:DIM] = src[0:BLK, lanes]
            rows[p, h * BLK : (h + 1) * BLK, DIM : 2 * DIM] = src[BLK : 2 * BLK, lanes]
        cols[p] = rows[p].T

    fetch[1].wait()
    spread(0, mq, qn, qt)
    got("ay1", "ay2", "bz1", "bz2")
    go("ay3", "bz3", "bz4", "azp1", "azm1", "azp2", "azm2", "byp1", "bym1", "byp2", "bym2")
    got("q1")
    spread(1, pq.at[0], qn, qt)

    tok_k = lax.broadcasted_iota(jnp.int32, (BLK, ROWS), 0)
    tok_q = lax.broadcasted_iota(jnp.int32, (BLK, ROWS), 1) % BLK
    diag = tok_k <= tok_q

    def own(kind):
        return jnp.concatenate([buf[0, 0, kind], buf[1, 0, kind]], axis=0)

    for lh in range(2):
        s = jnp.where(diag, nt(own(lh), qt[0, lh * DIM : (lh + 1) * DIM]), NEG)
        m = row_max(s)
        p = jnp.exp2((s - m) * C2)
        stat[lh : lh + 1] = m
        ls[lh] = fold(p, jnp.sum)
        ot[0, lh * DIM : (lh + 1) * DIM] = tn(own(2 + lh), p.astype(jnp.bfloat16))
    stat[2:8] = jnp.full((6, ROWS), NEG, jnp.float32)
    ls[2:8] = jnp.zeros((6, 8, ROWS), jnp.float32)

    fetch[2].wait()
    spread(0, mg, gn, gt)
    got("ay3", "bz3", "bz4")
    go("azp3", "azm3", "bz5", "bz6", "byp3", "bym3")
    for p in range(1, 4):
        ot[p] = jnp.zeros((2 * DIM, ROWS), jnp.float32)
    for c in (6, 9, 13, 14, 15):
        r1[c] = jnp.zeros((4, 4, HALF, DIM), jnp.bfloat16)
    r1[11, 2:4] = jnp.zeros((2, 4, HALF, DIM), jnp.bfloat16)
    r1[12, 0:2] = jnp.zeros((2, 4, HALF, DIM), jnp.bfloat16)

    def take(i, kind):
        return buf[pl.ds(2 * i, 2), :, kind].reshape(KEYS, DIM)

    def picks(i, p):
        number = [kt[8 * i + w] for w in range(8)]
        mine = kt[4 * CHUNKS + p]
        return [n < mine for n in number], [n == mine for n in number]

    def windows(x):
        return [x[w * HALF : (w + 1) * HALF] for w in range(8)]

    def cat(low, high, chosen):
        zero = jnp.zeros((HALF, DIM), jnp.bfloat16)
        rows = []
        for a, b, pick in zip(windows(low), windows(high), chosen):
            rows.append(
                jnp.concatenate([lax.select(pick, a, zero), lax.select(pick, zero, b)], axis=1)
            )
        return jnp.concatenate(rows, axis=0)

    neg_rows = jnp.full((8, ROWS // 2), NEG, jnp.float32)
    big_row = jnp.full((1, ROWS // 2), BIG, jnp.float32)
    high = slice(DIM, 2 * DIM)

    def row(ref, r):
        return ref[pl.ds(r, 1)]

    def arrive(n):
        def do(at_step, *steps):
            @pl.when(n == at_step)
            def _():
                for step, names in steps:
                    step(*names)

        quads = range(4)

        @pl.when(n == 1)
        def _():
            got("q2")
            go("q3")
            spread(2, pq.at[1], qn, qt)
            got("q3")
            spread(3, pq.at[2], qn, qt)

        do(2, (got, ["azp%d" % w for w in quads] + ["azm%d" % w for w in quads]), (go, ["a7", "a8"]))
        do(2, (got, ["bz5", "bz6"]), (go, ["bz7"]))
        do(4, (got, ["bz7"]), (go, ["b9", "b10"]), (got, ["byp%d" % w for w in quads]), (go, ["b13"]))
        do(5, (got, ["g2"]), (go, ["g3"]))

        @pl.when(n == 9)
        def _():
            got("g1", "g3")
            for p in range(1, 4):
                spread(p, pg.at[p - 1], gn, gt)

        do(6, (got, ["bym%d" % w for w in quads] + ["a7", "a8"]), (go, ["a11", "a12"]))
        do(8, (got, ["b9"]))
        do(9, (got, ["b10"]), (go, ["b14"]))
        do(10, (got, ["a11", "a12"]), (go, ["a15p", "a15m"]))
        do(12, (got, ["b13"]))
        do(14, (got, ["b14", "a15p", "a15m"]))

    def forward(n, carry):
        arrive(n)
        i = n // 2
        kl, kh, vl, vh = [take(i, kind) for kind in range(4)]
        parts = []
        for unrolled in range(2):
            p = 2 * (n % 2) + unrolled
            low, same = picks(i, p)
            kcat, vcat = cat(kl, kh, low), cat(vl, vh, low)
            for lanes in (slice(0, ROWS // 2), slice(ROWS // 2, ROWS)):
                olds = [stat[pl.ds(2 * p + lh, 1), lanes] for lh in range(2)]
                parts.append((p, lanes, low, same, kcat, vcat, olds))

        def scores(part):
            p, lanes, _, _, kcat, _, _ = part
            return nt(kl, qt[p, high, lanes]), windows(nt(kcat, qt[p, :, lanes]))

        def weigh(part, s1, s2):
            p, lanes, low, same, _, vcat, (ml, mh) = part
            rl, rh = 2 * p, 2 * p + 1
            tops_l, tops_h = neg_rows, fold(s1, jnp.max)
            for w in range(8):
                top = fold(s2[w], jnp.max)
                tops_l = jnp.maximum(tops_l, lax.select(low[w], top, neg_rows))
                tops_h = jnp.maximum(tops_h, lax.select(low[w] | same[w], neg_rows, top))
            nl, nh = jnp.maximum(ml, row_max(tops_l)), jnp.maximum(mh, row_max(tops_h))
            fl, fh = jnp.exp2((ml - nl) * C2), jnp.exp2((mh - nh) * C2)
            p1 = jnp.exp2((s1 - nh) * C2)
            tl, th = ls[rl, :, lanes] * fl, ls[rh, :, lanes] * fh + fold(p1, jnp.sum)
            pieces = []
            for w in range(8):
                ref = lax.select(same[w], big_row, lax.select(low[w], nl, nh))
                piece = jnp.exp2((s2[w] - ref) * C2)
                total = fold(piece, jnp.sum)
                zero = jnp.zeros_like(total)
                tl = tl + lax.select(low[w], total, zero)
                th = th + lax.select(low[w], zero, total)
                pieces.append(piece.astype(jnp.bfloat16))
            ls[rl, :, lanes], ls[rh, :, lanes] = tl, th
            stat[pl.ds(rl, 1), lanes], stat[pl.ds(rh, 1), lanes] = nl, nh
            mc[i, pl.ds(rl, 1), lanes], mc[i, pl.ds(rh, 1), lanes] = nl, nh
            w1, w2 = p1.astype(jnp.bfloat16), jnp.concatenate(pieces, axis=0)
            wt[i, p, 0, :, lanes], wt[i, p, 1, :, lanes] = w1, w2
            return p, lanes, fl, fh, tn(vl, w1), tn(vcat, w2)

        def update(p, lanes, fl, fh, o1, o2):
            ot[p, 0:DIM, lanes] = ot[p, 0:DIM, lanes] * fl + o2[0:DIM]
            ot[p, high, lanes] = ot[p, high, lanes] * fh + (o1 + o2[high])

        now, late = scores(parts[0]), None
        for k in range(4):
            later = scores(parts[k + 1]) if k < 3 else None
            done = weigh(parts[k], *now)
            if late is not None:
                update(*late)
            now, late = later, done
        update(*late)
        return carry

    lax.fori_loop(0, 2 * STEPS, forward, 0)

    for p in range(4):
        for lh in range(2):
            r = 2 * p + lh
            stat[8 + r : 9 + r] = row_sum(ls[r])
            rows = slice(lh * DIM, (lh + 1) * DIM)
            stat[16 + r : 17 + r] = row_sum(ot[p, rows] * gt[p, rows].astype(jnp.float32))
    go("stat2", "stat1", "stat0")
    go("ot0", "ot1", "ot2")

    dqt[1:4] = jnp.zeros((3, 2 * DIM, ROWS), jnp.float32)
    got("stat0", "stat1", "stat2")
    for p in range(4):
        for lh in range(2):
            r = 2 * p + lh
            held = [(stat, r)] + [(pstat.at[n - 1], 2 * (p ^ n) + lh) for n in range(1, 4)]
            tops = [row(ref, at_row) for ref, at_row in held]
            top = jnp.maximum(jnp.maximum(tops[0], tops[1]), jnp.maximum(tops[2], tops[3]))
            factors = [jnp.exp2((m - top) * C2) for m in tops]
            total, delta = 0.0, 0.0
            for factor, (ref, at_row) in zip(factors, held):
                total = total + factor * row(ref, 8 + at_row)
                delta = delta + factor * row(ref, 16 + at_row)
            lse[r : r + 1] = top + jnp.log(total) * (1.0 / SCALE)
            lse[8 + r : 9 + r] = delta / total
            if p == 0:
                for n in range(4):
                    lse[16 + 2 * n + lh : 17 + 2 * n + lh] = factors[n] / total

    for lh in range(2):
        rows = slice(lh * DIM, (lh + 1) * DIM)
        s = jnp.where(diag, nt(own(lh), qt[0, rows]), NEG)
        p = jnp.exp2((s - lse[lh : lh + 1]) * C2)
        ds = (p * (nt(own(2 + lh), gt[0, rows]) - lse[8 + lh : 9 + lh])).astype(jnp.bfloat16)
        dk = nt(ds, qn[0, :, rows])
        dv = nt(p.astype(jnp.bfloat16), gn[0, :, rows])
        for half in range(2):
            dg[half, lh] = dk[half * HALF : (half + 1) * HALF]
            dg[half, 2 + lh] = dv[half * HALF : (half + 1) * HALF]
        dqt[0, rows] = tn(own(lh), ds)

    def total_of(c, w, slot, ref, *arrived):
        total = tf[c, w] + r1[c, w].astype(jnp.float32) + r2[slot, w].astype(jnp.float32)
        for n in arrived:
            total = total + ref[n].astype(jnp.float32)
        return total

    def b_total(dz, *arrived):
        got(*["rz%d" % n for n in arrived])
        for slot, c in ((1, 1), (2, 4)):
            for w in range(4):
                if TABLE[c][w][1] == dz:
                    return total_of(c, w, slot, rz, *arrived)

    def chain(dz, leaving, *arrived):
        sz[leaving] = b_total(dz, *arrived).astype(jnp.bfloat16)
        go("rz%d" % leaving)

    def a_total(w, *arrived):
        got(*["ry%d" % n for n in arrived])
        return total_of(0, w, 0, ry, *arrived)

    def a_send(w, leaving, *arrived):
        sy[leaving] = a_total(w, *arrived).astype(jnp.bfloat16)
        go("ry%d" % leaving)

    def backward(n, carry):
        i = STEPS - 1 - n // 2
        vl, vh = take(i, 2), take(i, 3)
        parts = []
        for unrolled in range(2):
            p = 2 * (n % 2) + unrolled
            low, same = picks(i, p)
            vcat = cat(vl, vh, low)
            for lanes in (slice(0, ROWS // 2), slice(ROWS // 2, ROWS)):
                parts.append((p, lanes, low, vcat))

        def dots(part):
            p, lanes, _, vcat = part
            return nt(vl, gt[p, high, lanes]), windows(nt(vcat, gt[p, :, lanes]))

        def work(part, g1, g2):
            p, lanes, low, _ = part
            rl, rh = 2 * p, 2 * p + 1
            el, eh = lse[pl.ds(8 + rl, 1), lanes], lse[pl.ds(8 + rh, 1), lanes]
            fl = jnp.exp2((mc[i, pl.ds(rl, 1), lanes] - lse[pl.ds(rl, 1), lanes]) * C2)
            fh = jnp.exp2((mc[i, pl.ds(rh, 1), lanes] - lse[pl.ds(rh, 1), lanes]) * C2)
            p1 = wt[i, p, 0, :, lanes].astype(jnp.float32) * fh
            ds1 = (p1 * (g1 - eh)).astype(jnp.bfloat16)
            w2 = windows(wt[i, p, 1, :, lanes].astype(jnp.float32))
            ps, ds = [], []
            for w in range(8):
                piece = w2[w] * lax.select(low[w], fl, fh)
                ps.append(piece.astype(jnp.bfloat16))
                ds.append((piece * (g2[w] - lax.select(low[w], el, eh))).astype(jnp.bfloat16))
            p2, ds2 = jnp.concatenate(ps, axis=0), jnp.concatenate(ds, axis=0)
            wt[i, p, 0, :, lanes], wt[i, p, 1, :, lanes] = ds1, ds2
            return p1.astype(jnp.bfloat16), ds1, p2, ds2

        def products(p, low, left, right):
            p1, ds1, p2, ds2 = [jnp.concatenate([a, b], axis=1) for a, b in zip(left, right)]
            new = []
            for one, two in (
                (nt(ds1, qn[p, :, high]), nt(ds2, qn[p])),
                (nt(p1, gn[p, :, high]), nt(p2, gn[p])),
            ):
                zero = jnp.zeros((HALF, DIM), jnp.float32)
                lows, highs = [], []
                for w in range(8):
                    rows = slice(w * HALF, (w + 1) * HALF)
                    lows.append(one[rows] + lax.select(low[w], two[rows, 0:DIM], zero))
                    highs.append(lax.select(low[w], zero, two[rows, high]))
                new += [lows, highs]
            return new

        dot0, dot1 = dots(parts[0]), dots(parts[1])
        work0 = work(parts[0], *dot0)
        dot2 = dots(parts[2])
        work1 = work(parts[1], *dot1)
        dot3 = dots(parts[3])
        sums = products(parts[0][0], parts[0][2], work0, work1)
        work2 = work(parts[2], *dot2)
        work3 = work(parts[3], *dot3)
        others = products(parts[2][0], parts[2][2], work2, work3)
        sums = [[a + b for a, b in zip(x, y)] for x, y in zip(sums, others)]

        @pl.when(n % 2 == 0)
        def _():
            for kind in range(4):
                for w in range(8):
                    tf[2 * i + w // 4, w % 4, kind] = sums[kind][w]

        @pl.when(n % 2 == 1)
        def _():
            for kind in range(4):
                for w in range(8):
                    at_chunk = 2 * i + w // 4
                    tf[at_chunk, w % 4, kind] = tf[at_chunk, w % 4, kind] + sums[kind][w]

        def add(c):
            snd[c] = (tf[c] + r1[c].astype(jnp.float32)).astype(jnp.bfloat16)

        def finish(at_step, *chunks):
            @pl.when(n == 2 * (STEPS - 1 - at_step) + 1)
            def _():
                for c, waits, sends in chunks:
                    got(*waits)
                    add(c)
                    go(*sends)

        finish(7, (15, [], ["r15m", "r15p"]), (14, [], ["r14"]))
        finish(6, (13, [], ["r13"]), (12, ["r15p"], ["r12"]))
        finish(5, (11, ["r15m"], ["r11"]), (10, ["r14"], ["r10"]))
        finish(4, (9, [], ["r9"]), (8, ["r12"], ["r8"]))
        finish(3, (6, [], ["r6"]), (7, ["r11"], ["r7"]))
        finish(2, (5, ["r13"], ["r5"]))
        finish(1, (2, ["r7"], ["r2"]), (3, ["r8"], ["r3"]))

        @pl.when(n == 2 * (STEPS - 1 - 2) + 1)
        def _():
            got("r9", "r10")
            chain(4, 0)
            chain(3, 4)

        @pl.when(n == 2 * (STEPS - 1 - 1) + 1)
        def _():
            chain(-3, 1, 0)
            chain(2, 5, 4)

        return carry

    lax.fori_loop(0, 2 * STEPS, backward, 0)

    def store(ref, rows):
        for h in range(HEADS):
            lanes = slice(h * DIM, (h + 1) * DIM)
            ref[0:BLK, lanes] = rows[h * BLK : (h + 1) * BLK, 0:DIM]
            ref[BLK : 2 * BLK, lanes] = rows[h * BLK : (h + 1) * BLK, DIM : 2 * DIM]

    def attend():
        got("ot0", "ot1", "ot2")
        halves = []
        for lh in range(2):
            rows = slice(lh * DIM, (lh + 1) * DIM)
            total = ot[0, rows] * lse[16 + lh : 17 + lh]
            for n in range(1, 4):
                total = total + pot[n - 1, rows] * lse[16 + 2 * n + lh : 17 + 2 * n + lh]
            halves.append(total)
        store(att_ref, jnp.concatenate(halves, axis=0).T.astype(jnp.bfloat16))

    def queries_back(n, carry):
        def stage(at_step):
            return pl.when(n == at_step)

        @stage(0)
        def _():
            got("r5", "r6")
            chain(-2, 2, 1)
            chain(1, 6, 5)

        @stage(1)
        def _():
            attend()
            got("r2", "r3")
            a_send(3, 0)
            a_send(2, 2)

        @stage(2)
        def _():
            go("dq3")

        @stage(3)
        def _():
            a_send(1, 1, 0)
            chain(-1, 3, 2)

        @stage(4)
        def _():
            got("dq3")
            xd[...] = (dqt[2] + pd[0]).astype(jnp.bfloat16)
            go("dq2")

        @stage(6)
        def _():
            go("dq1")

        p = 3 - n // 2
        lows, cats, d1, d2 = [], [], [], []
        for k in range(4):
            i = 4 * (n % 2) + k
            kl, kh = take(i, 0), take(i, 1)
            low, same = picks(i, p)
            lows.append(kl)
            cats.append(cat(kl, kh, low))
            d1.append(wt[i, p, 0])
            d2.append(wt[i, p, 1])
        one = tn(jnp.concatenate(lows, axis=0), jnp.concatenate(d1, axis=0))
        two = tn(jnp.concatenate(cats, axis=0), jnp.concatenate(d2, axis=0))
        dqt[p, 0:DIM] = dqt[p, 0:DIM] + two[0:DIM]
        dqt[p, high] = dqt[p, high] + (one + two[high])
        return carry

    lax.fori_loop(0, 8, queries_back, 0)

    for half, total in enumerate((a_total(0, 1, 2), b_total(0, 3, 6))):
        total = total + dg[half]
        for lh in range(2):
            rows = slice(lh * BLK + half * HALF, lh * BLK + (half + 1) * HALF)
            dk_ref[rows, :] = (total[lh] * SCALE).astype(jnp.bfloat16)
            dv_ref[rows, :] = total[2 + lh].astype(jnp.bfloat16)

    got("dq2", "dq1")
    total = dqt[0] + pd[1] + px[...].astype(jnp.float32)
    store(dq_ref, (total * SCALE).T.astype(jnp.bfloat16))
    for copy in msgs.values():
        copy.wait_send()


def hand_out(*refs):
    sources, targets, sems = refs[:4], refs[4:8], refs[8]
    copies = [
        pltpu.make_async_copy(src, dst, sems.at[n])
        for n, (src, dst) in enumerate(zip(sources, targets))
    ]
    for copy in copies:
        copy.start()
    for copy in copies:
        copy.wait()


def body(queries, keys, values, grad_out, block_pos):
    vmem = pl.BlockSpec(memory_space=pltpu.VMEM)
    bf, f32 = jnp.bfloat16, jnp.float32
    window = (4, HALF, DIM)
    raw = (2 * BLK, HEADS * DIM)
    count = 80
    shapes = [
        jax.ShapeDtypeStruct(raw, bf),
        jax.ShapeDtypeStruct(raw, bf),
        jax.ShapeDtypeStruct((2 * BLK, DIM), bf),
        jax.ShapeDtypeStruct((2 * BLK, DIM), bf),
    ]
    outs = pl.pallas_call(
        kernel,
        out_shape=shapes,
        in_specs=[pl.BlockSpec(memory_space=pltpu.HBM)] * 5,
        out_specs=[vmem] * 4,
        scratch_shapes=[
            pltpu.VMEM((CHUNKS, 4) + window, bf),
            pltpu.VMEM(raw, bf),
            pltpu.VMEM(raw, bf),
            pltpu.VMEM((3,) + raw, bf),
            pltpu.VMEM((3,) + raw, bf),
            pltpu.VMEM((4, ROWS, 2 * DIM), bf),
            pltpu.VMEM((4, ROWS, 2 * DIM), bf),
            pltpu.VMEM((4, 2 * DIM, ROWS), bf),
            pltpu.VMEM((4, 2 * DIM, ROWS), bf),
            pltpu.VMEM((4, 2 * DIM, ROWS), f32),
            pltpu.VMEM((4, 2 * DIM, ROWS), f32),
            pltpu.VMEM((24, ROWS), f32),
            pltpu.VMEM((8, 8, ROWS), f32),
            pltpu.VMEM((3, 24, ROWS), f32),
            pltpu.VMEM((24, ROWS), f32),
            pltpu.VMEM((STEPS, 8, ROWS), f32),
            pltpu.VMEM((STEPS, 4, 2, KEYS, ROWS), bf),
            pltpu.VMEM((3, 2 * DIM, ROWS), f32),
            pltpu.VMEM((2, 2 * DIM, ROWS), f32),
            pltpu.VMEM((2 * DIM, ROWS), bf),
            pltpu.VMEM((2 * DIM, ROWS), bf),
            pltpu.VMEM((CHUNKS, 4) + window, f32),
            pltpu.VMEM((CHUNKS, 4) + window, bf),
            pltpu.VMEM((CHUNKS, 4) + window, bf),
            pltpu.VMEM((3, 4) + window, bf),
            pltpu.VMEM((3,) + window, bf),
            pltpu.VMEM((3,) + window, bf),
            pltpu.VMEM((7,) + window, bf),
            pltpu.VMEM((7,) + window, bf),
            pltpu.VMEM((2,) + window, f32),
            pltpu.SMEM((4, 2 * BLK), jnp.int32),
            pltpu.SMEM((4 * CHUNKS + 4,), jnp.int32),
            pltpu.SemaphoreType.DMA((11,)),
            pltpu.SemaphoreType.DMA((count,)),
            pltpu.SemaphoreType.DMA((count,)),
        ],
        compiler_params=pltpu.CompilerParams(
            collective_id=0, has_side_effects=True, vmem_limit_bytes=54 * 1024 * 1024
        ),
        name="attention",
    )(block_pos, queries[0], keys[0], values[0], grad_out[0])
    outs = pl.pallas_call(
        hand_out,
        out_shape=shapes,
        in_specs=[pl.BlockSpec(memory_space=pl.ANY)] * 4,
        out_specs=[pl.BlockSpec(memory_space=pltpu.HBM)] * 4,
        scratch_shapes=[pltpu.SemaphoreType.DMA((4,))],
        name="hand_out",
    )(*outs)
    return tuple(out[None] for out in outs)


def solution(mesh):
    spec = P("inner", "outer", None)
    return jax.shard_map(
        body,
        mesh=mesh,
        in_specs=(spec, spec, spec, spec, P()),
        out_specs=(spec, spec, spec, spec),
        check_vma=False,
    )
```

```python
import jax
import jax.numpy as jnp
from jax import lax
from jax.experimental import pallas as pl
from jax.experimental.pallas import tpu as pltpu
from jax.sharding import PartitionSpec as P

MESH = pl.DeviceIdType.MESH
NEG = -1e30
BIG = 1e30
BLK = 64
HALF = 32
DIM = 128
HEADS = 8
ROWS = BLK * HEADS
CHUNKS = 16
STEPS = 8
KEYS = 8 * HALF
SCALE = DIM**-0.5
C2 = SCALE * 1.4426950408889634

YORDER = (0, -1, 1, 2)
NEAR = (0, -1, 1, -2)
FAR = (2, -3, 3, 4)


def a_chunk(dz):
    return [(dy, dz) for dy in YORDER]


def b_chunk(dy, part):
    return [(dy, dz) for dz in part]


NAMES = (
    ("A0", a_chunk(0)),
    ("B0n", b_chunk(0, NEAR)),
    ("A-1", a_chunk(-1)),
    ("A+1", a_chunk(1)),
    ("B+1n", b_chunk(1, NEAR)),
    ("B0f", b_chunk(0, FAR)),
    ("A-2", a_chunk(-2)),
    ("A+2", a_chunk(2)),
    ("B-1n", b_chunk(-1, NEAR)),
    ("B+1f", b_chunk(1, FAR)),
    ("A-3", a_chunk(-3)),
    ("A+3", a_chunk(3)),
    ("B2n", b_chunk(2, NEAR)),
    ("B-1f", b_chunk(-1, FAR)),
    ("B2f", b_chunk(2, FAR)),
    ("A4", a_chunk(4)),
)
TABLE = [windows for _, windows in NAMES]
AT = {name: number for number, (name, _) in enumerate(NAMES)}


def nt(a, b):
    return lax.dot_general(a, b, (((1,), (0,)), ((), ())), preferred_element_type=jnp.float32)


def tn(a, b):
    return lax.dot_general(a, b, (((0,), (0,)), ((), ())), preferred_element_type=jnp.float32)


def fold(x, op):
    rows, lanes = x.shape
    return op(x.reshape(rows // 8, 8, lanes), axis=0)


def row_sum(x):
    return jnp.sum(x, axis=0, keepdims=True)


def row_max(x):
    return jnp.max(x, axis=0, keepdims=True)


def kernel(
    pos_ref,
    q_ref,
    k_ref,
    v_ref,
    g_ref,
    att_ref,
    dq_ref,
    dk_ref,
    dv_ref,
    buf,
    mq,
    mg,
    pq,
    pg,
    qn,
    gn,
    qt,
    gt,
    ot,
    dqt,
    stat,
    ls,
    pstat,
    lse,
    mc,
    wt,
    mot,
    pot,
    pd,
    xd,
    px,
    tf,
    snd,
    r1,
    r2,
    sy,
    ry,
    sz,
    rz,
    dg,
    pos,
    kt,
    lsem,
    ssem,
    rsem,
):
    outer = lax.axis_index("outer")
    inner = lax.axis_index("inner")
    yy = outer // 16
    xx = (outer // 8) % 2
    zz = outer % 8
    mate = inner + 1 - 2 * (inner % 2)

    def at(x, dy, dz):
        return (((yy + dy + 4) % 4) * 2 + x) * 8 + (zz + dz + 8) % 8

    beside = at(1 - xx, 0, 0)
    yp, ym = (at(xx, 1, 0), inner), (at(xx, -1, 0), inner)
    zp, zm = (at(xx, 0, 1), inner), (at(xx, 0, -1), inner)
    cp, xp, dp = (outer, mate), (beside, inner), (beside, mate)

    barrier = pltpu.get_barrier_semaphore()
    for dev in (yp, ym, zp, zm, cp, xp, dp):
        pl.semaphore_signal(barrier, inc=1, device_id=dev, device_id_type=MESH)

    fetch = [
        pltpu.make_async_copy(pos_ref, pos, lsem.at[0]),
        pltpu.make_async_copy(q_ref, mq, lsem.at[1]),
        pltpu.make_async_copy(g_ref, mg, lsem.at[2]),
    ]
    pieces = []
    for n, ref in enumerate((k_ref, v_ref)):
        for lh in range(2):
            for half in range(2):
                pieces.append(
                    pltpu.make_async_copy(
                        ref.at[pl.ds(lh * BLK + half * HALF, HALF)],
                        buf.at[half, 0, 2 * n + lh],
                        lsem.at[3 + len(pieces)],
                    )
                )
    for copy in pieces + fetch:
        copy.start()
    pl.semaphore_wait(barrier, 7)

    msgs = {}

    def msg(name, src, dst, dev):
        at_sem = len(msgs)
        msgs[name] = pltpu.make_async_remote_copy(
            src_ref=src,
            dst_ref=dst,
            send_sem=ssem.at[at_sem],
            recv_sem=rsem.at[at_sem],
            device_id=dev,
            device_id_type=MESH,
        )

    def go(*names):
        for name in names:
            msgs[name].start()

    def got(*names):
        for name in names:
            msgs[name].wait_recv()

    for name, src, dst in (("q", q_ref, pq), ("g", g_ref, pg)):
        msg(name + "1", src, dst.at[0], cp)
        msg(name + "2", src, dst.at[1], xp)
        msg(name + "3", dst.at[1], dst.at[2], cp)
    msg("ay1", buf.at[0, 0], buf.at[0, 1], yp)
    msg("ay2", buf.at[0, 0], buf.at[0, 2], ym)
    msg("ay3", buf.at[0, 1], buf.at[0, 3], yp)
    for w in range(4):
        msg("azp%d" % w, buf.at[0, w], buf.at[AT["A-1"], w], zp)
        msg("azm%d" % w, buf.at[0, w], buf.at[AT["A+1"], w], zm)
        msg("byp%d" % w, buf.at[1, w], buf.at[AT["B-1n"], w], yp)
        msg("bym%d" % w, buf.at[1, w], buf.at[AT["B+1n"], w], ym)

    def block(name, source, target, first, count, dev):
        span = pl.ds(first, count)
        msg(name, buf.at[AT[source], span], buf.at[AT[target], span], dev)

    block("a7a", "A-1", "A-2", 0, 3, zp)
    block("a7b", "A-1", "A-2", 3, 1, zp)
    block("a8a", "A+1", "A+2", 0, 3, zm)
    block("a8b", "A+1", "A+2", 3, 1, zm)
    block("a11a", "A-2", "A-3", 0, 2, zp)
    block("a11b", "A-2", "A-3", 2, 2, zp)
    block("a12a", "A+2", "A+3", 2, 2, zm)
    block("a12b", "A+2", "A+3", 0, 2, zm)
    block("a15p", "A-3", "A4", 0, 2, zp)
    block("a15m", "A+3", "A4", 2, 2, zm)
    far = AT["B0f"]
    msg("bz1", buf.at[1, 0], buf.at[1, 1], zp)
    msg("bz2", buf.at[1, 0], buf.at[1, 2], zm)
    msg("bz3", buf.at[1, 1], buf.at[1, 3], zp)
    msg("bz4", buf.at[1, 2], buf.at[far, 0], zm)
    msg("bz5", buf.at[1, 3], buf.at[far, 1], zp)
    msg("bz6", buf.at[far, 0], buf.at[far, 2], zm)
    msg("bz7", buf.at[far, 1], buf.at[far, 3], zp)
    block("b9a", "B0f", "B-1f", 0, 3, yp)
    block("b9b", "B0f", "B-1f", 3, 1, yp)
    block("b10a", "B0f", "B+1f", 0, 3, ym)
    block("b10b", "B0f", "B+1f", 3, 1, ym)
    block("b13", "B-1n", "B2n", 0, 4, yp)
    block("b14a", "B+1f", "B2f", 0, 3, ym)
    block("b14b", "B+1f", "B2f", 3, 1, ym)
    for n, dev in enumerate((cp, xp, dp)):
        msg("stat%d" % n, stat, pstat.at[n], dev)
    for n, dev in enumerate((cp, xp, dp)):
        msg("ot%d" % n, mot.at[n], pot.at[n], dev)
    msg("dq3", dqt.at[3], pd.at[0], cp)
    msg("dq2", xd, px, xp)
    msg("dq1", dqt.at[1], pd.at[1], cp)
    def back(name, source, target, first, count, dev, into=None):
        span = pl.ds(first, count)
        into = r1.at[AT[target], span] if into is None else r2.at[into, span]
        msg(name, snd.at[AT[source], span], into, dev)

    back("rA4m", "A4", "A-3", 0, 2, zm)
    back("rA4p", "A4", "A+3", 2, 2, zp)
    back("rA-3", "A-3", "A-2", 0, 4, zm)
    back("rA+3", "A+3", "A+2", 0, 4, zp)
    back("rA-2", "A-2", "A-1", 0, 4, zm)
    back("rA+2", "A+2", "A+1", 0, 4, zp)
    back("rA-1a", "A-1", "A0", 2, 2, zm)
    back("rA-1b", "A-1", "A0", 0, 2, zm)
    back("rA+1a", "A+1", "A0", 2, 2, zp, 0)
    back("rA+1b", "A+1", "A0", 0, 2, zp, 0)
    back("rB2n", "B2n", "B-1n", 0, 4, ym)
    back("rB2f", "B2f", "B+1f", 0, 4, yp)
    back("rB-1n", "B-1n", "B0n", 0, 4, ym)
    back("rB-1f", "B-1f", "B0f", 0, 4, ym)
    back("rB+1n", "B+1n", "B0n", 0, 4, yp, 1)
    back("rB+1f", "B+1f", "B0f", 0, 4, yp, 2)
    for n, dev in enumerate((ym, ym, yp)):
        msg("ry%d" % n, sy.at[n], ry.at[n], dev)
    for n, dev in enumerate((zm, zm, zm, zm, zp, zp, zp)):
        msg("rz%d" % n, sz.at[n], rz.at[n], dev)

    go("q2", "q1")
    for copy in pieces:
        copy.wait()
    go("ay1", "ay2", "bz1", "bz2", "azp0", "azm0", "byp0", "bym0", "g1")
    fetch[0].wait()

    for p, (row, column) in enumerate(
        ((inner, outer), (mate, outer), (inner, beside), (mate, beside))
    ):
        kt[4 * CHUNKS + p] = pos[row, 2 * column]
    for c in range(CHUNKS):
        for w in range(4):
            dy, dz = TABLE[c][w]
            kt[4 * c + w] = pos[inner, 2 * at(xx, dy, dz)]

    def spread(p, src, rows, cols):
        for h in range(HEADS):
            lanes = slice(h * DIM, (h + 1) * DIM)
            rows[p, h * BLK : (h + 1) * BLK, 0:DIM] = src[0:BLK, lanes]
            rows[p, h * BLK : (h + 1) * BLK, DIM : 2 * DIM] = src[BLK : 2 * BLK, lanes]
        cols[p] = rows[p].T

    fetch[1].wait()
    spread(0, mq, qn, qt)
    got("ay1", "ay2", "bz1", "bz2")
    go("ay3", "bz3", "bz4", "azp1", "azm1", "azp2", "azm2", "byp1", "bym1", "byp2", "bym2")
    got("q1")
    spread(1, pq.at[0], qn, qt)

    tok_k = lax.broadcasted_iota(jnp.int32, (BLK, ROWS), 0)
    tok_q = lax.broadcasted_iota(jnp.int32, (BLK, ROWS), 1) % BLK
    diag = tok_k <= tok_q

    def own(kind):
        return jnp.concatenate([buf[0, 0, kind], buf[1, 0, kind]], axis=0)

    for lh in range(2):
        s = jnp.where(diag, nt(own(lh), qt[0, lh * DIM : (lh + 1) * DIM]), NEG)
        m = row_max(s)
        p = jnp.exp2((s - m) * C2)
        stat[lh : lh + 1] = m
        ls[lh] = fold(p, jnp.sum)
        ot[0, lh * DIM : (lh + 1) * DIM] = tn(own(2 + lh), p.astype(jnp.bfloat16))
    stat[2:8] = jnp.full((6, ROWS), NEG, jnp.float32)
    ls[2:8] = jnp.zeros((6, 8, ROWS), jnp.float32)

    got("ay3", "bz3", "bz4")
    go("azp3", "azm3", "bz5", "bz6", "byp3", "bym3")
    for w in range(3):
        got("azp%d" % w, "azm%d" % w)
    go("a7a", "a8a")
    for p in range(1, 4):
        ot[p] = jnp.zeros((2 * DIM, ROWS), jnp.float32)
    for name in ("B+1n", "B2n", "B-1f", "B2f", "A4"):
        r1[AT[name]] = jnp.zeros((4, 4, HALF, DIM), jnp.bfloat16)
    r1[AT["A-3"], 2:4] = jnp.zeros((2, 4, HALF, DIM), jnp.bfloat16)
    r1[AT["A+3"], 0:2] = jnp.zeros((2, 4, HALF, DIM), jnp.bfloat16)

    def take(i, kind):
        return buf[pl.ds(2 * i, 2), :, kind].reshape(KEYS, DIM)

    def picks(i, p):
        number = [kt[8 * i + w] for w in range(8)]
        mine = kt[4 * CHUNKS + p]
        return [n < mine for n in number], [n == mine for n in number]

    def windows(x):
        return [x[w * HALF : (w + 1) * HALF] for w in range(8)]

    def cat(low, high, chosen):
        zero = jnp.zeros((HALF, DIM), jnp.bfloat16)
        rows = []
        for a, b, pick in zip(windows(low), windows(high), chosen):
            rows.append(
                jnp.concatenate([lax.select(pick, a, zero), lax.select(pick, zero, b)], axis=1)
            )
        return jnp.concatenate(rows, axis=0)

    neg_rows = jnp.full((8, ROWS // 2), NEG, jnp.float32)
    big_row = jnp.full((1, ROWS // 2), BIG, jnp.float32)
    high = slice(DIM, 2 * DIM)

    def row(ref, r):
        return ref[pl.ds(r, 1)]

    def arrive(n):
        def do(at_step, *steps):
            @pl.when(n == at_step)
            def _():
                for step, names in steps:
                    step(*names)

        @pl.when(n == 1)
        def _():
            got("azp3", "azm3", "bz5", "bz6")
            go("a7b", "a8b", "bz7", "b9a", "b10a")
            got("byp0", "byp1", "byp2", "byp3")
            go("b13")
            fetch[2].wait()
            spread(0, mg, gn, gt)
            got("q2")
            go("q3", "g2")
            spread(2, pq.at[1], qn, qt)
            got("q3")
            spread(3, pq.at[2], qn, qt)

        do(2, (got, ["a7a", "a7b", "a8a", "a8b", "bz7"]))
        do(2, (go, ["a11a", "a12a", "a11b", "a12b", "b9b", "b10b"]))
        do(4, (got, ["bym%d" % w for w in range(4)] + ["b10a"]), (go, ["b14a"]))
        do(6, (got, ["a11a", "a12a"]), (go, ["a15p", "a15m"]))
        do(6, (got, ["b10b"]), (go, ["b14b"]))
        do(7, (got, ["g2"]), (go, ["g3"]))

        @pl.when(n == 9)
        def _():
            got("g1", "g3")
            for p in range(1, 4):
                spread(p, pg.at[p - 1], gn, gt)

        do(10, (got, ["a11b", "a12b"]))
        do(12, (got, ["b13", "b9a", "b9b"]))
        do(14, (got, ["b14a", "b14b", "a15p", "a15m"]))

    def forward(n, carry):
        arrive(n)
        i = n // 2
        kl, kh, vl, vh = [take(i, kind) for kind in range(4)]
        parts = []
        for unrolled in range(2):
            p = 2 * (n % 2) + unrolled
            low, same = picks(i, p)
            kcat, vcat = cat(kl, kh, low), cat(vl, vh, low)
            for lanes in (slice(0, ROWS // 2), slice(ROWS // 2, ROWS)):
                olds = [stat[pl.ds(2 * p + lh, 1), lanes] for lh in range(2)]
                parts.append((p, lanes, low, same, kcat, vcat, olds))

        def scores(part):
            p, lanes, _, _, kcat, _, _ = part
            return nt(kl, qt[p, high, lanes]), windows(nt(kcat, qt[p, :, lanes]))

        def weigh(part, s1, s2):
            p, lanes, low, same, _, vcat, (ml, mh) = part
            rl, rh = 2 * p, 2 * p + 1
            tops_l, tops_h = neg_rows, fold(s1, jnp.max)
            for w in range(8):
                top = fold(s2[w], jnp.max)
                tops_l = jnp.maximum(tops_l, lax.select(low[w], top, neg_rows))
                tops_h = jnp.maximum(tops_h, lax.select(low[w] | same[w], neg_rows, top))
            nl, nh = jnp.maximum(ml, row_max(tops_l)), jnp.maximum(mh, row_max(tops_h))
            fl, fh = jnp.exp2((ml - nl) * C2), jnp.exp2((mh - nh) * C2)
            p1 = jnp.exp2((s1 - nh) * C2)
            tl, th = ls[rl, :, lanes] * fl, ls[rh, :, lanes] * fh + fold(p1, jnp.sum)
            pieces = []
            for w in range(8):
                ref = lax.select(same[w], big_row, lax.select(low[w], nl, nh))
                piece = jnp.exp2((s2[w] - ref) * C2)
                total = fold(piece, jnp.sum)
                zero = jnp.zeros_like(total)
                tl = tl + lax.select(low[w], total, zero)
                th = th + lax.select(low[w], zero, total)
                pieces.append(piece.astype(jnp.bfloat16))
            ls[rl, :, lanes], ls[rh, :, lanes] = tl, th
            stat[pl.ds(rl, 1), lanes], stat[pl.ds(rh, 1), lanes] = nl, nh
            mc[i, pl.ds(rl, 1), lanes], mc[i, pl.ds(rh, 1), lanes] = nl, nh
            w1, w2 = p1.astype(jnp.bfloat16), jnp.concatenate(pieces, axis=0)
            wt[i, p, 0, :, lanes], wt[i, p, 1, :, lanes] = w1, w2
            return p, lanes, fl, fh, tn(vl, w1), tn(vcat, w2)

        def update(p, lanes, fl, fh, o1, o2):
            ot[p, 0:DIM, lanes] = ot[p, 0:DIM, lanes] * fl + o2[0:DIM]
            ot[p, high, lanes] = ot[p, high, lanes] * fh + (o1 + o2[high])

        now, late = scores(parts[0]), None
        for k in range(4):
            later = scores(parts[k + 1]) if k < 3 else None
            done = weigh(parts[k], *now)
            if late is not None:
                update(*late)
            now, late = later, done
        update(*late)
        return carry

    lax.fori_loop(0, 2 * STEPS, forward, 0)

    for p in range(4):
        for lh in range(2):
            r = 2 * p + lh
            stat[8 + r : 9 + r] = row_sum(ls[r])
            rows = slice(lh * DIM, (lh + 1) * DIM)
            stat[16 + r : 17 + r] = row_sum(ot[p, rows] * gt[p, rows].astype(jnp.float32))
    go("stat2", "stat1", "stat0")
    for n in range(3):
        mot[n] = ot[n + 1].astype(jnp.bfloat16)
    go("ot0", "ot1", "ot2")

    dqt[1:4] = jnp.zeros((3, 2 * DIM, ROWS), jnp.float32)
    got("stat0", "stat1", "stat2")
    for p in range(4):
        for lh in range(2):
            r = 2 * p + lh
            held = [(stat, r)] + [(pstat.at[n - 1], 2 * (p ^ n) + lh) for n in range(1, 4)]
            tops = [row(ref, at_row) for ref, at_row in held]
            top = jnp.maximum(jnp.maximum(tops[0], tops[1]), jnp.maximum(tops[2], tops[3]))
            factors = [jnp.exp2((m - top) * C2) for m in tops]
            total, delta = 0.0, 0.0
            for factor, (ref, at_row) in zip(factors, held):
                total = total + factor * row(ref, 8 + at_row)
                delta = delta + factor * row(ref, 16 + at_row)
            lse[r : r + 1] = top + jnp.log(total) * (1.0 / SCALE)
            lse[8 + r : 9 + r] = delta / total
            if p == 0:
                for n in range(4):
                    lse[16 + 2 * n + lh : 17 + 2 * n + lh] = factors[n] / total

    for lh in range(2):
        rows = slice(lh * DIM, (lh + 1) * DIM)
        s = jnp.where(diag, nt(own(lh), qt[0, rows]), NEG)
        p = jnp.exp2((s - lse[lh : lh + 1]) * C2)
        ds = (p * (nt(own(2 + lh), gt[0, rows]) - lse[8 + lh : 9 + lh])).astype(jnp.bfloat16)
        dk = nt(ds, qn[0, :, rows])
        dv = nt(p.astype(jnp.bfloat16), gn[0, :, rows])
        for half in range(2):
            dg[half, lh] = dk[half * HALF : (half + 1) * HALF]
            dg[half, 2 + lh] = dv[half * HALF : (half + 1) * HALF]
        dqt[0, rows] = tn(own(lh), ds)

    def total_of(c, w, slot, ref, *arrived):
        total = tf[c, w] + r1[c, w].astype(jnp.float32) + r2[slot, w].astype(jnp.float32)
        for n in arrived:
            total = total + ref[n].astype(jnp.float32)
        return total

    def b_total(dz, *arrived):
        got(*["rz%d" % n for n in arrived])
        for slot, c in ((1, 1), (2, far)):
            for w in range(4):
                if TABLE[c][w][1] == dz:
                    return total_of(c, w, slot, rz, *arrived)

    def chain(dz, leaving, *arrived):
        sz[leaving] = b_total(dz, *arrived).astype(jnp.bfloat16)
        go("rz%d" % leaving)

    def a_total(w, *arrived):
        got(*["ry%d" % n for n in arrived])
        return total_of(0, w, 0, ry, *arrived)

    def a_send(w, leaving, *arrived):
        sy[leaving] = a_total(w, *arrived).astype(jnp.bfloat16)
        go("ry%d" % leaving)

    def backward(n, carry):
        i = STEPS - 1 - n // 2
        vl, vh = take(i, 2), take(i, 3)
        parts = []
        for unrolled in range(2):
            p = 2 * (n % 2) + unrolled
            low, same = picks(i, p)
            vcat = cat(vl, vh, low)
            for lanes in (slice(0, ROWS // 2), slice(ROWS // 2, ROWS)):
                parts.append((p, lanes, low, vcat))

        def dots(part):
            p, lanes, _, vcat = part
            return nt(vl, gt[p, high, lanes]), windows(nt(vcat, gt[p, :, lanes]))

        def work(part, g1, g2):
            p, lanes, low, _ = part
            rl, rh = 2 * p, 2 * p + 1
            el, eh = lse[pl.ds(8 + rl, 1), lanes], lse[pl.ds(8 + rh, 1), lanes]
            fl = jnp.exp2((mc[i, pl.ds(rl, 1), lanes] - lse[pl.ds(rl, 1), lanes]) * C2)
            fh = jnp.exp2((mc[i, pl.ds(rh, 1), lanes] - lse[pl.ds(rh, 1), lanes]) * C2)
            p1 = wt[i, p, 0, :, lanes].astype(jnp.float32) * fh
            ds1 = (p1 * (g1 - eh)).astype(jnp.bfloat16)
            w2 = windows(wt[i, p, 1, :, lanes].astype(jnp.float32))
            ps, ds = [], []
            for w in range(8):
                piece = w2[w] * lax.select(low[w], fl, fh)
                ps.append(piece.astype(jnp.bfloat16))
                ds.append((piece * (g2[w] - lax.select(low[w], el, eh))).astype(jnp.bfloat16))
            p2, ds2 = jnp.concatenate(ps, axis=0), jnp.concatenate(ds, axis=0)
            wt[i, p, 0, :, lanes], wt[i, p, 1, :, lanes] = ds1, ds2
            return p1.astype(jnp.bfloat16), ds1, p2, ds2

        def products(p, low, left, right):
            p1, ds1, p2, ds2 = [jnp.concatenate([a, b], axis=1) for a, b in zip(left, right)]
            new = []
            for one, two in (
                (nt(ds1, qn[p, :, high]), nt(ds2, qn[p])),
                (nt(p1, gn[p, :, high]), nt(p2, gn[p])),
            ):
                zero = jnp.zeros((HALF, DIM), jnp.float32)
                lows, highs = [], []
                for w in range(8):
                    rows = slice(w * HALF, (w + 1) * HALF)
                    lows.append(one[rows] + lax.select(low[w], two[rows, 0:DIM], zero))
                    highs.append(lax.select(low[w], zero, two[rows, high]))
                new += [lows, highs]
            return new

        dot0, dot1 = dots(parts[0]), dots(parts[1])
        work0 = work(parts[0], *dot0)
        dot2 = dots(parts[2])
        work1 = work(parts[1], *dot1)
        dot3 = dots(parts[3])
        sums = products(parts[0][0], parts[0][2], work0, work1)
        work2 = work(parts[2], *dot2)
        work3 = work(parts[3], *dot3)
        others = products(parts[2][0], parts[2][2], work2, work3)
        sums = [[a + b for a, b in zip(x, y)] for x, y in zip(sums, others)]

        @pl.when(n % 2 == 0)
        def _():
            for kind in range(4):
                for w in range(8):
                    tf[2 * i + w // 4, w % 4, kind] = sums[kind][w]

        @pl.when(n % 2 == 1)
        def _():
            for kind in range(4):
                for w in range(8):
                    at_chunk = 2 * i + w // 4
                    tf[at_chunk, w % 4, kind] = tf[at_chunk, w % 4, kind] + sums[kind][w]

        def add(c):
            snd[c] = (tf[c] + r1[c].astype(jnp.float32)).astype(jnp.bfloat16)

        def finish(at_step, *chunks):
            @pl.when(n == 2 * (STEPS - 1 - at_step) + 1)
            def _():
                for c, waits, sends in chunks:
                    got(*waits)
                    add(c)
                    go(*sends)

        def step(name, waits=(), sends=None):
            return AT[name], waits, ["r" + name] if sends is None else sends

        finish(7, step("B2f"), step("A4", (), ["rA4m", "rA4p"]))
        finish(6, step("B2n"), step("B-1f"))
        finish(5, step("A-3", ["rA4m"]), step("A+3", ["rA4p"]))
        finish(4, step("B-1n", ["rB2n"]), step("B+1f", ["rB2f"]))
        finish(3, step("A-2", ["rA-3"]), step("A+2", ["rA+3"]))
        finish(2, step("B+1n"))
        finish(
            1,
            step("A-1", ["rA-2"], ["rA-1a", "rA-1b"]),
            step("A+1", ["rA+2"], ["rA+1a", "rA+1b"]),
        )

        @pl.when(n == 2 * (STEPS - 1 - 2) + 1)
        def _():
            got("rB-1f", "rB+1f")
            chain(4, 0)
            chain(3, 4)

        @pl.when(n == 2 * (STEPS - 1 - 1) + 1)
        def _():
            chain(-3, 1, 0)
            chain(2, 5, 4)

        return carry

    lax.fori_loop(0, 2 * STEPS, backward, 0)

    def store(ref, rows):
        for h in range(HEADS):
            lanes = slice(h * DIM, (h + 1) * DIM)
            ref[0:BLK, lanes] = rows[h * BLK : (h + 1) * BLK, 0:DIM]
            ref[BLK : 2 * BLK, lanes] = rows[h * BLK : (h + 1) * BLK, DIM : 2 * DIM]

    def attend():
        got("ot0", "ot1", "ot2")
        halves = []
        for lh in range(2):
            rows = slice(lh * DIM, (lh + 1) * DIM)
            total = ot[0, rows] * lse[16 + lh : 17 + lh]
            for n in range(1, 4):
                total = total + pot[n - 1, rows].astype(jnp.float32) * lse[16 + 2 * n + lh : 17 + 2 * n + lh]
            halves.append(total)
        store(att_ref, jnp.concatenate(halves, axis=0).T.astype(jnp.bfloat16))

    def queries_back(n, carry):
        def stage(at_step):
            return pl.when(n == at_step)

        @stage(0)
        def _():
            got("rB-1n", "rB+1n")
            chain(-2, 2, 1)
            chain(1, 6, 5)

        @stage(1)
        def _():
            got("rA-1a", "rA+1a")
            a_send(3, 0)
            a_send(2, 2)

        @stage(2)
        def _():
            go("dq3")

        @stage(3)
        def _():
            chain(-1, 3, 2)
            got("rA-1b", "rA+1b")
            a_send(1, 1, 0)

        @stage(4)
        def _():
            got("dq3")
            xd[...] = (dqt[2] + pd[0]).astype(jnp.bfloat16)
            go("dq2")

        @stage(6)
        def _():
            go("dq1")
            attend()

        p = 3 - n // 2
        lows, cats, d1, d2 = [], [], [], []
        for k in range(4):
            i = 4 * (n % 2) + k
            kl, kh = take(i, 0), take(i, 1)
            low, same = picks(i, p)
            lows.append(kl)
            cats.append(cat(kl, kh, low))
            d1.append(wt[i, p, 0])
            d2.append(wt[i, p, 1])
        one = tn(jnp.concatenate(lows, axis=0), jnp.concatenate(d1, axis=0))
        two = tn(jnp.concatenate(cats, axis=0), jnp.concatenate(d2, axis=0))
        dqt[p, 0:DIM] = dqt[p, 0:DIM] + two[0:DIM]
        dqt[p, high] = dqt[p, high] + (one + two[high])
        return carry

    lax.fori_loop(0, 8, queries_back, 0)

    for half, total in enumerate((a_total(0, 1, 2), b_total(0, 3, 6))):
        total = total + dg[half]
        for lh in range(2):
            rows = slice(lh * BLK + half * HALF, lh * BLK + (half + 1) * HALF)
            dk_ref[rows, :] = (total[lh] * SCALE).astype(jnp.bfloat16)
            dv_ref[rows, :] = total[2 + lh].astype(jnp.bfloat16)

    got("dq2", "dq1")
    total = dqt[0] + pd[1] + px[...].astype(jnp.float32)
    store(dq_ref, (total * SCALE).T.astype(jnp.bfloat16))
    for copy in msgs.values():
        copy.wait_send()


def hand_out(*refs):
    for source, target in zip(refs[:4], refs[4:]):
        target[...] = source[...]


def body(queries, keys, values, grad_out, block_pos):
    vmem = pl.BlockSpec(memory_space=pltpu.VMEM)
    bf, f32 = jnp.bfloat16, jnp.float32
    window = (4, HALF, DIM)
    raw = (2 * BLK, HEADS * DIM)
    count = 96
    shapes = [
        jax.ShapeDtypeStruct(raw, bf),
        jax.ShapeDtypeStruct(raw, bf),
        jax.ShapeDtypeStruct((2 * BLK, DIM), bf),
        jax.ShapeDtypeStruct((2 * BLK, DIM), bf),
    ]
    outs = pl.pallas_call(
        kernel,
        out_shape=shapes,
        in_specs=[pl.BlockSpec(memory_space=pltpu.HBM)] * 5,
        out_specs=[vmem] * 4,
        scratch_shapes=[
            pltpu.VMEM((CHUNKS, 4) + window, bf),
            pltpu.VMEM(raw, bf),
            pltpu.VMEM(raw, bf),
            pltpu.VMEM((3,) + raw, bf),
            pltpu.VMEM((3,) + raw, bf),
            pltpu.VMEM((4, ROWS, 2 * DIM), bf),
            pltpu.VMEM((4, ROWS, 2 * DIM), bf),
            pltpu.VMEM((4, 2 * DIM, ROWS), bf),
            pltpu.VMEM((4, 2 * DIM, ROWS), bf),
            pltpu.VMEM((4, 2 * DIM, ROWS), f32),
            pltpu.VMEM((4, 2 * DIM, ROWS), f32),
            pltpu.VMEM((24, ROWS), f32),
            pltpu.VMEM((8, 8, ROWS), f32),
            pltpu.VMEM((3, 24, ROWS), f32),
            pltpu.VMEM((24, ROWS), f32),
            pltpu.VMEM((STEPS, 8, ROWS), f32),
            pltpu.VMEM((STEPS, 4, 2, KEYS, ROWS), bf),
            pltpu.VMEM((3, 2 * DIM, ROWS), bf),
            pltpu.VMEM((3, 2 * DIM, ROWS), bf),
            pltpu.VMEM((2, 2 * DIM, ROWS), f32),
            pltpu.VMEM((2 * DIM, ROWS), bf),
            pltpu.VMEM((2 * DIM, ROWS), bf),
            pltpu.VMEM((CHUNKS, 4) + window, f32),
            pltpu.VMEM((CHUNKS, 4) + window, bf),
            pltpu.VMEM((CHUNKS, 4) + window, bf),
            pltpu.VMEM((3, 4) + window, bf),
            pltpu.VMEM((3,) + window, bf),
            pltpu.VMEM((3,) + window, bf),
            pltpu.VMEM((7,) + window, bf),
            pltpu.VMEM((7,) + window, bf),
            pltpu.VMEM((2,) + window, f32),
            pltpu.SMEM((4, 2 * BLK), jnp.int32),
            pltpu.SMEM((4 * CHUNKS + 4,), jnp.int32),
            pltpu.SemaphoreType.DMA((11,)),
            pltpu.SemaphoreType.DMA((count,)),
            pltpu.SemaphoreType.DMA((count,)),
        ],
        compiler_params=pltpu.CompilerParams(
            collective_id=0, has_side_effects=True, vmem_limit_bytes=54 * 1024 * 1024
        ),
        name="attention",
    )(block_pos, queries[0], keys[0], values[0], grad_out[0])
    outs = pl.pallas_call(
        hand_out,
        out_shape=shapes,
        in_specs=[pl.BlockSpec(one.shape, lambda n: (0, 0)) for one in shapes],
        out_specs=[pl.BlockSpec(one.shape, lambda n: (0, 0)) for one in shapes],
        grid=(1,),
        compiler_params=pltpu.CompilerParams(vmem_limit_bytes=54 * 1024 * 1024),
        name="hand_out",
    )(*outs)
    return tuple(out[None] for out in outs)


def solution(mesh):
    spec = P("inner", "outer", None)
    return jax.shard_map(
        body,
        mesh=mesh,
        in_specs=(spec, spec, spec, spec, P()),
        out_specs=(spec, spec, spec, spec),
        check_vma=False,
    )
```

```python
import jax
import jax.numpy as jnp
from jax import lax
from jax.experimental import pallas as pl
from jax.experimental.pallas import tpu as pltpu
from jax.sharding import PartitionSpec as P

MESH = pl.DeviceIdType.MESH
NEG = -1e30
BIG = 1e30
BLK = 64
HALF = 32
DIM = 128
HEADS = 8
ROWS = BLK * HEADS
CHUNKS = 16
STEPS = 4
BACK_STEPS = 8
KEYS = 16 * HALF
BACK_KEYS = 8 * HALF
SCALE = DIM**-0.5
C2 = SCALE * 1.4426950408889634

YORDER = (0, -1, 1, 2)
NEAR = (0, -1, 1, -2)
FAR = (2, -3, 3, 4)


def a_chunk(dz):
    return [(dy, dz) for dy in YORDER]


def b_chunk(dy, part):
    return [(dy, dz) for dz in part]


NAMES = (
    ("A0", a_chunk(0)),
    ("B0n", b_chunk(0, NEAR)),
    ("A-1", a_chunk(-1)),
    ("A+1", a_chunk(1)),
    ("B+1n", b_chunk(1, NEAR)),
    ("B0f", b_chunk(0, FAR)),
    ("A-2", a_chunk(-2)),
    ("A+2", a_chunk(2)),
    ("B-1n", b_chunk(-1, NEAR)),
    ("B+1f", b_chunk(1, FAR)),
    ("A-3", a_chunk(-3)),
    ("A+3", a_chunk(3)),
    ("B2f", b_chunk(2, FAR)),
    ("B-1f", b_chunk(-1, FAR)),
    ("B2n", b_chunk(2, NEAR)),
    ("A4", a_chunk(4)),
)
TABLE = [windows for _, windows in NAMES]
AT = {name: number for number, (name, _) in enumerate(NAMES)}


def nt(a, b):
    return lax.dot_general(a, b, (((1,), (0,)), ((), ())), preferred_element_type=jnp.float32)


def tn(a, b):
    return lax.dot_general(a, b, (((0,), (0,)), ((), ())), preferred_element_type=jnp.float32)


def fold(x, op):
    rows, lanes = x.shape
    return op(x.reshape(rows // 8, 8, lanes), axis=0)


def row_sum(x):
    return jnp.sum(x, axis=0, keepdims=True)


def row_max(x):
    return jnp.max(x, axis=0, keepdims=True)


def kernel(
    pos_ref,
    q_ref,
    k_ref,
    v_ref,
    g_ref,
    att_out,
    dq_out,
    dk_out,
    dv_out,
    att_ref,
    dq_ref,
    dk_ref,
    dv_ref,
    buf,
    mq,
    mg,
    pq,
    pg,
    qn,
    gn,
    qt,
    gt,
    ot,
    dqt,
    stat,
    ls,
    pstat,
    lse,
    mc,
    wt,
    mot,
    pot,
    sd,
    pd,
    xd,
    px,
    tf,
    snd,
    r1,
    r2,
    sy,
    ry,
    sz,
    rz,
    dg,
    pos,
    kt,
    lsem,
    ssem,
    rsem,
):
    outer = lax.axis_index("outer")
    inner = lax.axis_index("inner")
    yy = outer // 16
    xx = (outer // 8) % 2
    zz = outer % 8
    mate = inner + 1 - 2 * (inner % 2)

    def at(x, dy, dz):
        return (((yy + dy + 4) % 4) * 2 + x) * 8 + (zz + dz + 8) % 8

    beside = at(1 - xx, 0, 0)
    yp, ym = (at(xx, 1, 0), inner), (at(xx, -1, 0), inner)
    zp, zm = (at(xx, 0, 1), inner), (at(xx, 0, -1), inner)
    cp, xp, dp = (outer, mate), (beside, inner), (beside, mate)

    barrier = pltpu.get_barrier_semaphore()
    for dev in (yp, ym, zp, zm, cp, xp, dp):
        pl.semaphore_signal(barrier, inc=1, device_id=dev, device_id_type=MESH)

    fetch = [
        pltpu.make_async_copy(pos_ref, pos, lsem.at[0]),
        pltpu.make_async_copy(q_ref, mq, lsem.at[1]),
        pltpu.make_async_copy(g_ref, mg, lsem.at[2]),
    ]
    pieces = []
    for n, ref in enumerate((k_ref, v_ref)):
        for lh in range(2):
            for half in range(2):
                pieces.append(
                    pltpu.make_async_copy(
                        ref.at[pl.ds(lh * BLK + half * HALF, HALF)],
                        buf.at[half, 0, 2 * n + lh],
                        lsem.at[3 + len(pieces)],
                    )
                )
    for copy in pieces + fetch:
        copy.start()
    pl.semaphore_wait(barrier, 7)

    msgs = {}

    def msg(name, src, dst, dev):
        at_sem = len(msgs)
        msgs[name] = pltpu.make_async_remote_copy(
            src_ref=src,
            dst_ref=dst,
            send_sem=ssem.at[at_sem],
            recv_sem=rsem.at[at_sem],
            device_id=dev,
            device_id_type=MESH,
        )

    def go(*names):
        for name in names:
            msgs[name].start()

    def got(*names):
        for name in names:
            msgs[name].wait_recv()

    for name, src, dst in (("q", q_ref, pq), ("g", g_ref, pg)):
        msg(name + "1", src, dst.at[0], cp)
        for half in range(2):
            span = pl.ds(half * BLK, BLK)
            msg("%s2%d" % (name, half), src.at[span], dst.at[1, span], xp)
            msg("%s3%d" % (name, half), dst.at[1, span], dst.at[2, span], cp)
    msg("ay1", buf.at[0, 0], buf.at[0, 1], yp)
    msg("ay2", buf.at[0, 0], buf.at[0, 2], ym)
    msg("ay3", buf.at[0, 1], buf.at[0, 3], yp)
    for w in range(4):
        msg("azp%d" % w, buf.at[0, w], buf.at[AT["A-1"], w], zp)
        msg("azm%d" % w, buf.at[0, w], buf.at[AT["A+1"], w], zm)
        msg("byp%d" % w, buf.at[1, w], buf.at[AT["B-1n"], w], yp)
        msg("bym%d" % w, buf.at[1, w], buf.at[AT["B+1n"], w], ym)

    def block(name, source, target, first, count, dev):
        span = pl.ds(first, count)
        msg(name, buf.at[AT[source], span], buf.at[AT[target], span], dev)

    block("a7a", "A-1", "A-2", 0, 3, zp)
    block("a7b", "A-1", "A-2", 3, 1, zp)
    block("a8a", "A+1", "A+2", 0, 3, zm)
    block("a8b", "A+1", "A+2", 3, 1, zm)
    block("a11a", "A-2", "A-3", 0, 2, zp)
    block("a11b", "A-2", "A-3", 2, 2, zp)
    block("a12a", "A+2", "A+3", 2, 2, zm)
    block("a12b", "A+2", "A+3", 0, 2, zm)
    block("a15p", "A-3", "A4", 0, 2, zp)
    block("a15m", "A+3", "A4", 2, 2, zm)
    far = AT["B0f"]
    msg("bz1", buf.at[1, 0], buf.at[1, 1], zp)
    msg("bz2", buf.at[1, 0], buf.at[1, 2], zm)
    msg("bz3", buf.at[1, 1], buf.at[1, 3], zp)
    msg("bz4", buf.at[1, 2], buf.at[far, 0], zm)
    msg("bz5", buf.at[1, 3], buf.at[far, 1], zp)
    msg("bz6", buf.at[far, 0], buf.at[far, 2], zm)
    msg("bz7", buf.at[far, 1], buf.at[far, 3], zp)
    block("b9a", "B0f", "B-1f", 0, 3, yp)
    block("b9b", "B0f", "B-1f", 3, 1, yp)
    block("b10a", "B0f", "B+1f", 0, 3, ym)
    block("b10b", "B0f", "B+1f", 3, 1, ym)
    block("b13", "B-1n", "B2n", 0, 4, yp)
    block("b14a", "B+1f", "B2f", 0, 3, ym)
    block("b14b", "B+1f", "B2f", 3, 1, ym)
    for n, dev in enumerate((cp, xp, dp)):
        msg("stat%d" % n, stat, pstat.at[n], dev)
    for n, dev in enumerate((cp, xp, dp)):
        msg("ot%d" % n, mot.at[n], pot.at[n], dev)
    for lh in range(2):
        msg("dq3%d" % lh, sd.at[lh], pd.at[lh], cp)
        msg("dq2%d" % lh, xd.at[lh], px.at[lh], xp)
    msg("dq1", sd.at[pl.ds(2, 2)], pd.at[pl.ds(2, 2)], cp)
    def back(name, source, target, first, count, dev, into=None):
        span = pl.ds(first, count)
        into = r1.at[AT[target], span] if into is None else r2.at[into, span]
        msg(name, snd.at[AT[source], span], into, dev)

    back("rA4m", "A4", "A-3", 0, 2, zm)
    back("rA4p", "A4", "A+3", 2, 2, zp)
    for half in range(2):
        span = 2 * half, 2

        def both(source, target, dev, into=None):
            back("r%s%d" % (source, half), source, target, *span, dev, into)

        both("A-3", "A-2", zm)
        both("A+3", "A+2", zp)
        both("A-2", "A-1", zm)
        both("A+2", "A+1", zp)
        both("A-1", "A0", zm)
        both("A+1", "A0", zp, 0)
        both("B2n", "B-1n", ym)
        both("B2f", "B+1f", yp)
        both("B-1n", "B0n", ym)
        both("B-1f", "B0f", ym)
        both("B+1n", "B0n", yp, 1)
        both("B+1f", "B0f", yp, 2)
    for n, dev in enumerate((ym, ym, yp)):
        msg("ry%d" % n, sy.at[n], ry.at[n], dev)
    for n, dev in enumerate((zm, zm, zm, zm, zp, zp, zp)):
        msg("rz%d" % n, sz.at[n], rz.at[n], dev)

    go("q20", "q21", "q1")
    for copy in pieces:
        copy.wait()
    go("ay1", "ay2", "bz1", "bz2", "azp0", "azm0", "byp0", "bym0", "g1")
    fetch[0].wait()

    for p, (row, column) in enumerate(
        ((inner, outer), (mate, outer), (inner, beside), (mate, beside))
    ):
        kt[4 * CHUNKS + p] = pos[row, 2 * column]
    for c in range(CHUNKS):
        for w in range(4):
            dy, dz = TABLE[c][w]
            kt[4 * c + w] = pos[inner, 2 * at(xx, dy, dz)]

    def spread(p, src, rows, cols):
        for h in range(HEADS):
            lanes = slice(h * DIM, (h + 1) * DIM)
            rows[p, h * BLK : (h + 1) * BLK, 0:DIM] = src[0:BLK, lanes]
            rows[p, h * BLK : (h + 1) * BLK, DIM : 2 * DIM] = src[BLK : 2 * BLK, lanes]
        cols[p] = rows[p].T

    fetch[1].wait()
    spread(0, mq, qn, qt)
    got("ay1", "ay2", "bz1", "bz2")
    go("ay3", "bz3", "bz4", "azp1", "azm1", "azp2", "azm2", "byp1", "bym1", "byp2", "bym2")
    got("q1")
    spread(1, pq.at[0], qn, qt)

    tok_k = lax.broadcasted_iota(jnp.int32, (BLK, ROWS), 0)
    tok_q = lax.broadcasted_iota(jnp.int32, (BLK, ROWS), 1) % BLK
    diag = tok_k <= tok_q

    def own(kind):
        return jnp.concatenate([buf[0, 0, kind], buf[1, 0, kind]], axis=0)

    for lh in range(2):
        s = jnp.where(diag, nt(own(lh), qt[0, lh * DIM : (lh + 1) * DIM]), NEG)
        m = row_max(s)
        p = jnp.exp2((s - m) * C2)
        stat[lh : lh + 1] = m
        ls[lh] = fold(p, jnp.sum)
        ot[0, lh * DIM : (lh + 1) * DIM] = tn(own(2 + lh), p.astype(jnp.bfloat16))
    stat[2:8] = jnp.full((6, ROWS), NEG, jnp.float32)
    ls[2:8] = jnp.zeros((6, 8, ROWS), jnp.float32)

    got("ay3", "bz3", "bz4")
    go("azp3", "azm3", "bz5", "bz6", "byp3", "bym3")
    for w in range(3):
        got("azp%d" % w, "azm%d" % w)
    go("a7a", "a8a")
    for p in range(1, 4):
        ot[p] = jnp.zeros((2 * DIM, ROWS), jnp.float32)
    for name in ("B+1n", "B2n", "B-1f", "B2f", "A4"):
        r1[AT[name]] = jnp.zeros((4, 4, HALF, DIM), jnp.bfloat16)
    r1[AT["A-3"], 2:4] = jnp.zeros((2, 4, HALF, DIM), jnp.bfloat16)
    r1[AT["A+3"], 0:2] = jnp.zeros((2, 4, HALF, DIM), jnp.bfloat16)

    got("azp3", "azm3", "bz5", "bz6")
    go("a7b", "a8b", "bz7", "b9a", "b10a")
    got("byp0", "byp1", "byp2", "byp3")
    go("b13")
    got("q20")
    go("q30")
    fetch[2].wait()
    spread(0, mg, gn, gt)
    def take(first, count, kind):
        return buf[pl.ds(first, count), :, kind].reshape(count * 4 * HALF, DIM)

    def picks(first, count, p):
        number = [kt[4 * first + w] for w in range(4 * count)]
        mine = kt[4 * CHUNKS + p]
        return [n < mine for n in number], [n == mine for n in number]

    def windows(x):
        return [x[w * HALF : (w + 1) * HALF] for w in range(x.shape[0] // HALF)]

    def cat(low, high, chosen):
        zero = jnp.zeros((HALF, DIM), jnp.bfloat16)
        rows = []
        for a, b, pick in zip(windows(low), windows(high), chosen):
            rows.append(
                jnp.concatenate([lax.select(pick, a, zero), lax.select(pick, zero, b)], axis=1)
            )
        return jnp.concatenate(rows, axis=0)

    neg_rows = jnp.full((8, ROWS), NEG, jnp.float32)
    big_row = jnp.full((1, ROWS), BIG, jnp.float32)
    high = slice(DIM, 2 * DIM)

    def row(ref, r):
        return ref[pl.ds(r, 1)]

    def arrive(n):
        def do(at_step, *steps):
            @pl.when(n == at_step)
            def _():
                for step, names in steps:
                    step(*names)

        @pl.when(n == 1)
        def _():
            got("q21")
            go("q31", "g20", "g21")
            spread(2, pq.at[1], qn, qt)
            got("q30", "q31")
            spread(3, pq.at[2], qn, qt)
            got("a7a", "a8a", "bz7")
            go("b9b", "b10b")

        do(2, (got, ["a7b", "a8b"]), (go, ["a11a", "a12a", "a11b", "a12b"]))
        do(2, (got, ["bym%d" % w for w in range(4)] + ["b10a"]), (go, ["b14a"]))
        do(3, (got, ["b10b"]), (go, ["b14b"]))
        do(4, (got, ["a11a", "a12a"]), (go, ["a15p", "a15m"]))
        do(4, (got, ["g20", "g21"]), (go, ["g30", "g31"]), (got, ["a11b", "a12b"]))
        do(6, (got, ["b14a", "b14b", "b9a", "b9b", "b13", "a15p", "a15m"]))

        @pl.when(n == 5)
        def _():
            got("g1", "g30", "g31")
            for p in range(1, 4):
                spread(p, pg.at[p - 1], gn, gt)

    def forward(n, carry):
        i, pair = n // 2, n % 2
        arrive(n)
        kl, kh, vl, vh = [take(4 * i, 4, kind) for kind in range(4)]
        parts = []
        for p in (2 * pair, 2 * pair + 1):
            low, same = picks(4 * i, 4, p)
            kcat, vcat = cat(kl, kh, low), cat(vl, vh, low)
            olds = [row(stat, 2 * p + lh) for lh in range(2)]
            parts.append((p, low, same, kcat, vcat, olds))

        def scores(part):
            p, _, _, kcat, _, _ = part
            return nt(kl, qt[p, high]), windows(nt(kcat, qt[p]))

        def weigh(part, s1, s2):
            p, low, same, _, vcat, (ml, mh) = part
            rl, rh = 2 * p, 2 * p + 1
            tops_l, tops_h = neg_rows, fold(s1, jnp.max)
            for w in range(16):
                top = fold(s2[w], jnp.max)
                tops_l = jnp.maximum(tops_l, lax.select(low[w], top, neg_rows))
                tops_h = jnp.maximum(tops_h, lax.select(low[w] | same[w], neg_rows, top))
            nl, nh = jnp.maximum(ml, row_max(tops_l)), jnp.maximum(mh, row_max(tops_h))
            fl, fh = jnp.exp2((ml - nl) * C2), jnp.exp2((mh - nh) * C2)
            p1 = jnp.exp2((s1 - nh) * C2)
            tl, th = ls[rl] * fl, ls[rh] * fh + fold(p1, jnp.sum)
            pieces = []
            for w in range(16):
                ref = lax.select(same[w], big_row, lax.select(low[w], nl, nh))
                piece = jnp.exp2((s2[w] - ref) * C2)
                total = fold(piece, jnp.sum)
                zero = jnp.zeros_like(total)
                tl = tl + lax.select(low[w], total, zero)
                th = th + lax.select(low[w], zero, total)
                pieces.append(piece.astype(jnp.bfloat16))
            ls[rl], ls[rh] = tl, th
            stat[pl.ds(rl, 1)], stat[pl.ds(rh, 1)] = nl, nh
            mc[i, pl.ds(rl, 1)], mc[i, pl.ds(rh, 1)] = nl, nh
            w1, w2 = p1.astype(jnp.bfloat16), jnp.concatenate(pieces, axis=0)
            wt[i, p, 0], wt[i, p, 1] = w1, w2
            return p, fl, fh, w1, w2, vcat

        def update(p, fl, fh, w1, w2, vcat):
            o1, o2 = tn(vl, w1), tn(vcat, w2)
            ot[p, 0:DIM] = ot[p, 0:DIM] * fl + o2[0:DIM]
            ot[p, high] = ot[p, high] * fh + (o1 + o2[high])

        now, late = scores(parts[0]), None
        for k in range(2):
            later = scores(parts[k + 1]) if k < 1 else None
            done = weigh(parts[k], *now)
            if late is not None:
                update(*late)
            now, late = later, done
        update(*late)
        return carry

    lax.fori_loop(0, 2 * STEPS, forward, 0)

    for p in range(4):
        for lh in range(2):
            r = 2 * p + lh
            stat[8 + r : 9 + r] = row_sum(ls[r])
            rows = slice(lh * DIM, (lh + 1) * DIM)
            stat[16 + r : 17 + r] = row_sum(ot[p, rows] * gt[p, rows].astype(jnp.float32))
    go("stat2", "stat1", "stat0")
    for n in range(3):
        mot[n] = ot[n + 1].astype(jnp.bfloat16)
    go("ot0", "ot1", "ot2")

    dqt[1:4] = jnp.zeros((3, 2 * DIM, ROWS), jnp.float32)
    early = [name for name in msgs if name[0] in "qgab"]
    for name in early:
        msgs[name].wait_send()
    got("stat0", "stat1", "stat2")
    for p in range(4):
        for lh in range(2):
            r = 2 * p + lh
            held = [(stat, r)] + [(pstat.at[n - 1], 2 * (p ^ n) + lh) for n in range(1, 4)]
            tops = [row(ref, at_row) for ref, at_row in held]
            top = jnp.maximum(jnp.maximum(tops[0], tops[1]), jnp.maximum(tops[2], tops[3]))
            factors = [jnp.exp2((m - top) * C2) for m in tops]
            total, delta = 0.0, 0.0
            for factor, (ref, at_row) in zip(factors, held):
                total = total + factor * row(ref, 8 + at_row)
                delta = delta + factor * row(ref, 16 + at_row)
            lse[r : r + 1] = top + jnp.log(total) * (1.0 / SCALE)
            lse[8 + r : 9 + r] = delta / total
            if p == 0:
                for n in range(4):
                    lse[16 + 2 * n + lh : 17 + 2 * n + lh] = factors[n] / total

    for lh in range(2):
        rows = slice(lh * DIM, (lh + 1) * DIM)
        s = jnp.where(diag, nt(own(lh), qt[0, rows]), NEG)
        p = jnp.exp2((s - lse[lh : lh + 1]) * C2)
        ds = (p * (nt(own(2 + lh), gt[0, rows]) - lse[8 + lh : 9 + lh])).astype(jnp.bfloat16)
        dk = nt(ds, qn[0, :, rows])
        dv = nt(p.astype(jnp.bfloat16), gn[0, :, rows])
        for half in range(2):
            dg[half, lh] = dk[half * HALF : (half + 1) * HALF]
            dg[half, 2 + lh] = dv[half * HALF : (half + 1) * HALF]
        dqt[0, rows] = tn(own(lh), ds)

    def total_of(c, w, slot, ref, *arrived):
        total = tf[c, w] + r1[c, w].astype(jnp.float32) + r2[slot, w].astype(jnp.float32)
        for n in arrived:
            total = total + ref[n].astype(jnp.float32)
        return total

    def b_total(dz, *arrived):
        got(*["rz%d" % n for n in arrived])
        for slot, c in ((1, 1), (2, far)):
            for w in range(4):
                if TABLE[c][w][1] == dz:
                    return total_of(c, w, slot, rz, *arrived)

    def chain(dz, leaving, *arrived):
        sz[leaving] = b_total(dz, *arrived).astype(jnp.bfloat16)
        go("rz%d" % leaving)

    def a_total(w, *arrived):
        got(*["ry%d" % n for n in arrived])
        return total_of(0, w, 0, ry, *arrived)

    def a_send(w, leaving, *arrived):
        sy[leaving] = a_total(w, *arrived).astype(jnp.bfloat16)
        go("ry%d" % leaving)

    def backward(n, carry):
        i = BACK_STEPS - 1 - n
        step, rows = i // 2, pl.ds((i % 2) * BACK_KEYS, BACK_KEYS)
        kl, kh, vl, vh = [take(2 * i, 2, kind) for kind in range(4)]
        parts = []
        for p in range(4):
            low, same = picks(2 * i, 2, p)
            parts.append((p, low, cat(vl, vh, low)))

        def dots(part):
            p, _, vcat = part
            return nt(vl, gt[p, high]), windows(nt(vcat, gt[p]))

        def work(part, g1, g2):
            p, low, _ = part
            rl, rh = 2 * p, 2 * p + 1
            el, eh = lse[8 + rl : 9 + rl], lse[8 + rh : 9 + rh]
            fl = jnp.exp2((mc[step, rl : rl + 1] - lse[rl : rl + 1]) * C2)
            fh = jnp.exp2((mc[step, rh : rh + 1] - lse[rh : rh + 1]) * C2)
            p1 = wt[step, p, 0, rows].astype(jnp.float32) * fh
            ds1 = (p1 * (g1 - eh)).astype(jnp.bfloat16)
            w2 = windows(wt[step, p, 1, rows].astype(jnp.float32))
            ps, ds = [], []
            for w in range(8):
                piece = w2[w] * lax.select(low[w], fl, fh)
                ps.append(piece.astype(jnp.bfloat16))
                ds.append((piece * (g2[w] - lax.select(low[w], el, eh))).astype(jnp.bfloat16))
            p2, ds2 = jnp.concatenate(ps, axis=0), jnp.concatenate(ds, axis=0)
            if p < 2:
                wt[step, p, 0, rows], wt[step, p, 1, rows] = ds1, ds2
            if p >= 2:
                one, two = tn(kl, ds1), tn(cat(kl, kh, low), ds2)
                dqt[p, 0:DIM] = dqt[p, 0:DIM] + two[0:DIM]
                dqt[p, high] = dqt[p, high] + (one + two[high])
            return p, low, p1.astype(jnp.bfloat16), ds1, p2, ds2

        def products(sums, p, low, p1, ds1, p2, ds2):
            new = []
            for one, two in (
                (nt(ds1, qn[p, :, high]), nt(ds2, qn[p])),
                (nt(p1, gn[p, :, high]), nt(p2, gn[p])),
            ):
                zero = jnp.zeros((HALF, DIM), jnp.float32)
                lows, highs = [], []
                for w in range(8):
                    here = slice(w * HALF, (w + 1) * HALF)
                    lows.append(one[here] + lax.select(low[w], two[here, 0:DIM], zero))
                    highs.append(lax.select(low[w], zero, two[here, high]))
                new += [lows, highs]
            if sums is None:
                return new
            return [[a + b for a, b in zip(x, y)] for x, y in zip(sums, new)]

        sums, late = None, None
        now = dots(parts[0])
        for k in range(4):
            later = dots(parts[k + 1]) if k < 3 else None
            done = work(parts[k], *now)
            if late is not None:
                sums = products(sums, *late)
            now, late = later, done
        sums = products(sums, *late)
        for kind in range(4):
            for w in range(8):
                tf[2 * i + w // 4, w % 4, kind] = sums[kind][w]

        def finish(at_step, *chunks):
            @pl.when(i == at_step)
            def _():
                for name, waits in chunks:
                    for half in (1, 0) if name in ("A-1", "A+1") else (0, 1):
                        c, span = AT[name], pl.ds(2 * half, 2)
                        if waits[half]:
                            got(waits[half])
                        total = tf[c, span] + r1[c, span].astype(jnp.float32)
                        snd[c, span] = total.astype(jnp.bfloat16)
                        go(("rA4m", "rA4p")[half] if name == "A4" else "r%s%d" % (name, half))

        def upstream(name):
            return ["r%s%d" % (name, half) for half in range(2)]

        none = [None, None]
        finish(7, ("A4", none), ("B2n", none))
        finish(6, ("B2f", none), ("B-1f", none))
        finish(5, ("A-3", ["rA4m", None]), ("A+3", [None, "rA4p"]))
        finish(4, ("B-1n", upstream("B2n")), ("B+1f", upstream("B2f")))
        finish(3, ("A-2", upstream("A-3")), ("A+2", upstream("A+3")))
        finish(2, ("B+1n", none))
        finish(1, ("A-1", upstream("A-2")), ("A+1", upstream("A+2")))

        @pl.when(i == 2)
        def _():
            got("rB-1f0", "rB-1f1", "rB+1f0", "rB+1f1")
            chain(4, 0)
            chain(3, 4)

        @pl.when(i == 1)
        def _():
            chain(-3, 1, 0)
            chain(2, 5, 4)

        return carry

    lax.fori_loop(0, BACK_STEPS, backward, 0)

    def store(ref, rows):
        for h in range(HEADS):
            lanes = slice(h * DIM, (h + 1) * DIM)
            ref[0:BLK, lanes] = rows[h * BLK : (h + 1) * BLK, 0:DIM]
            ref[BLK : 2 * BLK, lanes] = rows[h * BLK : (h + 1) * BLK, DIM : 2 * DIM]

    leave = [
        pltpu.make_async_copy(src, dst, lsem.at[11 + n])
        for n, (src, dst) in enumerate(
            ((att_ref, att_out), (dq_ref, dq_out), (dk_ref, dk_out), (dv_ref, dv_out))
        )
    ]

    def attend():
        got("ot0", "ot1", "ot2")
        halves = []
        for lh in range(2):
            rows = slice(lh * DIM, (lh + 1) * DIM)
            total = ot[0, rows] * lse[16 + lh : 17 + lh]
            for n in range(1, 4):
                total = total + pot[n - 1, rows].astype(jnp.float32) * lse[16 + 2 * n + lh : 17 + 2 * n + lh]
            halves.append(total)
        store(att_ref, jnp.concatenate(halves, axis=0).T.astype(jnp.bfloat16))

    for lh in range(2):
        sd[lh] = dqt[3, lh * DIM : (lh + 1) * DIM].astype(jnp.bfloat16)
        go("dq3%d" % lh)
    got("rB-1n0", "rB-1n1", "rB+1n0", "rB+1n1")
    chain(-2, 2, 1)
    chain(1, 6, 5)
    attend()
    leave[0].start()
    for lh in range(2):
        got("dq3%d" % lh)
        part = dqt[2, lh * DIM : (lh + 1) * DIM] + pd[lh].astype(jnp.float32)
        xd[lh] = part.astype(jnp.bfloat16)
        go("dq2%d" % lh)

    def queries_back(n, carry):
        def stage(at_step):
            return pl.when(n == at_step)

        @stage(0)
        def _():
            got("rA-11", "rA+11")
            a_send(3, 0)
            a_send(2, 2)

        @stage(2)
        def _():
            for lh in range(2):
                sd[2 + lh] = dqt[1, lh * DIM : (lh + 1) * DIM].astype(jnp.bfloat16)
            go("dq1")
            chain(-1, 3, 2)
            got("rA-10", "rA+10")
            a_send(1, 1, 0)

        p = 1 - n // 2
        lows, cats, d1, d2 = [], [], [], []
        for k in range(2):
            i = 2 * (n % 2) + k
            kl, kh = take(4 * i, 4, 0), take(4 * i, 4, 1)
            low, same = picks(4 * i, 4, p)
            lows.append(kl)
            cats.append(cat(kl, kh, low))
            d1.append(wt[i, p, 0])
            d2.append(wt[i, p, 1])
        one = tn(jnp.concatenate(lows, axis=0), jnp.concatenate(d1, axis=0))
        two = tn(jnp.concatenate(cats, axis=0), jnp.concatenate(d2, axis=0))
        dqt[p, 0:DIM] = dqt[p, 0:DIM] + two[0:DIM]
        dqt[p, high] = dqt[p, high] + (one + two[high])
        return carry

    lax.fori_loop(0, 4, queries_back, 0)

    for half, total in enumerate((a_total(0, 1, 2), b_total(0, 3, 6))):
        total = total + dg[half]
        for lh in range(2):
            rows = slice(lh * BLK + half * HALF, lh * BLK + (half + 1) * HALF)
            dk_ref[rows, :] = (total[lh] * SCALE).astype(jnp.bfloat16)
            dv_ref[rows, :] = total[2 + lh].astype(jnp.bfloat16)

    leave[2].start()
    leave[3].start()
    got("dq1", "dq20", "dq21")
    halves = []
    for lh in range(2):
        part = dqt[0, lh * DIM : (lh + 1) * DIM] + pd[2 + lh].astype(jnp.float32)
        halves.append(part + px[lh].astype(jnp.float32))
    store(dq_ref, (jnp.concatenate(halves, axis=0) * SCALE).T.astype(jnp.bfloat16))
    leave[1].start()
    for name, copy in msgs.items():
        if name not in early:
            copy.wait_send()
    for copy in leave:
        copy.wait()


def hand_out(*refs):
    for source, target in zip(refs[:4], refs[4:]):
        target[...] = source[...]


def body(queries, keys, values, grad_out, block_pos):
    bf, f32 = jnp.bfloat16, jnp.float32
    window = (4, HALF, DIM)
    raw = (2 * BLK, HEADS * DIM)
    count = 108
    shapes = [
        jax.ShapeDtypeStruct(raw, bf),
        jax.ShapeDtypeStruct(raw, bf),
        jax.ShapeDtypeStruct((2 * BLK, DIM), bf),
        jax.ShapeDtypeStruct((2 * BLK, DIM), bf),
    ]
    outs = pl.pallas_call(
        kernel,
        out_shape=shapes,
        in_specs=[pl.BlockSpec(memory_space=pltpu.HBM)] * 5,
        out_specs=[pl.BlockSpec(memory_space=pltpu.HBM)] * 4,
        scratch_shapes=[
            pltpu.VMEM(raw, bf),
            pltpu.VMEM(raw, bf),
            pltpu.VMEM((2 * BLK, DIM), bf),
            pltpu.VMEM((2 * BLK, DIM), bf),
            pltpu.VMEM((CHUNKS, 4) + window, bf),
            pltpu.VMEM(raw, bf),
            pltpu.VMEM(raw, bf),
            pltpu.VMEM((3,) + raw, bf),
            pltpu.VMEM((3,) + raw, bf),
            pltpu.VMEM((4, ROWS, 2 * DIM), bf),
            pltpu.VMEM((4, ROWS, 2 * DIM), bf),
            pltpu.VMEM((4, 2 * DIM, ROWS), bf),
            pltpu.VMEM((4, 2 * DIM, ROWS), bf),
            pltpu.VMEM((4, 2 * DIM, ROWS), f32),
            pltpu.VMEM((4, 2 * DIM, ROWS), f32),
            pltpu.VMEM((24, ROWS), f32),
            pltpu.VMEM((8, 8, ROWS), f32),
            pltpu.VMEM((3, 24, ROWS), f32),
            pltpu.VMEM((24, ROWS), f32),
            pltpu.VMEM((STEPS, 8, ROWS), f32),
            pltpu.VMEM((STEPS, 4, 2, KEYS, ROWS), bf),
            pltpu.VMEM((3, 2 * DIM, ROWS), bf),
            pltpu.VMEM((3, 2 * DIM, ROWS), bf),
            pltpu.VMEM((4, DIM, ROWS), bf),
            pltpu.VMEM((4, DIM, ROWS), bf),
            pltpu.VMEM((2, DIM, ROWS), bf),
            pltpu.VMEM((2, DIM, ROWS), bf),
            pltpu.VMEM((CHUNKS, 4) + window, f32),
            pltpu.VMEM((CHUNKS, 4) + window, bf),
            pltpu.VMEM((CHUNKS, 4) + window, bf),
            pltpu.VMEM((3, 4) + window, bf),
            pltpu.VMEM((3,) + window, bf),
            pltpu.VMEM((3,) + window, bf),
            pltpu.VMEM((7,) + window, bf),
            pltpu.VMEM((7,) + window, bf),
            pltpu.VMEM((2,) + window, f32),
            pltpu.SMEM((4, 2 * BLK), jnp.int32),
            pltpu.SMEM((4 * CHUNKS + 4,), jnp.int32),
            pltpu.SemaphoreType.DMA((15,)),
            pltpu.SemaphoreType.DMA((count,)),
            pltpu.SemaphoreType.DMA((count,)),
        ],
        compiler_params=pltpu.CompilerParams(
            collective_id=0, has_side_effects=True, vmem_limit_bytes=54 * 1024 * 1024
        ),
        name="attention",
    )(block_pos, queries[0], keys[0], values[0], grad_out[0])
    outs = pl.pallas_call(
        hand_out,
        out_shape=shapes,
        in_specs=[pl.BlockSpec(one.shape, lambda n: (0, 0)) for one in shapes],
        out_specs=[pl.BlockSpec(one.shape, lambda n: (0, 0)) for one in shapes],
        grid=(1,),
        compiler_params=pltpu.CompilerParams(vmem_limit_bytes=54 * 1024 * 1024),
        name="hand_out",
    )(*outs)
    return tuple(out[None] for out in outs)


def solution(mesh):
    spec = P("inner", "outer", None)
    return jax.shard_map(
        body,
        mesh=mesh,
        in_specs=(spec, spec, spec, spec, P()),
        out_specs=(spec, spec, spec, spec),
        check_vma=False,
    )
```

```python
import jax
import jax.numpy as jnp
from jax import lax
from jax.experimental import pallas as pl
from jax.experimental.pallas import tpu as pltpu
from jax.sharding import PartitionSpec as P

MESH = pl.DeviceIdType.MESH
NEG = -1e30
BIG = 1e30
BLK = 64
HALF = 32
DIM = 128
HEADS = 8
ROWS = BLK * HEADS
CHUNKS = 16
STEPS = 4
BACK_STEPS = 8
KEYS = 16 * HALF
BACK_KEYS = 8 * HALF
SCALE = DIM**-0.5
C2 = SCALE * 1.4426950408889634

YORDER = (0, -1, 1, 2)
NEAR = (0, -1, 1, -2)
FAR = (2, -3, 3, 4)


def a_chunk(dz):
    return [(dy, dz) for dy in YORDER]


def b_chunk(dy, part):
    return [(dy, dz) for dz in part]


NAMES = (
    ("A0", a_chunk(0)),
    ("B0n", b_chunk(0, NEAR)),
    ("A-1", a_chunk(-1)),
    ("A+1", a_chunk(1)),
    ("B+1n", b_chunk(1, NEAR)),
    ("B0f", b_chunk(0, FAR)),
    ("A-2", a_chunk(-2)),
    ("A+2", a_chunk(2)),
    ("B-1n", b_chunk(-1, NEAR)),
    ("B+1f", b_chunk(1, FAR)),
    ("A-3", a_chunk(-3)),
    ("A+3", a_chunk(3)),
    ("B2f", b_chunk(2, FAR)),
    ("B-1f", b_chunk(-1, FAR)),
    ("B2n", b_chunk(2, NEAR)),
    ("A4", a_chunk(4)),
)
TABLE = [windows for _, windows in NAMES]
AT = {name: number for number, (name, _) in enumerate(NAMES)}


def nt(a, b):
    return lax.dot_general(a, b, (((1,), (0,)), ((), ())), preferred_element_type=jnp.float32)


def tn(a, b):
    return lax.dot_general(a, b, (((0,), (0,)), ((), ())), preferred_element_type=jnp.float32)


def across(a, b):
    return lax.dot_general(a, b, (((1,), (1,)), ((), ())), preferred_element_type=jnp.float32)


def fold(x, op):
    rows, lanes = x.shape
    return op(x.reshape(rows // 8, 8, lanes), axis=0)


def row_sum(x):
    return jnp.sum(x, axis=0, keepdims=True)


def row_max(x):
    return jnp.max(x, axis=0, keepdims=True)


def kernel(
    pos_ref,
    q_ref,
    k_ref,
    v_ref,
    g_ref,
    att_out,
    dq_out,
    dk_out,
    dv_out,
    att_ref,
    dq_ref,
    dk_ref,
    dv_ref,
    buf,
    mq,
    mg,
    pq,
    pg,
    qn,
    gn,
    qt,
    gt,
    ot,
    dqt,
    stat,
    ls,
    pstat,
    lse,
    mc,
    wt,
    mot,
    pot,
    sd,
    pd,
    xd,
    px,
    tf,
    snd,
    r1,
    r2,
    sy,
    ry,
    sz,
    rz,
    dg,
    pos,
    kt,
    lsem,
    ssem,
    rsem,
):
    outer = lax.axis_index("outer")
    inner = lax.axis_index("inner")
    yy = outer // 16
    xx = (outer // 8) % 2
    zz = outer % 8
    mate = inner + 1 - 2 * (inner % 2)

    def at(x, dy, dz):
        return (((yy + dy + 4) % 4) * 2 + x) * 8 + (zz + dz + 8) % 8

    beside = at(1 - xx, 0, 0)
    yp, ym = (at(xx, 1, 0), inner), (at(xx, -1, 0), inner)
    zp, zm = (at(xx, 0, 1), inner), (at(xx, 0, -1), inner)
    cp, xp, dp = (outer, mate), (beside, inner), (beside, mate)

    barrier = pltpu.get_barrier_semaphore()
    for dev in (yp, ym, zp, zm, cp, xp, dp):
        pl.semaphore_signal(barrier, inc=1, device_id=dev, device_id_type=MESH)

    fetch = [
        pltpu.make_async_copy(pos_ref, pos, lsem.at[0]),
        pltpu.make_async_copy(q_ref, mq, lsem.at[1]),
        pltpu.make_async_copy(g_ref, mg, lsem.at[2]),
    ]
    pieces = []
    for n, ref in enumerate((k_ref, v_ref)):
        for lh in range(2):
            for half in range(2):
                pieces.append(
                    pltpu.make_async_copy(
                        ref.at[pl.ds(lh * BLK + half * HALF, HALF)],
                        buf.at[half, 0, 2 * n + lh],
                        lsem.at[3 + len(pieces)],
                    )
                )
    for copy in pieces + fetch:
        copy.start()
    pl.semaphore_wait(barrier, 7)

    msgs = {}

    def msg(name, src, dst, dev):
        at_sem = len(msgs)
        msgs[name] = pltpu.make_async_remote_copy(
            src_ref=src,
            dst_ref=dst,
            send_sem=ssem.at[at_sem],
            recv_sem=rsem.at[at_sem],
            device_id=dev,
            device_id_type=MESH,
        )

    def go(*names):
        for name in names:
            msgs[name].start()

    def got(*names):
        for name in names:
            msgs[name].wait_recv()

    for name, src, dst in (("q", q_ref, pq), ("g", g_ref, pg)):
        msg(name + "1", src, dst.at[0], cp)
        for half in range(2):
            span = pl.ds(half * BLK, BLK)
            msg("%s2%d" % (name, half), src.at[span], dst.at[1, span], xp)
            msg("%s3%d" % (name, half), dst.at[1, span], dst.at[2, span], cp)
    msg("ay1", buf.at[0, 0], buf.at[0, 1], yp)
    msg("ay2", buf.at[0, 0], buf.at[0, 2], ym)
    msg("ay3", buf.at[0, 1], buf.at[0, 3], yp)
    for w in range(4):
        msg("azp%d" % w, buf.at[0, w], buf.at[AT["A-1"], w], zp)
        msg("azm%d" % w, buf.at[0, w], buf.at[AT["A+1"], w], zm)
        msg("byp%d" % w, buf.at[1, w], buf.at[AT["B-1n"], w], yp)
        msg("bym%d" % w, buf.at[1, w], buf.at[AT["B+1n"], w], ym)

    def block(name, source, target, first, count, dev):
        span = pl.ds(first, count)
        msg(name, buf.at[AT[source], span], buf.at[AT[target], span], dev)

    block("a7a", "A-1", "A-2", 0, 3, zp)
    block("a7b", "A-1", "A-2", 3, 1, zp)
    block("a8a", "A+1", "A+2", 0, 3, zm)
    block("a8b", "A+1", "A+2", 3, 1, zm)
    block("a11a", "A-2", "A-3", 0, 2, zp)
    block("a11b", "A-2", "A-3", 2, 2, zp)
    block("a12a", "A+2", "A+3", 2, 2, zm)
    block("a12b", "A+2", "A+3", 0, 2, zm)
    block("a15p", "A-3", "A4", 0, 2, zp)
    block("a15m", "A+3", "A4", 2, 2, zm)
    far = AT["B0f"]
    msg("bz1", buf.at[1, 0], buf.at[1, 1], zp)
    msg("bz2", buf.at[1, 0], buf.at[1, 2], zm)
    msg("bz3", buf.at[1, 1], buf.at[1, 3], zp)
    msg("bz4", buf.at[1, 2], buf.at[far, 0], zm)
    msg("bz5", buf.at[1, 3], buf.at[far, 1], zp)
    msg("bz6", buf.at[far, 0], buf.at[far, 2], zm)
    msg("bz7", buf.at[far, 1], buf.at[far, 3], zp)
    block("b9a", "B0f", "B-1f", 0, 3, yp)
    block("b9b", "B0f", "B-1f", 3, 1, yp)
    block("b10a", "B0f", "B+1f", 0, 3, ym)
    block("b10b", "B0f", "B+1f", 3, 1, ym)
    block("b13", "B-1n", "B2n", 0, 4, yp)
    block("b14a", "B+1f", "B2f", 0, 3, ym)
    block("b14b", "B+1f", "B2f", 3, 1, ym)
    for n, dev in enumerate((cp, xp, dp)):
        msg("stat%d" % n, stat, pstat.at[n], dev)
    for n, dev in enumerate((cp, xp, dp)):
        msg("ot%d" % n, mot.at[n], pot.at[n], dev)
    for lh in range(2):
        msg("dq3%d" % lh, sd.at[lh], pd.at[lh], cp)
        msg("dq2%d" % lh, xd.at[lh], px.at[lh], xp)
    msg("dq1", sd.at[pl.ds(2, 2)], pd.at[pl.ds(2, 2)], cp)
    def back(name, source, target, first, count, dev, into=None):
        span = pl.ds(first, count)
        into = r1.at[AT[target], span] if into is None else r2.at[into, span]
        msg(name, snd.at[AT[source], span], into, dev)

    back("rA4m", "A4", "A-3", 0, 2, zm)
    back("rA4p", "A4", "A+3", 2, 2, zp)
    for half in range(2):
        span = 2 * half, 2

        def both(source, target, dev, into=None):
            back("r%s%d" % (source, half), source, target, *span, dev, into)

        both("A-3", "A-2", zm)
        both("A+3", "A+2", zp)
        both("A-2", "A-1", zm)
        both("A+2", "A+1", zp)
        both("A-1", "A0", zm)
        both("A+1", "A0", zp, 0)
        both("B2n", "B-1n", ym)
        both("B2f", "B+1f", yp)
        both("B-1n", "B0n", ym)
        both("B-1f", "B0f", ym)
        both("B+1n", "B0n", yp, 1)
        both("B+1f", "B0f", yp, 2)
    for n, dev in enumerate((ym, ym, yp)):
        msg("ry%d" % n, sy.at[n], ry.at[n], dev)
    for n, dev in enumerate((zm, zm, zm, zm, zp, zp, zp)):
        msg("rz%d" % n, sz.at[n], rz.at[n], dev)

    go("q20", "q21", "q1")
    for copy in pieces:
        copy.wait()
    go("ay1", "ay2", "bz1", "bz2", "azp0", "azm0", "byp0", "bym0", "g1")
    fetch[0].wait()

    for p, (row, column) in enumerate(
        ((inner, outer), (mate, outer), (inner, beside), (mate, beside))
    ):
        kt[4 * CHUNKS + p] = pos[row, 2 * column]
    for c in range(CHUNKS):
        for w in range(4):
            dy, dz = TABLE[c][w]
            kt[4 * c + w] = pos[inner, 2 * at(xx, dy, dz)]

    def spread(p, src, rows, cols):
        for h in range(HEADS):
            lanes = slice(h * DIM, (h + 1) * DIM)
            rows[p, h * BLK : (h + 1) * BLK, 0:DIM] = src[0:BLK, lanes]
            rows[p, h * BLK : (h + 1) * BLK, DIM : 2 * DIM] = src[BLK : 2 * BLK, lanes]
        cols[p] = rows[p].T

    fetch[1].wait()
    spread(0, mq, qn, qt)
    got("ay1", "ay2", "bz1", "bz2")
    go("ay3", "bz3", "bz4", "azp1", "azm1", "azp2", "azm2", "byp1", "bym1", "byp2", "bym2")
    got("q1")
    spread(1, pq.at[0], qn, qt)

    tok_k = lax.broadcasted_iota(jnp.int32, (BLK, ROWS), 0)
    tok_q = lax.broadcasted_iota(jnp.int32, (BLK, ROWS), 1) % BLK
    diag = tok_k <= tok_q

    def own(kind):
        return jnp.concatenate([buf[0, 0, kind], buf[1, 0, kind]], axis=0)

    for lh in range(2):
        s = jnp.where(diag, nt(own(lh), qt[0, lh * DIM : (lh + 1) * DIM]), NEG)
        m = row_max(s)
        p = jnp.exp2((s - m) * C2)
        stat[lh : lh + 1] = m
        ls[lh] = fold(p, jnp.sum)
        ot[0, lh * DIM : (lh + 1) * DIM] = tn(own(2 + lh), p.astype(jnp.bfloat16))
    stat[2:8] = jnp.full((6, ROWS), NEG, jnp.float32)
    ls[2:8] = jnp.zeros((6, 8, ROWS), jnp.float32)

    got("ay3", "bz3", "bz4")
    go("azp3", "azm3", "bz5", "bz6", "byp3", "bym3")
    for w in range(3):
        got("azp%d" % w, "azm%d" % w)
    go("a7a", "a8a")
    for p in range(1, 4):
        ot[p] = jnp.zeros((2 * DIM, ROWS), jnp.float32)
    for name in ("B+1n", "B2n", "B-1f", "B2f", "A4"):
        r1[AT[name]] = jnp.zeros((4, 4, HALF, DIM), jnp.bfloat16)
    r1[AT["A-3"], 2:4] = jnp.zeros((2, 4, HALF, DIM), jnp.bfloat16)
    r1[AT["A+3"], 0:2] = jnp.zeros((2, 4, HALF, DIM), jnp.bfloat16)

    got("azp3", "azm3", "bz5", "bz6")
    go("a7b", "a8b", "bz7", "b9a", "b10a")
    got("byp0", "byp1", "byp2", "byp3")
    go("b13")
    got("q20")
    go("q30")
    fetch[2].wait()
    spread(0, mg, gn, gt)
    def take(first, count, kind):
        return buf[pl.ds(first, count), :, kind].reshape(count * 4 * HALF, DIM)

    def picks(first, count, p):
        number = [kt[4 * first + w] for w in range(4 * count)]
        mine = kt[4 * CHUNKS + p]
        return [n < mine for n in number], [n == mine for n in number]

    def windows(x):
        return [x[w * HALF : (w + 1) * HALF] for w in range(x.shape[0] // HALF)]

    def cat(low, high, chosen):
        zero = jnp.zeros((HALF, DIM), jnp.bfloat16)
        rows = []
        for a, b, pick in zip(windows(low), windows(high), chosen):
            rows.append(
                jnp.concatenate([lax.select(pick, a, zero), lax.select(pick, zero, b)], axis=1)
            )
        return jnp.concatenate(rows, axis=0)

    neg_rows = jnp.full((8, ROWS), NEG, jnp.float32)
    big_row = jnp.full((1, ROWS), BIG, jnp.float32)
    high = slice(DIM, 2 * DIM)

    def row(ref, r):
        return ref[pl.ds(r, 1)]

    def arrive(n):
        def do(at_step, *steps):
            @pl.when(n == at_step)
            def _():
                for step, names in steps:
                    step(*names)

        @pl.when(n == 1)
        def _():
            got("q21")
            go("q31", "g20", "g21")
            spread(2, pq.at[1], qn, qt)
            got("q30", "q31")
            spread(3, pq.at[2], qn, qt)
            got("a7a", "a8a", "bz7")
            go("b9b", "b10b")

        do(2, (got, ["a7b", "a8b"]), (go, ["a11a", "a12a", "a11b", "a12b"]))
        do(2, (got, ["bym%d" % w for w in range(4)] + ["b10a"]), (go, ["b14a"]))
        do(3, (got, ["b10b"]), (go, ["b14b"]))
        do(4, (got, ["a11a", "a12a"]), (go, ["a15p", "a15m"]))
        do(4, (got, ["g20", "g21"]), (go, ["g30", "g31"]), (got, ["a11b", "a12b"]))
        do(6, (got, ["b14a", "b14b", "b9a", "b9b", "b13", "a15p", "a15m"]))

        @pl.when(n == 5)
        def _():
            got("g1", "g30", "g31")
            for p in range(1, 4):
                spread(p, pg.at[p - 1], gn, gt)

    def forward(n, carry):
        i, pair = n // 2, n % 2
        arrive(n)
        kl, kh, vl, vh = [take(4 * i, 4, kind) for kind in range(4)]
        parts = []
        for p in (2 * pair, 2 * pair + 1):
            low, same = picks(4 * i, 4, p)
            kcat, vcat = cat(kl, kh, low), cat(vl, vh, low)
            olds = [row(stat, 2 * p + lh) for lh in range(2)]
            parts.append((p, low, same, kcat, vcat, olds))

        def scores(part):
            p, _, _, kcat, _, _ = part
            return nt(kl, qt[p, high]), windows(nt(kcat, qt[p]))

        def weigh(part, s1, s2):
            p, low, same, _, vcat, (ml, mh) = part
            rl, rh = 2 * p, 2 * p + 1
            tops_l, tops_h = neg_rows, fold(s1, jnp.max)
            for w in range(16):
                top = fold(s2[w], jnp.max)
                tops_l = jnp.maximum(tops_l, lax.select(low[w], top, neg_rows))
                tops_h = jnp.maximum(tops_h, lax.select(low[w] | same[w], neg_rows, top))
            nl, nh = jnp.maximum(ml, row_max(tops_l)), jnp.maximum(mh, row_max(tops_h))
            fl, fh = jnp.exp2((ml - nl) * C2), jnp.exp2((mh - nh) * C2)
            p1 = jnp.exp2((s1 - nh) * C2)
            tl, th = ls[rl] * fl, ls[rh] * fh + fold(p1, jnp.sum)
            pieces = []
            for w in range(16):
                ref = lax.select(same[w], big_row, lax.select(low[w], nl, nh))
                piece = jnp.exp2((s2[w] - ref) * C2)
                total = fold(piece, jnp.sum)
                zero = jnp.zeros_like(total)
                tl = tl + lax.select(low[w], total, zero)
                th = th + lax.select(low[w], zero, total)
                pieces.append(piece.astype(jnp.bfloat16))
            ls[rl], ls[rh] = tl, th
            stat[pl.ds(rl, 1)], stat[pl.ds(rh, 1)] = nl, nh
            mc[i, pl.ds(rl, 1)], mc[i, pl.ds(rh, 1)] = nl, nh
            w1, w2 = p1.astype(jnp.bfloat16), jnp.concatenate(pieces, axis=0)
            wt[i, p, 0], wt[i, p, 1] = w1, w2
            return p, fl, fh, w1, w2, vcat

        def update(p, fl, fh, w1, w2, vcat):
            o1, o2 = tn(vl, w1), tn(vcat, w2)
            ot[p, 0:DIM] = ot[p, 0:DIM] * fl + o2[0:DIM]
            ot[p, high] = ot[p, high] * fh + (o1 + o2[high])

        now, late = scores(parts[0]), None
        for k in range(2):
            later = scores(parts[k + 1]) if k < 1 else None
            done = weigh(parts[k], *now)
            if late is not None:
                update(*late)
            now, late = later, done
        update(*late)
        return carry

    lax.fori_loop(0, 2 * STEPS, forward, 0)

    for p in range(4):
        for lh in range(2):
            r = 2 * p + lh
            stat[8 + r : 9 + r] = row_sum(ls[r])
            rows = slice(lh * DIM, (lh + 1) * DIM)
            stat[16 + r : 17 + r] = row_sum(ot[p, rows] * gt[p, rows].astype(jnp.float32))
    go("stat2", "stat1", "stat0")
    for n in range(3):
        mot[n] = ot[n + 1].astype(jnp.bfloat16)
    go("ot0", "ot1", "ot2")

    dqt[1:4] = jnp.zeros((3, 2 * DIM, ROWS), jnp.float32)
    early = [name for name in msgs if name[0] in "qgab"]
    for name in early:
        msgs[name].wait_send()
    got("stat0", "stat1", "stat2")
    for p in range(4):
        for lh in range(2):
            r = 2 * p + lh
            held = [(stat, r)] + [(pstat.at[n - 1], 2 * (p ^ n) + lh) for n in range(1, 4)]
            tops = [row(ref, at_row) for ref, at_row in held]
            top = jnp.maximum(jnp.maximum(tops[0], tops[1]), jnp.maximum(tops[2], tops[3]))
            factors = [jnp.exp2((m - top) * C2) for m in tops]
            total, delta = 0.0, 0.0
            for factor, (ref, at_row) in zip(factors, held):
                total = total + factor * row(ref, 8 + at_row)
                delta = delta + factor * row(ref, 16 + at_row)
            lse[r : r + 1] = top + jnp.log(total) * (1.0 / SCALE)
            lse[8 + r : 9 + r] = delta / total
            if p == 0:
                for n in range(4):
                    lse[16 + 2 * n + lh : 17 + 2 * n + lh] = factors[n] / total

    for lh in range(2):
        rows = slice(lh * DIM, (lh + 1) * DIM)
        s = jnp.where(diag, nt(own(lh), qt[0, rows]), NEG)
        p = jnp.exp2((s - lse[lh : lh + 1]) * C2)
        ds = (p * (nt(own(2 + lh), gt[0, rows]) - lse[8 + lh : 9 + lh])).astype(jnp.bfloat16)
        dk = nt(ds, qn[0, :, rows])
        dv = nt(p.astype(jnp.bfloat16), gn[0, :, rows])
        for half in range(2):
            dg[half, lh] = dk[half * HALF : (half + 1) * HALF]
            dg[half, 2 + lh] = dv[half * HALF : (half + 1) * HALF]
        dqt[0, rows] = tn(own(lh), ds)

    def total_of(c, w, slot, ref, *arrived):
        total = tf[c, w] + r1[c, w].astype(jnp.float32) + r2[slot, w].astype(jnp.float32)
        for n in arrived:
            total = total + ref[n].astype(jnp.float32)
        return total

    def b_total(dz, *arrived):
        got(*["rz%d" % n for n in arrived])
        for slot, c in ((1, 1), (2, far)):
            for w in range(4):
                if TABLE[c][w][1] == dz:
                    return total_of(c, w, slot, rz, *arrived)

    def chain(dz, leaving, *arrived):
        sz[leaving] = b_total(dz, *arrived).astype(jnp.bfloat16)
        go("rz%d" % leaving)

    def a_total(w, *arrived):
        got(*["ry%d" % n for n in arrived])
        return total_of(0, w, 0, ry, *arrived)

    def a_send(w, leaving, *arrived):
        sy[leaving] = a_total(w, *arrived).astype(jnp.bfloat16)
        go("ry%d" % leaving)

    def backward(n, carry):
        i = BACK_STEPS - 1 - n
        step, rows = i // 2, pl.ds((i % 2) * BACK_KEYS, BACK_KEYS)
        kl, kh, vl, vh = [take(2 * i, 2, kind) for kind in range(4)]
        parts = []
        for p in range(4):
            low, same = picks(2 * i, 2, p)
            parts.append((p, low, cat(vl, vh, low)))

        def dots(part):
            p, _, vcat = part
            return nt(vl, gt[p, high]), windows(nt(vcat, gt[p]))

        def work(part, g1, g2):
            p, low, _ = part
            rl, rh = 2 * p, 2 * p + 1
            el, eh = lse[8 + rl : 9 + rl], lse[8 + rh : 9 + rh]
            fl = jnp.exp2((mc[step, rl : rl + 1] - lse[rl : rl + 1]) * C2)
            fh = jnp.exp2((mc[step, rh : rh + 1] - lse[rh : rh + 1]) * C2)
            p1 = wt[step, p, 0, rows].astype(jnp.float32) * fh
            ds1 = (p1 * (g1 - eh)).astype(jnp.bfloat16)
            w2 = windows(wt[step, p, 1, rows].astype(jnp.float32))
            ps, ds = [], []
            for w in range(8):
                piece = w2[w] * lax.select(low[w], fl, fh)
                ps.append(piece.astype(jnp.bfloat16))
                ds.append((piece * (g2[w] - lax.select(low[w], el, eh))).astype(jnp.bfloat16))
            p2, ds2 = jnp.concatenate(ps, axis=0), jnp.concatenate(ds, axis=0)
            if p < 2:
                wt[step, p, 0, rows], wt[step, p, 1, rows] = ds1, ds2
            if p >= 2:
                one, two = tn(kl, ds1), tn(cat(kl, kh, low), ds2)
                dqt[p, 0:DIM] = dqt[p, 0:DIM] + two[0:DIM]
                dqt[p, high] = dqt[p, high] + (one + two[high])
            return p, low, p1.astype(jnp.bfloat16), ds1, p2, ds2

        def products(sums, p, low, p1, ds1, p2, ds2):
            news = []
            for two in (nt(ds2, qn[p]), nt(p2, gn[p])):
                zero = jnp.zeros((HALF, DIM), jnp.float32)
                lows, highs = [], []
                for w in range(8):
                    here = slice(w * HALF, (w + 1) * HALF)
                    lows.append(lax.select(low[w], two[here, 0:DIM], zero))
                    highs.append(lax.select(low[w], zero, two[here, high]))
                news += [lows, highs]
            turned = [across(qt[p, high], ds1), across(gt[p, high], p1)]
            if sums is None:
                return news, turned
            old, last = sums
            news = [[a + b for a, b in zip(x, y)] for x, y in zip(old, news)]
            return news, [a + b for a, b in zip(last, turned)]

        sums, late = None, None
        now = dots(parts[0])
        for k in range(4):
            later = dots(parts[k + 1]) if k < 3 else None
            done = work(parts[k], *now)
            if late is not None:
                sums = products(sums, *late)
            now, late = later, done
        sums, turned = products(sums, *late)
        for kind, term in zip((0, 2), turned):
            sums[kind] = [a + b for a, b in zip(sums[kind], windows(term.T))]
        for kind in range(4):
            for w in range(8):
                tf[2 * i + w // 4, w % 4, kind] = sums[kind][w]

        def finish(at_step, *chunks):
            @pl.when(i == at_step)
            def _():
                for name, waits in chunks:
                    for half in (1, 0) if name in ("A-1", "A+1") else (0, 1):
                        c, span = AT[name], pl.ds(2 * half, 2)
                        if waits[half]:
                            got(waits[half])
                        total = tf[c, span] + r1[c, span].astype(jnp.float32)
                        snd[c, span] = total.astype(jnp.bfloat16)
                        go(("rA4m", "rA4p")[half] if name == "A4" else "r%s%d" % (name, half))

        def upstream(name):
            return ["r%s%d" % (name, half) for half in range(2)]

        none = [None, None]
        finish(7, ("A4", none), ("B2n", none))
        finish(6, ("B2f", none), ("B-1f", none))
        finish(5, ("A-3", ["rA4m", None]), ("A+3", [None, "rA4p"]))
        finish(4, ("B-1n", upstream("B2n")), ("B+1f", upstream("B2f")))
        finish(3, ("A-2", upstream("A-3")), ("A+2", upstream("A+3")))
        finish(2, ("B+1n", none))
        finish(1, ("A-1", upstream("A-2")), ("A+1", upstream("A+2")))

        @pl.when(i == 2)
        def _():
            got("rB-1f0", "rB-1f1", "rB+1f0", "rB+1f1")
            chain(4, 0)
            chain(3, 4)

        @pl.when(i == 1)
        def _():
            chain(-3, 1, 0)
            chain(2, 5, 4)

        return carry

    lax.fori_loop(0, BACK_STEPS, backward, 0)

    def store(ref, rows):
        for h in range(HEADS):
            lanes = slice(h * DIM, (h + 1) * DIM)
            ref[0:BLK, lanes] = rows[h * BLK : (h + 1) * BLK, 0:DIM]
            ref[BLK : 2 * BLK, lanes] = rows[h * BLK : (h + 1) * BLK, DIM : 2 * DIM]

    leave = [
        pltpu.make_async_copy(src, dst, lsem.at[11 + n])
        for n, (src, dst) in enumerate(
            ((att_ref, att_out), (dq_ref, dq_out), (dk_ref, dk_out), (dv_ref, dv_out))
        )
    ]

    def attend():
        got("ot0", "ot1", "ot2")
        halves = []
        for lh in range(2):
            rows = slice(lh * DIM, (lh + 1) * DIM)
            total = ot[0, rows] * lse[16 + lh : 17 + lh]
            for n in range(1, 4):
                total = total + pot[n - 1, rows].astype(jnp.float32) * lse[16 + 2 * n + lh : 17 + 2 * n + lh]
            halves.append(total)
        store(att_ref, jnp.concatenate(halves, axis=0).T.astype(jnp.bfloat16))

    for lh in range(2):
        sd[lh] = dqt[3, lh * DIM : (lh + 1) * DIM].astype(jnp.bfloat16)
        go("dq3%d" % lh)
    got("rB-1n0", "rB-1n1", "rB+1n0", "rB+1n1")
    chain(-2, 2, 1)
    chain(1, 6, 5)
    attend()
    leave[0].start()
    for lh in range(2):
        got("dq3%d" % lh)
        part = dqt[2, lh * DIM : (lh + 1) * DIM] + pd[lh].astype(jnp.float32)
        xd[lh] = part.astype(jnp.bfloat16)
        go("dq2%d" % lh)

    def queries_back(n, carry):
        def stage(at_step):
            return pl.when(n == at_step)

        @stage(0)
        def _():
            got("rA-11", "rA+11")
            a_send(3, 0)
            a_send(2, 2)

        @stage(2)
        def _():
            for lh in range(2):
                sd[2 + lh] = dqt[1, lh * DIM : (lh + 1) * DIM].astype(jnp.bfloat16)
            go("dq1")
            chain(-1, 3, 2)
            got("rA-10", "rA+10")
            a_send(1, 1, 0)

        p = 1 - n // 2
        lows, cats, d1, d2 = [], [], [], []
        for k in range(2):
            i = 2 * (n % 2) + k
            kl, kh = take(4 * i, 4, 0), take(4 * i, 4, 1)
            low, same = picks(4 * i, 4, p)
            lows.append(kl)
            cats.append(cat(kl, kh, low))
            d1.append(wt[i, p, 0])
            d2.append(wt[i, p, 1])
        one = tn(jnp.concatenate(lows, axis=0), jnp.concatenate(d1, axis=0))
        two = tn(jnp.concatenate(cats, axis=0), jnp.concatenate(d2, axis=0))
        dqt[p, 0:DIM] = dqt[p, 0:DIM] + two[0:DIM]
        dqt[p, high] = dqt[p, high] + (one + two[high])
        return carry

    lax.fori_loop(0, 4, queries_back, 0)

    for half, total in enumerate((a_total(0, 1, 2), b_total(0, 3, 6))):
        total = total + dg[half]
        for lh in range(2):
            rows = slice(lh * BLK + half * HALF, lh * BLK + (half + 1) * HALF)
            dk_ref[rows, :] = (total[lh] * SCALE).astype(jnp.bfloat16)
            dv_ref[rows, :] = total[2 + lh].astype(jnp.bfloat16)

    leave[2].start()
    leave[3].start()
    got("dq1", "dq20", "dq21")
    halves = []
    for lh in range(2):
        part = dqt[0, lh * DIM : (lh + 1) * DIM] + pd[2 + lh].astype(jnp.float32)
        halves.append(part + px[lh].astype(jnp.float32))
    store(dq_ref, (jnp.concatenate(halves, axis=0) * SCALE).T.astype(jnp.bfloat16))
    leave[1].start()
    for name, copy in msgs.items():
        if name not in early:
            copy.wait_send()
    for copy in leave:
        copy.wait()


def hand_out(*refs):
    for source, target in zip(refs[:4], refs[4:]):
        target[...] = source[...]


def body(queries, keys, values, grad_out, block_pos):
    bf, f32 = jnp.bfloat16, jnp.float32
    window = (4, HALF, DIM)
    raw = (2 * BLK, HEADS * DIM)
    count = 108
    shapes = [
        jax.ShapeDtypeStruct(raw, bf),
        jax.ShapeDtypeStruct(raw, bf),
        jax.ShapeDtypeStruct((2 * BLK, DIM), bf),
        jax.ShapeDtypeStruct((2 * BLK, DIM), bf),
    ]
    outs = pl.pallas_call(
        kernel,
        out_shape=shapes,
        in_specs=[pl.BlockSpec(memory_space=pltpu.HBM)] * 5,
        out_specs=[pl.BlockSpec(memory_space=pltpu.HBM)] * 4,
        scratch_shapes=[
            pltpu.VMEM(raw, bf),
            pltpu.VMEM(raw, bf),
            pltpu.VMEM((2 * BLK, DIM), bf),
            pltpu.VMEM((2 * BLK, DIM), bf),
            pltpu.VMEM((CHUNKS, 4) + window, bf),
            pltpu.VMEM(raw, bf),
            pltpu.VMEM(raw, bf),
            pltpu.VMEM((3,) + raw, bf),
            pltpu.VMEM((3,) + raw, bf),
            pltpu.VMEM((4, ROWS, 2 * DIM), bf),
            pltpu.VMEM((4, ROWS, 2 * DIM), bf),
            pltpu.VMEM((4, 2 * DIM, ROWS), bf),
            pltpu.VMEM((4, 2 * DIM, ROWS), bf),
            pltpu.VMEM((4, 2 * DIM, ROWS), f32),
            pltpu.VMEM((4, 2 * DIM, ROWS), f32),
            pltpu.VMEM((24, ROWS), f32),
            pltpu.VMEM((8, 8, ROWS), f32),
            pltpu.VMEM((3, 24, ROWS), f32),
            pltpu.VMEM((24, ROWS), f32),
            pltpu.VMEM((STEPS, 8, ROWS), f32),
            pltpu.VMEM((STEPS, 4, 2, KEYS, ROWS), bf),
            pltpu.VMEM((3, 2 * DIM, ROWS), bf),
            pltpu.VMEM((3, 2 * DIM, ROWS), bf),
            pltpu.VMEM((4, DIM, ROWS), bf),
            pltpu.VMEM((4, DIM, ROWS), bf),
            pltpu.VMEM((2, DIM, ROWS), bf),
            pltpu.VMEM((2, DIM, ROWS), bf),
            pltpu.VMEM((CHUNKS, 4) + window, f32),
            pltpu.VMEM((CHUNKS, 4) + window, bf),
            pltpu.VMEM((CHUNKS, 4) + window, bf),
            pltpu.VMEM((3, 4) + window, bf),
            pltpu.VMEM((3,) + window, bf),
            pltpu.VMEM((3,) + window, bf),
            pltpu.VMEM((7,) + window, bf),
            pltpu.VMEM((7,) + window, bf),
            pltpu.VMEM((2,) + window, f32),
            pltpu.SMEM((4, 2 * BLK), jnp.int32),
            pltpu.SMEM((4 * CHUNKS + 4,), jnp.int32),
            pltpu.SemaphoreType.DMA((15,)),
            pltpu.SemaphoreType.DMA((count,)),
            pltpu.SemaphoreType.DMA((count,)),
        ],
        compiler_params=pltpu.CompilerParams(
            collective_id=0, has_side_effects=True, vmem_limit_bytes=54 * 1024 * 1024
        ),
        name="attention",
    )(block_pos, queries[0], keys[0], values[0], grad_out[0])
    outs = pl.pallas_call(
        hand_out,
        out_shape=shapes,
        in_specs=[pl.BlockSpec(one.shape, lambda n: (0, 0)) for one in shapes],
        out_specs=[pl.BlockSpec(one.shape, lambda n: (0, 0)) for one in shapes],
        grid=(1,),
        compiler_params=pltpu.CompilerParams(vmem_limit_bytes=54 * 1024 * 1024),
        name="hand_out",
    )(*outs)
    return tuple(out[None] for out in outs)


def solution(mesh):
    spec = P("inner", "outer", None)
    return jax.shard_map(
        body,
        mesh=mesh,
        in_specs=(spec, spec, spec, spec, P()),
        out_specs=(spec, spec, spec, spec),
        check_vma=False,
    )
```

```python
import jax
import jax.numpy as jnp
from jax import lax
from jax.experimental import pallas as pl
from jax.experimental.pallas import tpu as pltpu
from jax.sharding import PartitionSpec as P

MESH = pl.DeviceIdType.MESH
NEG = -1e30
BIG = 1e30
BLK = 64
HALF = 32
DIM = 128
HEADS = 8
ROWS = BLK * HEADS
CHUNKS = 16
STEPS = 4
BACK_STEPS = 8
KEYS = 16 * HALF
BACK_KEYS = 8 * HALF
SCALE = DIM**-0.5
C2 = SCALE * 1.4426950408889634

YORDER = (0, -1, 1, 2)
NEAR = (0, -1, 1, -2)
FAR = (2, -3, 3, 4)


def a_chunk(dz):
    return [(dy, dz) for dy in YORDER]


def b_chunk(dy, part):
    return [(dy, dz) for dz in part]


NAMES = (
    ("A0", a_chunk(0)),
    ("B0n", b_chunk(0, NEAR)),
    ("A-1", a_chunk(-1)),
    ("A+1", a_chunk(1)),
    ("B+1n", b_chunk(1, NEAR)),
    ("B0f", b_chunk(0, FAR)),
    ("A-2", a_chunk(-2)),
    ("A+2", a_chunk(2)),
    ("B-1n", b_chunk(-1, NEAR)),
    ("B+1f", b_chunk(1, FAR)),
    ("A-3", a_chunk(-3)),
    ("A+3", a_chunk(3)),
    ("B2f", b_chunk(2, FAR)),
    ("B-1f", b_chunk(-1, FAR)),
    ("B2n", b_chunk(2, NEAR)),
    ("A4", a_chunk(4)),
)
TABLE = [windows for _, windows in NAMES]
AT = {name: number for number, (name, _) in enumerate(NAMES)}


def nt(a, b):
    return lax.dot_general(a, b, (((1,), (0,)), ((), ())), preferred_element_type=jnp.float32)


def tn(a, b):
    return lax.dot_general(a, b, (((0,), (0,)), ((), ())), preferred_element_type=jnp.float32)


def fold(x, op):
    rows, lanes = x.shape
    return op(x.reshape(rows // 8, 8, lanes), axis=0)


def row_sum(x):
    return jnp.sum(x, axis=0, keepdims=True)


def row_max(x):
    return jnp.max(x, axis=0, keepdims=True)


def kernel(
    pos_ref,
    q_ref,
    k_ref,
    v_ref,
    g_ref,
    att_out,
    dq_out,
    dk_out,
    dv_out,
    att_ref,
    dq_ref,
    dk_ref,
    dv_ref,
    buf,
    mq,
    mg,
    pq,
    pg,
    qn,
    gn,
    qt,
    gt,
    ot,
    dqt,
    stat,
    ls,
    pstat,
    lse,
    mc,
    wt,
    mot,
    pot,
    sd,
    pd,
    xd,
    px,
    tf,
    snd,
    r1,
    r2,
    sy,
    ry,
    sz,
    rz,
    dg,
    pos,
    kt,
    lsem,
    ssem,
    rsem,
):
    outer = lax.axis_index("outer")
    inner = lax.axis_index("inner")
    yy = outer // 16
    xx = (outer // 8) % 2
    zz = outer % 8
    mate = inner + 1 - 2 * (inner % 2)

    def at(x, dy, dz):
        return (((yy + dy + 4) % 4) * 2 + x) * 8 + (zz + dz + 8) % 8

    beside = at(1 - xx, 0, 0)
    yp, ym = (at(xx, 1, 0), inner), (at(xx, -1, 0), inner)
    zp, zm = (at(xx, 0, 1), inner), (at(xx, 0, -1), inner)
    cp, xp, dp = (outer, mate), (beside, inner), (beside, mate)
    yp2, zp2, zm2 = (at(xx, 2, 0), inner), (at(xx, 0, 2), inner), (at(xx, 0, -2), inner)

    barrier = pltpu.get_barrier_semaphore()
    for dev in (yp, ym, zp, zm, cp, xp, dp, yp2, zp2, zm2):
        pl.semaphore_signal(barrier, inc=1, device_id=dev, device_id_type=MESH)

    fetch = [
        pltpu.make_async_copy(pos_ref, pos, lsem.at[0]),
        pltpu.make_async_copy(q_ref, mq, lsem.at[1]),
        pltpu.make_async_copy(g_ref, mg, lsem.at[2]),
    ]
    pieces = []
    for n, ref in enumerate((k_ref, v_ref)):
        for lh in range(2):
            for half in range(2):
                pieces.append(
                    pltpu.make_async_copy(
                        ref.at[pl.ds(lh * BLK + half * HALF, HALF)],
                        buf.at[half, 0, 2 * n + lh],
                        lsem.at[3 + len(pieces)],
                    )
                )
    for copy in pieces + fetch:
        copy.start()
    pl.semaphore_wait(barrier, 10)

    msgs = {}

    def msg(name, src, dst, dev):
        at_sem = len(msgs)
        msgs[name] = pltpu.make_async_remote_copy(
            src_ref=src,
            dst_ref=dst,
            send_sem=ssem.at[at_sem],
            recv_sem=rsem.at[at_sem],
            device_id=dev,
            device_id_type=MESH,
        )

    def go(*names):
        for name in names:
            msgs[name].start()

    def got(*names):
        for name in names:
            msgs[name].wait_recv()

    for name, src, dst in (("q", q_ref, pq), ("g", g_ref, pg)):
        msg(name + "1", src, dst.at[0], cp)
        for half in range(2):
            span = pl.ds(half * BLK, BLK)
            msg("%s2%d" % (name, half), src.at[span], dst.at[1, span], xp)
            msg("%s3%d" % (name, half), dst.at[1, span], dst.at[2, span], cp)
    msg("ay1", buf.at[0, 0], buf.at[0, 1], yp)
    msg("ay2", buf.at[0, 0], buf.at[0, 2], ym)
    msg("ay3", buf.at[0, 0], buf.at[0, 3], yp2)
    for w in range(4):
        msg("azp%d" % w, buf.at[0, w], buf.at[AT["A-1"], w], zp)
        msg("azm%d" % w, buf.at[0, w], buf.at[AT["A+1"], w], zm)
        msg("byp%d" % w, buf.at[1, w], buf.at[AT["B-1n"], w], yp)
        msg("bym%d" % w, buf.at[1, w], buf.at[AT["B+1n"], w], ym)

    def block(name, source, target, first, count, dev):
        span = pl.ds(first, count)
        msg(name, buf.at[AT[source], span], buf.at[AT[target], span], dev)

    block("a7a", "A-1", "A-2", 0, 3, zp)
    block("a7b", "A-1", "A-2", 3, 1, zp)
    block("a8a", "A+1", "A+2", 0, 3, zm)
    block("a8b", "A+1", "A+2", 3, 1, zm)
    block("a11a", "A-2", "A-3", 0, 2, zp)
    block("a11b", "A-2", "A-3", 2, 2, zp)
    block("a12a", "A+2", "A+3", 2, 2, zm)
    block("a12b", "A+2", "A+3", 0, 2, zm)
    block("a15p", "A-3", "A4", 0, 2, zp)
    block("a15m", "A+3", "A4", 2, 2, zm)
    far = AT["B0f"]
    msg("bz1", buf.at[1, 0], buf.at[1, 1], zp)
    msg("bz2", buf.at[1, 0], buf.at[1, 2], zm)
    msg("bz3", buf.at[1, 0], buf.at[1, 3], zp2)
    msg("bz4", buf.at[1, 0], buf.at[far, 0], zm2)
    msg("bz5", buf.at[1, 3], buf.at[far, 1], zp)
    msg("bz6", buf.at[far, 0], buf.at[far, 2], zm)
    msg("bz7", buf.at[far, 1], buf.at[far, 3], zp)
    block("b9a", "B0f", "B-1f", 0, 3, yp)
    block("b9b", "B0f", "B-1f", 3, 1, yp)
    block("b10a", "B0f", "B+1f", 0, 3, ym)
    block("b10b", "B0f", "B+1f", 3, 1, ym)
    block("b13", "B-1n", "B2n", 0, 4, yp)
    block("b14a", "B+1f", "B2f", 0, 3, ym)
    block("b14b", "B+1f", "B2f", 3, 1, ym)
    for n, dev in enumerate((cp, xp, dp)):
        msg("stat%d" % n, stat, pstat.at[n], dev)
    for n, dev in enumerate((cp, xp, dp)):
        msg("ot%d" % n, mot.at[n], pot.at[n], dev)
    for lh in range(2):
        msg("dq3%d" % lh, sd.at[lh], pd.at[lh], cp)
        msg("dq2%d" % lh, xd.at[lh], px.at[lh], xp)
    msg("dq1", sd.at[pl.ds(2, 2)], pd.at[pl.ds(2, 2)], cp)
    def back(name, source, target, first, count, dev, into=None):
        span = pl.ds(first, count)
        into = r1.at[AT[target], span] if into is None else r2.at[into, span]
        msg(name, snd.at[AT[source], span], into, dev)

    back("rA4m", "A4", "A-3", 0, 2, zm)
    back("rA4p", "A4", "A+3", 2, 2, zp)
    for half in range(2):
        span = 2 * half, 2

        def both(source, target, dev, into=None):
            back("r%s%d" % (source, half), source, target, *span, dev, into)

        both("A-3", "A-2", zm)
        both("A+3", "A+2", zp)
        both("A-2", "A-1", zm)
        both("A+2", "A+1", zp)
        both("A-1", "A0", zm)
        both("A+1", "A0", zp, 0)
        both("B2n", "B-1n", ym)
        both("B2f", "B+1f", yp)
        both("B-1n", "B0n", ym)
        both("B-1f", "B0f", ym)
        both("B+1n", "B0n", yp, 1)
        both("B+1f", "B0f", yp, 2)
    for n, dev in enumerate((ym, ym, yp)):
        msg("ry%d" % n, sy.at[n], ry.at[n], dev)
    for n, dev in enumerate((zm, zm, zm, zm, zp, zp, zp)):
        msg("rz%d" % n, sz.at[n], rz.at[n], dev)

    go("q20", "q21", "q1")
    for copy in pieces:
        copy.wait()
    go("ay1", "ay2", "ay3", "bz1", "bz2", "bz3", "bz4", "azp0", "azm0", "byp0", "bym0", "g1")
    fetch[0].wait()

    for p, (row, column) in enumerate(
        ((inner, outer), (mate, outer), (inner, beside), (mate, beside))
    ):
        kt[4 * CHUNKS + p] = pos[row, 2 * column]
    for c in range(CHUNKS):
        for w in range(4):
            dy, dz = TABLE[c][w]
            kt[4 * c + w] = pos[inner, 2 * at(xx, dy, dz)]

    def spread(p, src, rows, cols):
        for h in range(HEADS):
            lanes = slice(h * DIM, (h + 1) * DIM)
            rows[p, h * BLK : (h + 1) * BLK, 0:DIM] = src[0:BLK, lanes]
            rows[p, h * BLK : (h + 1) * BLK, DIM : 2 * DIM] = src[BLK : 2 * BLK, lanes]
        cols[p] = rows[p].T

    fetch[1].wait()
    spread(0, mq, qn, qt)
    got("ay1", "ay2", "ay3", "bz1", "bz2", "bz3", "bz4")
    for w in range(1, 4):
        go("azp%d" % w, "azm%d" % w)
    go("bz5", "bz6")
    for w in range(1, 4):
        go("byp%d" % w, "bym%d" % w)
    got("q1")
    spread(1, pq.at[0], qn, qt)

    tok_k = lax.broadcasted_iota(jnp.int32, (BLK, ROWS), 0)
    tok_q = lax.broadcasted_iota(jnp.int32, (BLK, ROWS), 1) % BLK
    diag = tok_k <= tok_q

    def own(kind):
        return jnp.concatenate([buf[0, 0, kind], buf[1, 0, kind]], axis=0)

    for lh in range(2):
        s = jnp.where(diag, nt(own(lh), qt[0, lh * DIM : (lh + 1) * DIM]), NEG)
        m = row_max(s)
        p = jnp.exp2((s - m) * C2)
        stat[lh : lh + 1] = m
        ls[lh] = fold(p, jnp.sum)
        ot[0, lh * DIM : (lh + 1) * DIM] = tn(own(2 + lh), p.astype(jnp.bfloat16))
    stat[2:8] = jnp.full((6, ROWS), NEG, jnp.float32)
    ls[2:8] = jnp.zeros((6, 8, ROWS), jnp.float32)

    for w in range(3):
        got("azp%d" % w, "azm%d" % w)
    go("a7a", "a8a")
    got("azp3", "azm3")
    go("a7b", "a8b")
    got("bz5", "bz6")
    go("bz7", "b9a", "b10a")
    for p in range(1, 4):
        ot[p] = jnp.zeros((2 * DIM, ROWS), jnp.float32)
    for name in ("B+1n", "B2n", "B-1f", "B2f", "A4"):
        r1[AT[name]] = jnp.zeros((4, 4, HALF, DIM), jnp.bfloat16)
    r1[AT["A-3"], 2:4] = jnp.zeros((2, 4, HALF, DIM), jnp.bfloat16)
    r1[AT["A+3"], 0:2] = jnp.zeros((2, 4, HALF, DIM), jnp.bfloat16)

    got("byp0", "byp1", "byp2", "byp3")
    go("b13")
    got("q20")
    go("q30")
    fetch[2].wait()
    spread(0, mg, gn, gt)
    def take(first, count, kind):
        return buf[pl.ds(first, count), :, kind].reshape(count * 4 * HALF, DIM)

    def picks(first, count, p):
        number = [kt[4 * first + w] for w in range(4 * count)]
        mine = kt[4 * CHUNKS + p]
        return [n < mine for n in number], [n == mine for n in number]

    def windows(x):
        return [x[w * HALF : (w + 1) * HALF] for w in range(x.shape[0] // HALF)]

    def cat(low, high, chosen):
        zero = jnp.zeros((HALF, DIM), jnp.bfloat16)
        rows = []
        for a, b, pick in zip(windows(low), windows(high), chosen):
            rows.append(
                jnp.concatenate([lax.select(pick, a, zero), lax.select(pick, zero, b)], axis=1)
            )
        return jnp.concatenate(rows, axis=0)

    neg_rows = jnp.full((8, ROWS), NEG, jnp.float32)
    big_row = jnp.full((1, ROWS), BIG, jnp.float32)
    high = slice(DIM, 2 * DIM)

    def row(ref, r):
        return ref[pl.ds(r, 1)]

    def arrive(n):
        def do(at_step, *steps):
            @pl.when(n == at_step)
            def _():
                for step, names in steps:
                    step(*names)

        @pl.when(n == 1)
        def _():
            got("a7a", "a8a", "a7b", "a8b")
            go("a11a", "a12a", "a11b", "a12b")
            got("bz7")
            go("b9b", "b10b")
            got("q21")
            go("q31", "g20", "g21")
            spread(2, pq.at[1], qn, qt)
            got("q30", "q31")
            spread(3, pq.at[2], qn, qt)

        do(2, (got, ["bym%d" % w for w in range(4)] + ["b10a"]), (go, ["b14a"]))
        do(3, (got, ["b10b"]), (go, ["b14b"]), (got, ["a11a", "a12a"]), (go, ["a15p", "a15m"]))
        do(4, (got, ["a11b", "a12b", "g20", "g21"]), (go, ["g30", "g31"]))
        do(6, (got, ["b14a", "b14b", "b9a", "b9b", "b13", "a15p", "a15m"]))

        @pl.when(n == 5)
        def _():
            got("g1", "g30", "g31")
            for p in range(1, 4):
                spread(p, pg.at[p - 1], gn, gt)

    def forward(n, carry):
        i, pair = n // 2, n % 2
        arrive(n)
        kl, kh, vl, vh = [take(4 * i, 4, kind) for kind in range(4)]
        parts = []
        for p in (2 * pair, 2 * pair + 1):
            low, same = picks(4 * i, 4, p)
            kcat, vcat = cat(kl, kh, low), cat(vl, vh, low)
            olds = [row(stat, 2 * p + lh) for lh in range(2)]
            parts.append((p, low, same, kcat, vcat, olds))

        def scores(part):
            p, _, _, kcat, _, _ = part
            return nt(kl, qt[p, high]), windows(nt(kcat, qt[p]))

        def weigh(part, s1, s2):
            p, low, same, _, vcat, (ml, mh) = part
            rl, rh = 2 * p, 2 * p + 1
            tops_l, tops_h = neg_rows, fold(s1, jnp.max)
            for w in range(16):
                top = fold(s2[w], jnp.max)
                tops_l = jnp.maximum(tops_l, lax.select(low[w], top, neg_rows))
                tops_h = jnp.maximum(tops_h, lax.select(low[w] | same[w], neg_rows, top))
            nl, nh = jnp.maximum(ml, row_max(tops_l)), jnp.maximum(mh, row_max(tops_h))
            fl, fh = jnp.exp2((ml - nl) * C2), jnp.exp2((mh - nh) * C2)
            p1 = jnp.exp2((s1 - nh) * C2)
            tl, th = ls[rl] * fl, ls[rh] * fh + fold(p1, jnp.sum)
            pieces = []
            for w in range(16):
                ref = lax.select(same[w], big_row, lax.select(low[w], nl, nh))
                piece = jnp.exp2((s2[w] - ref) * C2)
                total = fold(piece, jnp.sum)
                zero = jnp.zeros_like(total)
                tl = tl + lax.select(low[w], total, zero)
                th = th + lax.select(low[w], zero, total)
                pieces.append(piece.astype(jnp.bfloat16))
            ls[rl], ls[rh] = tl, th
            stat[pl.ds(rl, 1)], stat[pl.ds(rh, 1)] = nl, nh
            mc[i, pl.ds(rl, 1)], mc[i, pl.ds(rh, 1)] = nl, nh
            w1, w2 = p1.astype(jnp.bfloat16), jnp.concatenate(pieces, axis=0)
            wt[i, p, 0], wt[i, p, 1] = w1, w2
            return p, fl, fh, w1, w2, vcat

        def update(p, fl, fh, w1, w2, vcat):
            o1, o2 = tn(vl, w1), tn(vcat, w2)
            ot[p, 0:DIM] = ot[p, 0:DIM] * fl + o2[0:DIM]
            ot[p, high] = ot[p, high] * fh + (o1 + o2[high])

        now, late = scores(parts[0]), None
        for k in range(2):
            later = scores(parts[k + 1]) if k < 1 else None
            done = weigh(parts[k], *now)
            if late is not None:
                update(*late)
            now, late = later, done
        update(*late)
        return carry

    lax.fori_loop(0, 2 * STEPS, forward, 0)

    for p in range(4):
        for lh in range(2):
            r = 2 * p + lh
            stat[8 + r : 9 + r] = row_sum(ls[r])
            rows = slice(lh * DIM, (lh + 1) * DIM)
            stat[16 + r : 17 + r] = row_sum(ot[p, rows] * gt[p, rows].astype(jnp.float32))
    go("stat2", "stat1", "stat0")
    for n in range(3):
        mot[n] = ot[n + 1].astype(jnp.bfloat16)
    go("ot0", "ot1", "ot2")

    dqt[1:4] = jnp.zeros((3, 2 * DIM, ROWS), jnp.float32)
    early = [name for name in msgs if name[0] in "qgab"]
    for name in early:
        msgs[name].wait_send()
    got("stat0", "stat1", "stat2")
    for p in range(4):
        for lh in range(2):
            r = 2 * p + lh
            held = [(stat, r)] + [(pstat.at[n - 1], 2 * (p ^ n) + lh) for n in range(1, 4)]
            tops = [row(ref, at_row) for ref, at_row in held]
            top = jnp.maximum(jnp.maximum(tops[0], tops[1]), jnp.maximum(tops[2], tops[3]))
            factors = [jnp.exp2((m - top) * C2) for m in tops]
            total, delta = 0.0, 0.0
            for factor, (ref, at_row) in zip(factors, held):
                total = total + factor * row(ref, 8 + at_row)
                delta = delta + factor * row(ref, 16 + at_row)
            lse[r : r + 1] = top + jnp.log(total) * (1.0 / SCALE)
            lse[8 + r : 9 + r] = delta / total
            if p == 0:
                for n in range(4):
                    lse[16 + 2 * n + lh : 17 + 2 * n + lh] = factors[n] / total

    for lh in range(2):
        rows = slice(lh * DIM, (lh + 1) * DIM)
        s = jnp.where(diag, nt(own(lh), qt[0, rows]), NEG)
        p = jnp.exp2((s - lse[lh : lh + 1]) * C2)
        ds = (p * (nt(own(2 + lh), gt[0, rows]) - lse[8 + lh : 9 + lh])).astype(jnp.bfloat16)
        dk = nt(ds, qn[0, :, rows])
        dv = nt(p.astype(jnp.bfloat16), gn[0, :, rows])
        for half in range(2):
            dg[half, lh] = dk[half * HALF : (half + 1) * HALF]
            dg[half, 2 + lh] = dv[half * HALF : (half + 1) * HALF]
        dqt[0, rows] = tn(own(lh), ds)

    def total_of(c, w, slot, ref, *arrived):
        total = tf[c, w] + r1[c, w].astype(jnp.float32) + r2[slot, w].astype(jnp.float32)
        for n in arrived:
            total = total + ref[n].astype(jnp.float32)
        return total

    def b_total(dz, *arrived):
        got(*["rz%d" % n for n in arrived])
        for slot, c in ((1, 1), (2, far)):
            for w in range(4):
                if TABLE[c][w][1] == dz:
                    return total_of(c, w, slot, rz, *arrived)

    def chain(dz, leaving, *arrived):
        sz[leaving] = b_total(dz, *arrived).astype(jnp.bfloat16)
        go("rz%d" % leaving)

    def a_total(w, *arrived):
        got(*["ry%d" % n for n in arrived])
        return total_of(0, w, 0, ry, *arrived)

    def a_send(w, leaving, *arrived):
        sy[leaving] = a_total(w, *arrived).astype(jnp.bfloat16)
        go("ry%d" % leaving)

    def backward(n, carry):
        i = BACK_STEPS - 1 - n
        step, rows = i // 2, pl.ds((i % 2) * BACK_KEYS, BACK_KEYS)
        kl, kh, vl, vh = [take(2 * i, 2, kind) for kind in range(4)]
        parts = []
        for p in range(4):
            low, same = picks(2 * i, 2, p)
            parts.append((p, low, cat(vl, vh, low)))

        def dots(part):
            p, _, vcat = part
            return nt(vl, gt[p, high]), windows(nt(vcat, gt[p]))

        def work(part, g1, g2):
            p, low, _ = part
            rl, rh = 2 * p, 2 * p + 1
            el, eh = lse[8 + rl : 9 + rl], lse[8 + rh : 9 + rh]
            fl = jnp.exp2((mc[step, rl : rl + 1] - lse[rl : rl + 1]) * C2)
            fh = jnp.exp2((mc[step, rh : rh + 1] - lse[rh : rh + 1]) * C2)
            p1 = wt[step, p, 0, rows].astype(jnp.float32) * fh
            ds1 = (p1 * (g1 - eh)).astype(jnp.bfloat16)
            w2 = windows(wt[step, p, 1, rows].astype(jnp.float32))
            ps, ds = [], []
            for w in range(8):
                piece = w2[w] * lax.select(low[w], fl, fh)
                ps.append(piece.astype(jnp.bfloat16))
                ds.append((piece * (g2[w] - lax.select(low[w], el, eh))).astype(jnp.bfloat16))
            p2, ds2 = jnp.concatenate(ps, axis=0), jnp.concatenate(ds, axis=0)
            if p < 2:
                wt[step, p, 0, rows], wt[step, p, 1, rows] = ds1, ds2
            if p >= 2:
                one, two = tn(kl, ds1), tn(cat(kl, kh, low), ds2)
                dqt[p, 0:DIM] = dqt[p, 0:DIM] + two[0:DIM]
                dqt[p, high] = dqt[p, high] + (one + two[high])
            return p, low, p1.astype(jnp.bfloat16), ds1, p2, ds2

        def products(sums, p, low, p1, ds1, p2, ds2):
            new = []
            for one, two in (
                (nt(ds1, qn[p, :, high]), nt(ds2, qn[p])),
                (nt(p1, gn[p, :, high]), nt(p2, gn[p])),
            ):
                zero = jnp.zeros((HALF, DIM), jnp.float32)
                lows, highs = [], []
                for w in range(8):
                    here = slice(w * HALF, (w + 1) * HALF)
                    lows.append(one[here] + lax.select(low[w], two[here, 0:DIM], zero))
                    highs.append(lax.select(low[w], zero, two[here, high]))
                new += [lows, highs]
            if sums is None:
                return new
            return [[a + b for a, b in zip(x, y)] for x, y in zip(sums, new)]

        sums, late = None, None
        now = dots(parts[0])
        for k in range(4):
            later = dots(parts[k + 1]) if k < 3 else None
            done = work(parts[k], *now)
            if late is not None:
                sums = products(sums, *late)
            now, late = later, done
        sums = products(sums, *late)
        for kind in range(4):
            for w in range(8):
                tf[2 * i + w // 4, w % 4, kind] = sums[kind][w]

        def finish(at_step, *chunks):
            @pl.when(i == at_step)
            def _():
                for name, waits in chunks:
                    for half in (1, 0) if name in ("A-1", "A+1") else (0, 1):
                        c, span = AT[name], pl.ds(2 * half, 2)
                        if waits[half]:
                            got(waits[half])
                        total = tf[c, span] + r1[c, span].astype(jnp.float32)
                        snd[c, span] = total.astype(jnp.bfloat16)
                        go(("rA4m", "rA4p")[half] if name == "A4" else "r%s%d" % (name, half))

        def upstream(name):
            return ["r%s%d" % (name, half) for half in range(2)]

        none = [None, None]
        finish(7, ("A4", none), ("B2n", none))
        finish(6, ("B2f", none), ("B-1f", none))
        finish(5, ("A-3", ["rA4m", None]), ("A+3", [None, "rA4p"]))
        finish(4, ("B-1n", upstream("B2n")), ("B+1f", upstream("B2f")))
        finish(3, ("A-2", upstream("A-3")), ("A+2", upstream("A+3")))
        finish(2, ("B+1n", none))
        finish(1, ("A-1", upstream("A-2")), ("A+1", upstream("A+2")))

        @pl.when(i == 2)
        def _():
            got("rB-1f0", "rB-1f1", "rB+1f0", "rB+1f1")
            chain(4, 0)
            chain(3, 4)

        @pl.when(i == 1)
        def _():
            chain(-3, 1, 0)
            chain(2, 5, 4)

        return carry

    lax.fori_loop(0, BACK_STEPS, backward, 0)

    def store(ref, rows):
        for h in range(HEADS):
            lanes = slice(h * DIM, (h + 1) * DIM)
            ref[0:BLK, lanes] = rows[h * BLK : (h + 1) * BLK, 0:DIM]
            ref[BLK : 2 * BLK, lanes] = rows[h * BLK : (h + 1) * BLK, DIM : 2 * DIM]

    leave = [
        pltpu.make_async_copy(src, dst, lsem.at[11 + n])
        for n, (src, dst) in enumerate(
            ((att_ref, att_out), (dq_ref, dq_out), (dk_ref, dk_out), (dv_ref, dv_out))
        )
    ]

    def attend():
        got("ot0", "ot1", "ot2")
        halves = []
        for lh in range(2):
            rows = slice(lh * DIM, (lh + 1) * DIM)
            total = ot[0, rows] * lse[16 + lh : 17 + lh]
            for n in range(1, 4):
                total = total + pot[n - 1, rows].astype(jnp.float32) * lse[16 + 2 * n + lh : 17 + 2 * n + lh]
            halves.append(total)
        store(att_ref, jnp.concatenate(halves, axis=0).T.astype(jnp.bfloat16))

    for lh in range(2):
        sd[lh] = dqt[3, lh * DIM : (lh + 1) * DIM].astype(jnp.bfloat16)
        go("dq3%d" % lh)
    got("rB-1n0", "rB-1n1", "rB+1n0", "rB+1n1")
    chain(-2, 2, 1)
    chain(1, 6, 5)
    attend()
    leave[0].start()
    for lh in range(2):
        got("dq3%d" % lh)
        part = dqt[2, lh * DIM : (lh + 1) * DIM] + pd[lh].astype(jnp.float32)
        xd[lh] = part.astype(jnp.bfloat16)
        go("dq2%d" % lh)

    def queries_back(n, carry):
        def stage(at_step):
            return pl.when(n == at_step)

        @stage(0)
        def _():
            got("rA-11", "rA+11")
            a_send(3, 0)
            a_send(2, 2)

        @stage(2)
        def _():
            for lh in range(2):
                sd[2 + lh] = dqt[1, lh * DIM : (lh + 1) * DIM].astype(jnp.bfloat16)
            go("dq1")
            chain(-1, 3, 2)
            got("rA-10", "rA+10")
            a_send(1, 1, 0)

        p = 1 - n // 2
        lows, cats, d1, d2 = [], [], [], []
        for k in range(2):
            i = 2 * (n % 2) + k
            kl, kh = take(4 * i, 4, 0), take(4 * i, 4, 1)
            low, same = picks(4 * i, 4, p)
            lows.append(kl)
            cats.append(cat(kl, kh, low))
            d1.append(wt[i, p, 0])
            d2.append(wt[i, p, 1])
        one = tn(jnp.concatenate(lows, axis=0), jnp.concatenate(d1, axis=0))
        two = tn(jnp.concatenate(cats, axis=0), jnp.concatenate(d2, axis=0))
        dqt[p, 0:DIM] = dqt[p, 0:DIM] + two[0:DIM]
        dqt[p, high] = dqt[p, high] + (one + two[high])
        return carry

    lax.fori_loop(0, 4, queries_back, 0)

    for half, total in enumerate((a_total(0, 1, 2), b_total(0, 3, 6))):
        total = total + dg[half]
        for lh in range(2):
            rows = slice(lh * BLK + half * HALF, lh * BLK + (half + 1) * HALF)
            dk_ref[rows, :] = (total[lh] * SCALE).astype(jnp.bfloat16)
            dv_ref[rows, :] = total[2 + lh].astype(jnp.bfloat16)

    leave[2].start()
    leave[3].start()
    got("dq1", "dq20", "dq21")
    halves = []
    for lh in range(2):
        part = dqt[0, lh * DIM : (lh + 1) * DIM] + pd[2 + lh].astype(jnp.float32)
        halves.append(part + px[lh].astype(jnp.float32))
    store(dq_ref, (jnp.concatenate(halves, axis=0) * SCALE).T.astype(jnp.bfloat16))
    leave[1].start()
    for name, copy in msgs.items():
        if name not in early:
            copy.wait_send()
    for copy in leave:
        copy.wait()


def hand_out(*refs):
    for source, target in zip(refs[:4], refs[4:]):
        target[...] = source[...]


def body(queries, keys, values, grad_out, block_pos):
    bf, f32 = jnp.bfloat16, jnp.float32
    window = (4, HALF, DIM)
    raw = (2 * BLK, HEADS * DIM)
    count = 108
    shapes = [
        jax.ShapeDtypeStruct(raw, bf),
        jax.ShapeDtypeStruct(raw, bf),
        jax.ShapeDtypeStruct((2 * BLK, DIM), bf),
        jax.ShapeDtypeStruct((2 * BLK, DIM), bf),
    ]
    outs = pl.pallas_call(
        kernel,
        out_shape=shapes,
        in_specs=[pl.BlockSpec(memory_space=pltpu.HBM)] * 5,
        out_specs=[pl.BlockSpec(memory_space=pltpu.HBM)] * 4,
        scratch_shapes=[
            pltpu.VMEM(raw, bf),
            pltpu.VMEM(raw, bf),
            pltpu.VMEM((2 * BLK, DIM), bf),
            pltpu.VMEM((2 * BLK, DIM), bf),
            pltpu.VMEM((CHUNKS, 4) + window, bf),
            pltpu.VMEM(raw, bf),
            pltpu.VMEM(raw, bf),
            pltpu.VMEM((3,) + raw, bf),
            pltpu.VMEM((3,) + raw, bf),
            pltpu.VMEM((4, ROWS, 2 * DIM), bf),
            pltpu.VMEM((4, ROWS, 2 * DIM), bf),
            pltpu.VMEM((4, 2 * DIM, ROWS), bf),
            pltpu.VMEM((4, 2 * DIM, ROWS), bf),
            pltpu.VMEM((4, 2 * DIM, ROWS), f32),
            pltpu.VMEM((4, 2 * DIM, ROWS), f32),
            pltpu.VMEM((24, ROWS), f32),
            pltpu.VMEM((8, 8, ROWS), f32),
            pltpu.VMEM((3, 24, ROWS), f32),
            pltpu.VMEM((24, ROWS), f32),
            pltpu.VMEM((STEPS, 8, ROWS), f32),
            pltpu.VMEM((STEPS, 4, 2, KEYS, ROWS), bf),
            pltpu.VMEM((3, 2 * DIM, ROWS), bf),
            pltpu.VMEM((3, 2 * DIM, ROWS), bf),
            pltpu.VMEM((4, DIM, ROWS), bf),
            pltpu.VMEM((4, DIM, ROWS), bf),
            pltpu.VMEM((2, DIM, ROWS), bf),
            pltpu.VMEM((2, DIM, ROWS), bf),
            pltpu.VMEM((CHUNKS, 4) + window, f32),
            pltpu.VMEM((CHUNKS, 4) + window, bf),
            pltpu.VMEM((CHUNKS, 4) + window, bf),
            pltpu.VMEM((3, 4) + window, bf),
            pltpu.VMEM((3,) + window, bf),
            pltpu.VMEM((3,) + window, bf),
            pltpu.VMEM((7,) + window, bf),
            pltpu.VMEM((7,) + window, bf),
            pltpu.VMEM((2,) + window, f32),
            pltpu.SMEM((4, 2 * BLK), jnp.int32),
            pltpu.SMEM((4 * CHUNKS + 4,), jnp.int32),
            pltpu.SemaphoreType.DMA((15,)),
            pltpu.SemaphoreType.DMA((count,)),
            pltpu.SemaphoreType.DMA((count,)),
        ],
        compiler_params=pltpu.CompilerParams(
            collective_id=0, has_side_effects=True, vmem_limit_bytes=54 * 1024 * 1024
        ),
        name="attention",
    )(block_pos, queries[0], keys[0], values[0], grad_out[0])
    outs = pl.pallas_call(
        hand_out,
        out_shape=shapes,
        in_specs=[pl.BlockSpec(one.shape, lambda n: (0, 0)) for one in shapes],
        out_specs=[pl.BlockSpec(one.shape, lambda n: (0, 0)) for one in shapes],
        grid=(1,),
        compiler_params=pltpu.CompilerParams(vmem_limit_bytes=54 * 1024 * 1024),
        name="hand_out",
    )(*outs)
    return tuple(out[None] for out in outs)


def solution(mesh):
    spec = P("inner", "outer", None)
    return jax.shard_map(
        body,
        mesh=mesh,
        in_specs=(spec, spec, spec, spec, P()),
        out_specs=(spec, spec, spec, spec),
        check_vma=False,
    )
```

```python
import jax
import jax.numpy as jnp
from jax import lax
from jax.experimental import pallas as pl
from jax.experimental.pallas import tpu as pltpu
from jax.sharding import PartitionSpec as P

MESH = pl.DeviceIdType.MESH
NEG = -1e30
BIG = 1e30
BLK = 64
HALF = 32
DIM = 128
HEADS = 8
ROWS = BLK * HEADS
CHUNKS = 16
STEPS = 4
BACK_STEPS = 8
KEYS = 16 * HALF
BACK_KEYS = 8 * HALF
SCALE = DIM**-0.5
C2 = SCALE * 1.4426950408889634

YORDER = (0, -1, 1, 2)
NEAR = (0, -1, 1, -2)
FAR = (2, -3, 3, 4)


def a_chunk(dz):
    return [(dy, dz) for dy in YORDER]


def b_chunk(dy, part):
    return [(dy, dz) for dz in part]


NAMES = (
    ("A0", a_chunk(0)),
    ("B0n", b_chunk(0, NEAR)),
    ("A-1", a_chunk(-1)),
    ("A+1", a_chunk(1)),
    ("B+1n", b_chunk(1, NEAR)),
    ("B0f", b_chunk(0, FAR)),
    ("A-2", a_chunk(-2)),
    ("A+2", a_chunk(2)),
    ("B-1n", b_chunk(-1, NEAR)),
    ("B+1f", b_chunk(1, FAR)),
    ("A-3", a_chunk(-3)),
    ("A+3", a_chunk(3)),
    ("B2f", b_chunk(2, FAR)),
    ("B-1f", b_chunk(-1, FAR)),
    ("B2n", b_chunk(2, NEAR)),
    ("A4", a_chunk(4)),
)
TABLE = [windows for _, windows in NAMES]
AT = {name: number for number, (name, _) in enumerate(NAMES)}


def nt(a, b):
    return lax.dot_general(a, b, (((1,), (0,)), ((), ())), preferred_element_type=jnp.float32)


def tn(a, b):
    return lax.dot_general(a, b, (((0,), (0,)), ((), ())), preferred_element_type=jnp.float32)


def fold(x, op):
    rows, lanes = x.shape
    return op(x.reshape(rows // 8, 8, lanes), axis=0)


def row_sum(x):
    return jnp.sum(x, axis=0, keepdims=True)


def row_max(x):
    return jnp.max(x, axis=0, keepdims=True)


def kernel(
    pos_ref,
    q_ref,
    k_ref,
    v_ref,
    g_ref,
    att_out,
    dq_out,
    dk_out,
    dv_out,
    att_ref,
    dq_ref,
    dk_ref,
    dv_ref,
    buf,
    mq,
    mg,
    pq,
    pg,
    qn,
    gn,
    qt,
    gt,
    ot,
    dqt,
    stat,
    ls,
    pstat,
    lse,
    mc,
    wt,
    mot,
    pot,
    sd,
    pd,
    xd,
    px,
    tf,
    snd,
    r1,
    r2,
    sy,
    ry,
    sz,
    rz,
    dg,
    pos,
    kt,
    lsem,
    ssem,
    rsem,
):
    outer = lax.axis_index("outer")
    inner = lax.axis_index("inner")
    yy = outer // 16
    xx = (outer // 8) % 2
    zz = outer % 8
    mate = inner + 1 - 2 * (inner % 2)

    def at(x, dy, dz):
        return (((yy + dy + 4) % 4) * 2 + x) * 8 + (zz + dz + 8) % 8

    beside = at(1 - xx, 0, 0)
    yp, ym = (at(xx, 1, 0), inner), (at(xx, -1, 0), inner)
    zp, zm = (at(xx, 0, 1), inner), (at(xx, 0, -1), inner)
    cp, xp, dp = (outer, mate), (beside, inner), (beside, mate)

    barrier = pltpu.get_barrier_semaphore()
    for dev in (yp, ym, zp, zm, cp, xp, dp):
        pl.semaphore_signal(barrier, inc=1, device_id=dev, device_id_type=MESH)

    fetch = [
        pltpu.make_async_copy(pos_ref, pos, lsem.at[0]),
        pltpu.make_async_copy(q_ref, mq, lsem.at[1]),
        pltpu.make_async_copy(g_ref, mg, lsem.at[2]),
    ]
    pieces = []
    for n, ref in enumerate((k_ref, v_ref)):
        for lh in range(2):
            for half in range(2):
                pieces.append(
                    pltpu.make_async_copy(
                        ref.at[pl.ds(lh * BLK + half * HALF, HALF)],
                        buf.at[half, 0, 2 * n + lh],
                        lsem.at[3 + len(pieces)],
                    )
                )
    for copy in pieces + fetch:
        copy.start()
    pl.semaphore_wait(barrier, 7)

    msgs = {}

    def msg(name, src, dst, dev):
        at_sem = len(msgs)
        msgs[name] = pltpu.make_async_remote_copy(
            src_ref=src,
            dst_ref=dst,
            send_sem=ssem.at[at_sem],
            recv_sem=rsem.at[at_sem],
            device_id=dev,
            device_id_type=MESH,
        )

    def go(*names):
        for name in names:
            msgs[name].start()

    def got(*names):
        for name in names:
            msgs[name].wait_recv()

    for name, src, dst in (("q", q_ref, pq), ("g", g_ref, pg)):
        msg(name + "1", src, dst.at[0], cp)
        for half in range(2):
            span = pl.ds(half * BLK, BLK)
            msg("%s2%d" % (name, half), src.at[span], dst.at[1, span], xp)
            msg("%s3%d" % (name, half), dst.at[1, span], dst.at[2, span], cp)
    msg("ay1", buf.at[0, 0], buf.at[0, 1], yp)
    msg("ay2", buf.at[0, 0], buf.at[0, 2], ym)
    msg("ay3", buf.at[0, 1], buf.at[0, 3], yp)
    for w in range(4):
        msg("azp%d" % w, buf.at[0, w], buf.at[AT["A-1"], w], zp)
        msg("azm%d" % w, buf.at[0, w], buf.at[AT["A+1"], w], zm)
        msg("byp%d" % w, buf.at[1, w], buf.at[AT["B-1n"], w], yp)
        msg("bym%d" % w, buf.at[1, w], buf.at[AT["B+1n"], w], ym)

    def block(name, source, target, first, count, dev):
        span = pl.ds(first, count)
        msg(name, buf.at[AT[source], span], buf.at[AT[target], span], dev)

    block("a7a", "A-1", "A-2", 0, 3, zp)
    block("a7b", "A-1", "A-2", 3, 1, zp)
    block("a8a", "A+1", "A+2", 0, 3, zm)
    block("a8b", "A+1", "A+2", 3, 1, zm)
    block("a11a", "A-2", "A-3", 0, 2, zp)
    block("a11b", "A-2", "A-3", 2, 2, zp)
    block("a12a", "A+2", "A+3", 2, 2, zm)
    block("a12b", "A+2", "A+3", 0, 2, zm)
    block("a15p", "A-3", "A4", 0, 2, zp)
    block("a15m", "A+3", "A4", 2, 2, zm)
    far = AT["B0f"]
    msg("bz1", buf.at[1, 0], buf.at[1, 1], zp)
    msg("bz2", buf.at[1, 0], buf.at[1, 2], zm)
    msg("bz3", buf.at[1, 1], buf.at[1, 3], zp)
    msg("bz4", buf.at[1, 2], buf.at[far, 0], zm)
    msg("bz5", buf.at[1, 3], buf.at[far, 1], zp)
    msg("bz6", buf.at[far, 0], buf.at[far, 2], zm)
    msg("bz7", buf.at[far, 1], buf.at[far, 3], zp)
    block("b9a", "B0f", "B-1f", 0, 3, yp)
    block("b9b", "B0f", "B-1f", 3, 1, yp)
    block("b10a", "B0f", "B+1f", 0, 3, ym)
    block("b10b", "B0f", "B+1f", 3, 1, ym)
    block("b13", "B-1n", "B2n", 0, 4, yp)
    block("b14a", "B+1f", "B2f", 0, 3, ym)
    block("b14b", "B+1f", "B2f", 3, 1, ym)
    for n, dev in enumerate((cp, xp, dp)):
        msg("stat%d" % n, stat, pstat.at[n], dev)
    for n, dev in enumerate((cp, xp, dp)):
        msg("ot%d" % n, mot.at[n], pot.at[n], dev)
    for lh in range(2):
        msg("dq3%d" % lh, sd.at[lh], pd.at[lh], cp)
        msg("dq2%d" % lh, xd.at[lh], px.at[lh], xp)
    msg("dq1", sd.at[pl.ds(2, 2)], pd.at[pl.ds(2, 2)], cp)
    def back(name, source, target, first, count, dev, into=None):
        span = pl.ds(first, count)
        into = r1.at[AT[target], span] if into is None else r2.at[into, span]
        msg(name, snd.at[AT[source], span], into, dev)

    back("rA4m", "A4", "A-3", 0, 2, zm)
    back("rA4p", "A4", "A+3", 2, 2, zp)
    for half in range(2):
        span = 2 * half, 2

        def both(source, target, dev, into=None):
            back("r%s%d" % (source, half), source, target, *span, dev, into)

        both("A-3", "A-2", zm)
        both("A+3", "A+2", zp)
        both("A-2", "A-1", zm)
        both("A+2", "A+1", zp)
        both("A-1", "A0", zm)
        both("A+1", "A0", zp, 0)
        both("B2n", "B-1n", ym)
        both("B2f", "B+1f", yp)
        both("B-1n", "B0n", ym)
        both("B-1f", "B0f", ym)
        both("B+1n", "B0n", yp, 1)
        both("B+1f", "B0f", yp, 2)
    for n, dev in enumerate((ym, ym, yp)):
        msg("ry%d" % n, sy.at[n], ry.at[n], dev)
    for n, dev in enumerate((zm, zm, zm, zm, zp, zp, zp)):
        msg("rz%d" % n, sz.at[n], rz.at[n], dev)

    go("q20", "q21", "q1")
    for copy in pieces:
        copy.wait()
    go("ay1", "ay2", "bz1", "bz2", "azp0", "azm0", "byp0", "bym0", "g1")
    fetch[0].wait()

    for p, (row, column) in enumerate(
        ((inner, outer), (mate, outer), (inner, beside), (mate, beside))
    ):
        kt[4 * CHUNKS + p] = pos[row, 2 * column]
    for c in range(CHUNKS):
        for w in range(4):
            dy, dz = TABLE[c][w]
            kt[4 * c + w] = pos[inner, 2 * at(xx, dy, dz)]

    def spread(p, src, rows, cols):
        for h in range(HEADS):
            lanes = slice(h * DIM, (h + 1) * DIM)
            rows[p, h * BLK : (h + 1) * BLK, 0:DIM] = src[0:BLK, lanes]
            rows[p, h * BLK : (h + 1) * BLK, DIM : 2 * DIM] = src[BLK : 2 * BLK, lanes]
        cols[p] = rows[p].T

    fetch[1].wait()
    spread(0, mq, qn, qt)
    got("ay1", "ay2", "bz1", "bz2")
    go("ay3", "bz3", "bz4", "azp1", "azm1", "azp2", "azm2", "byp1", "bym1", "byp2", "bym2")
    got("q1")
    spread(1, pq.at[0], qn, qt)

    tok_k = lax.broadcasted_iota(jnp.int32, (BLK, ROWS), 0)
    tok_q = lax.broadcasted_iota(jnp.int32, (BLK, ROWS), 1) % BLK
    diag = tok_k <= tok_q

    def own(kind):
        return jnp.concatenate([buf[0, 0, kind], buf[1, 0, kind]], axis=0)

    for lh in range(2):
        s = jnp.where(diag, nt(own(lh), qt[0, lh * DIM : (lh + 1) * DIM]), NEG)
        m = row_max(s)
        p = jnp.exp2((s - m) * C2)
        stat[lh : lh + 1] = m
        ls[lh] = fold(p, jnp.sum)
        ot[0, lh * DIM : (lh + 1) * DIM] = tn(own(2 + lh), p.astype(jnp.bfloat16))
    stat[2:8] = jnp.full((6, ROWS), NEG, jnp.float32)
    ls[2:8] = jnp.zeros((6, 8, ROWS), jnp.float32)

    got("ay3", "bz3", "bz4")
    go("azp3", "azm3", "bz5", "bz6", "byp3", "bym3")
    for w in range(3):
        got("azp%d" % w, "azm%d" % w)
    go("a7a", "a8a")
    for p in range(1, 4):
        ot[p] = jnp.zeros((2 * DIM, ROWS), jnp.float32)
    for name in ("B+1n", "B2n", "B-1f", "B2f", "A4"):
        r1[AT[name]] = jnp.zeros((4, 4, HALF, DIM), jnp.bfloat16)
    r1[AT["A-3"], 2:4] = jnp.zeros((2, 4, HALF, DIM), jnp.bfloat16)
    r1[AT["A+3"], 0:2] = jnp.zeros((2, 4, HALF, DIM), jnp.bfloat16)

    got("azp3", "azm3", "bz5", "bz6")
    go("a7b", "a8b", "bz7", "b9a", "b10a")
    got("byp0", "byp1", "byp2", "byp3")
    go("b13")
    got("q20")
    go("q30")
    fetch[2].wait()
    spread(0, mg, gn, gt)
    def take(first, count, kind):
        return buf[pl.ds(first, count), :, kind].reshape(count * 4 * HALF, DIM)

    def picks(first, count, p):
        number = [kt[4 * first + w] for w in range(4 * count)]
        mine = kt[4 * CHUNKS + p]
        return [n < mine for n in number], [n == mine for n in number]

    def windows(x):
        return [x[w * HALF : (w + 1) * HALF] for w in range(x.shape[0] // HALF)]

    def cat(low, high, chosen):
        zero = jnp.zeros((HALF, DIM), jnp.bfloat16)
        rows = []
        for a, b, pick in zip(windows(low), windows(high), chosen):
            rows.append(
                jnp.concatenate([lax.select(pick, a, zero), lax.select(pick, zero, b)], axis=1)
            )
        return jnp.concatenate(rows, axis=0)

    neg_rows = jnp.full((8, ROWS), NEG, jnp.float32)
    big_row = jnp.full((1, ROWS), BIG, jnp.float32)
    high = slice(DIM, 2 * DIM)

    def row(ref, r):
        return ref[pl.ds(r, 1)]

    def arrive(n):
        def do(at_step, *steps):
            @pl.when(n == at_step)
            def _():
                for step, names in steps:
                    step(*names)

        @pl.when(n == 1)
        def _():
            got("q21")
            go("q31", "g20", "g21")
            spread(2, pq.at[1], qn, qt)
            got("q30", "q31")
            spread(3, pq.at[2], qn, qt)
            got("a7a", "a8a", "bz7")
            go("b9b", "b10b")

        do(2, (got, ["a7b", "a8b"]), (go, ["a11a", "a12a", "a11b", "a12b"]))
        do(2, (got, ["bym%d" % w for w in range(4)] + ["b10a"]), (go, ["b14a"]))
        do(3, (got, ["b10b"]), (go, ["b14b"]))
        do(4, (got, ["a11a", "a12a"]), (go, ["a15p", "a15m"]))
        do(4, (got, ["g20", "g21"]), (go, ["g30", "g31"]), (got, ["a11b", "a12b"]))
        do(6, (got, ["b14a", "b14b", "b9a", "b9b", "b13", "a15p", "a15m"]))

        @pl.when(n == 5)
        def _():
            got("g1", "g30", "g31")
            for p in range(1, 4):
                spread(p, pg.at[p - 1], gn, gt)

    def forward(n, carry):
        i, pair = n // 2, n % 2
        arrive(n)
        kl, kh, vl, vh = [take(4 * i, 4, kind) for kind in range(4)]
        parts = []
        for p in (2 * pair, 2 * pair + 1):
            low, same = picks(4 * i, 4, p)
            kcat, vcat = cat(kl, kh, low), cat(vl, vh, low)
            olds = [row(stat, 2 * p + lh) for lh in range(2)]
            parts.append((p, low, same, kcat, vcat, olds))

        def scores(part):
            p, _, _, kcat, _, _ = part
            return nt(kl, qt[p, high]), windows(nt(kcat, qt[p]))

        def weigh(part, s1, s2):
            p, low, same, _, vcat, (ml, mh) = part
            rl, rh = 2 * p, 2 * p + 1
            tops_l, tops_h = neg_rows, fold(s1, jnp.max)
            for w in range(16):
                top = fold(s2[w], jnp.max)
                tops_l = jnp.maximum(tops_l, lax.select(low[w], top, neg_rows))
                tops_h = jnp.maximum(tops_h, lax.select(low[w] | same[w], neg_rows, top))
            nl, nh = jnp.maximum(ml, row_max(tops_l)), jnp.maximum(mh, row_max(tops_h))
            fl, fh = jnp.exp2((ml - nl) * C2), jnp.exp2((mh - nh) * C2)
            p1 = jnp.exp2((s1 - nh) * C2)
            tl, th = ls[rl] * fl, ls[rh] * fh + fold(p1, jnp.sum)
            pieces = []
            for w in range(16):
                ref = lax.select(same[w], big_row, lax.select(low[w], nl, nh))
                piece = jnp.exp2((s2[w] - ref) * C2)
                total = fold(piece, jnp.sum)
                zero = jnp.zeros_like(total)
                tl = tl + lax.select(low[w], total, zero)
                th = th + lax.select(low[w], zero, total)
                pieces.append(piece.astype(jnp.bfloat16))
            ls[rl], ls[rh] = tl, th
            stat[pl.ds(rl, 1)], stat[pl.ds(rh, 1)] = nl, nh
            mc[i, pl.ds(rl, 1)], mc[i, pl.ds(rh, 1)] = nl, nh
            w1, w2 = p1.astype(jnp.bfloat16), jnp.concatenate(pieces, axis=0)
            wt[i, p, 0], wt[i, p, 1] = w1, w2
            return p, fl, fh, w1, w2, vcat

        def update(p, fl, fh, w1, w2, vcat):
            o1, o2 = tn(vl, w1), tn(vcat, w2)
            ot[p, 0:DIM] = ot[p, 0:DIM] * fl + o2[0:DIM]
            ot[p, high] = ot[p, high] * fh + (o1 + o2[high])

        now, late = scores(parts[0]), None
        for k in range(2):
            later = scores(parts[k + 1]) if k < 1 else None
            done = weigh(parts[k], *now)
            if late is not None:
                update(*late)
            now, late = later, done
        update(*late)
        return carry

    lax.fori_loop(0, 2 * STEPS, forward, 0)

    for p in range(4):
        for lh in range(2):
            r = 2 * p + lh
            stat[8 + r : 9 + r] = row_sum(ls[r])
            rows = slice(lh * DIM, (lh + 1) * DIM)
            stat[16 + r : 17 + r] = row_sum(ot[p, rows] * gt[p, rows].astype(jnp.float32))
    go("stat2", "stat1", "stat0")
    for n in range(3):
        mot[n] = ot[n + 1].astype(jnp.bfloat16)
    go("ot0", "ot1", "ot2")

    dqt[1:4] = jnp.zeros((3, 2 * DIM, ROWS), jnp.float32)
    early = [name for name in msgs if name[0] in "qgab"]
    for name in early:
        msgs[name].wait_send()
    got("stat0", "stat1", "stat2")
    for p in range(4):
        for lh in range(2):
            r = 2 * p + lh
            held = [(stat, r)] + [(pstat.at[n - 1], 2 * (p ^ n) + lh) for n in range(1, 4)]
            tops = [row(ref, at_row) for ref, at_row in held]
            top = jnp.maximum(jnp.maximum(tops[0], tops[1]), jnp.maximum(tops[2], tops[3]))
            factors = [jnp.exp2((m - top) * C2) for m in tops]
            total, delta = 0.0, 0.0
            for factor, (ref, at_row) in zip(factors, held):
                total = total + factor * row(ref, 8 + at_row)
                delta = delta + factor * row(ref, 16 + at_row)
            lse[r : r + 1] = top + jnp.log(total) * (1.0 / SCALE)
            lse[8 + r : 9 + r] = delta / total
            if p == 0:
                for n in range(4):
                    lse[16 + 2 * n + lh : 17 + 2 * n + lh] = factors[n] / total

    for lh in range(2):
        rows = slice(lh * DIM, (lh + 1) * DIM)
        s = jnp.where(diag, nt(own(lh), qt[0, rows]), NEG)
        p = jnp.exp2((s - lse[lh : lh + 1]) * C2)
        ds = (p * (nt(own(2 + lh), gt[0, rows]) - lse[8 + lh : 9 + lh])).astype(jnp.bfloat16)
        dk = nt(ds, qn[0, :, rows])
        dv = nt(p.astype(jnp.bfloat16), gn[0, :, rows])
        for half in range(2):
            dg[half, lh] = dk[half * HALF : (half + 1) * HALF]
            dg[half, 2 + lh] = dv[half * HALF : (half + 1) * HALF]
        dqt[0, rows] = tn(own(lh), ds)

    def total_of(c, w, slot, ref, *arrived):
        total = tf[c, w] + r1[c, w].astype(jnp.float32) + r2[slot, w].astype(jnp.float32)
        for n in arrived:
            total = total + ref[n].astype(jnp.float32)
        return total

    def b_total(dz, *arrived):
        got(*["rz%d" % n for n in arrived])
        for slot, c in ((1, 1), (2, far)):
            for w in range(4):
                if TABLE[c][w][1] == dz:
                    return total_of(c, w, slot, rz, *arrived)

    def chain(dz, leaving, *arrived):
        sz[leaving] = b_total(dz, *arrived).astype(jnp.bfloat16)
        go("rz%d" % leaving)

    def a_total(w, *arrived):
        got(*["ry%d" % n for n in arrived])
        return total_of(0, w, 0, ry, *arrived)

    def a_send(w, leaving, *arrived):
        sy[leaving] = a_total(w, *arrived).astype(jnp.bfloat16)
        go("ry%d" % leaving)

    def backward(n, carry):
        i = BACK_STEPS - 1 - n
        step, rows = i // 2, pl.ds((i % 2) * BACK_KEYS, BACK_KEYS)
        kl, kh, vl, vh = [take(2 * i, 2, kind) for kind in range(4)]
        parts = []
        for p in range(4):
            low, same = picks(2 * i, 2, p)
            parts.append((p, low, cat(vl, vh, low)))

        def dots(part):
            p, low, vcat = part
            el, eh = lse[8 + 2 * p : 9 + 2 * p], lse[9 + 2 * p : 10 + 2 * p]
            first = (nt(vl, gt[p, high]) - eh).astype(jnp.bfloat16)
            second = [
                (dot - lax.select(pick, el, eh)).astype(jnp.bfloat16)
                for pick, dot in zip(low, windows(nt(vcat, gt[p])))
            ]
            return first, second

        def work(part, first, second):
            p, low, _ = part
            rl, rh = 2 * p, 2 * p + 1
            fl = jnp.exp2((mc[step, rl : rl + 1] - lse[rl : rl + 1]) * C2)
            fh = jnp.exp2((mc[step, rh : rh + 1] - lse[rh : rh + 1]) * C2)
            p1 = wt[step, p, 0, rows] * fh.astype(jnp.bfloat16)
            ds1 = p1 * first
            ps, ds = [], []
            for weight, dot, pick in zip(windows(wt[step, p, 1, rows]), second, low):
                piece = weight * lax.select(pick, fl, fh).astype(jnp.bfloat16)
                ps.append(piece)
                ds.append(piece * dot)
            p2, ds2 = jnp.concatenate(ps, axis=0), jnp.concatenate(ds, axis=0)
            if p < 2:
                wt[step, p, 0, rows], wt[step, p, 1, rows] = ds1, ds2
            if p >= 2:
                one, two = tn(kl, ds1), tn(cat(kl, kh, low), ds2)
                dqt[p, 0:DIM] = dqt[p, 0:DIM] + two[0:DIM]
                dqt[p, high] = dqt[p, high] + (one + two[high])
            return p, low, p1, ds1, p2, ds2

        def products(sums, p, low, p1, ds1, p2, ds2):
            new = []
            for one, two in (
                (nt(ds1, qn[p, :, high]), nt(ds2, qn[p])),
                (nt(p1, gn[p, :, high]), nt(p2, gn[p])),
            ):
                zero = jnp.zeros((HALF, DIM), jnp.float32)
                lows, highs = [], []
                for w in range(8):
                    here = slice(w * HALF, (w + 1) * HALF)
                    lows.append(one[here] + lax.select(low[w], two[here, 0:DIM], zero))
                    highs.append(lax.select(low[w], zero, two[here, high]))
                new += [lows, highs]
            if sums is None:
                return new
            return [[a + b for a, b in zip(x, y)] for x, y in zip(sums, new)]

        sums, late = None, None
        now = dots(parts[0])
        for k in range(4):
            later = dots(parts[k + 1]) if k < 3 else None
            done = work(parts[k], *now)
            if late is not None:
                sums = products(sums, *late)
            now, late = later, done
        sums = products(sums, *late)
        for kind in range(4):
            for w in range(8):
                tf[2 * i + w // 4, w % 4, kind] = sums[kind][w]

        def finish(at_step, *chunks):
            @pl.when(i == at_step)
            def _():
                for name, waits in chunks:
                    for half in (1, 0) if name in ("A-1", "A+1") else (0, 1):
                        c, span = AT[name], pl.ds(2 * half, 2)
                        if waits[half]:
                            got(waits[half])
                        total = tf[c, span] + r1[c, span].astype(jnp.float32)
                        snd[c, span] = total.astype(jnp.bfloat16)
                        go(("rA4m", "rA4p")[half] if name == "A4" else "r%s%d" % (name, half))

        def upstream(name):
            return ["r%s%d" % (name, half) for half in range(2)]

        none = [None, None]
        finish(7, ("A4", none), ("B2n", none))
        finish(6, ("B2f", none), ("B-1f", none))
        finish(5, ("A-3", ["rA4m", None]), ("A+3", [None, "rA4p"]))
        finish(4, ("B-1n", upstream("B2n")), ("B+1f", upstream("B2f")))
        finish(3, ("A-2", upstream("A-3")), ("A+2", upstream("A+3")))
        finish(2, ("B+1n", none))
        finish(1, ("A-1", upstream("A-2")), ("A+1", upstream("A+2")))

        @pl.when(i == 2)
        def _():
            got("rB-1f0", "rB-1f1", "rB+1f0", "rB+1f1")
            chain(4, 0)
            chain(3, 4)

        @pl.when(i == 1)
        def _():
            chain(-3, 1, 0)
            chain(2, 5, 4)

        return carry

    lax.fori_loop(0, BACK_STEPS, backward, 0)

    def store(ref, rows):
        for h in range(HEADS):
            lanes = slice(h * DIM, (h + 1) * DIM)
            ref[0:BLK, lanes] = rows[h * BLK : (h + 1) * BLK, 0:DIM]
            ref[BLK : 2 * BLK, lanes] = rows[h * BLK : (h + 1) * BLK, DIM : 2 * DIM]

    leave = [
        pltpu.make_async_copy(src, dst, lsem.at[11 + n])
        for n, (src, dst) in enumerate(
            ((att_ref, att_out), (dq_ref, dq_out), (dk_ref, dk_out), (dv_ref, dv_out))
        )
    ]

    def attend():
        got("ot0", "ot1", "ot2")
        halves = []
        for lh in range(2):
            rows = slice(lh * DIM, (lh + 1) * DIM)
            total = ot[0, rows] * lse[16 + lh : 17 + lh]
            for n in range(1, 4):
                total = total + pot[n - 1, rows].astype(jnp.float32) * lse[16 + 2 * n + lh : 17 + 2 * n + lh]
            halves.append(total)
        store(att_ref, jnp.concatenate(halves, axis=0).T.astype(jnp.bfloat16))

    for lh in range(2):
        sd[lh] = dqt[3, lh * DIM : (lh + 1) * DIM].astype(jnp.bfloat16)
        go("dq3%d" % lh)
    got("rB-1n0", "rB-1n1", "rB+1n0", "rB+1n1")
    chain(-2, 2, 1)
    chain(1, 6, 5)
    attend()
    leave[0].start()
    for lh in range(2):
        got("dq3%d" % lh)
        part = dqt[2, lh * DIM : (lh + 1) * DIM] + pd[lh].astype(jnp.float32)
        xd[lh] = part.astype(jnp.bfloat16)
        go("dq2%d" % lh)

    def queries_back(n, carry):
        def stage(at_step):
            return pl.when(n == at_step)

        @stage(0)
        def _():
            got("rA-11", "rA+11")
            a_send(3, 0)
            a_send(2, 2)

        @stage(2)
        def _():
            for lh in range(2):
                sd[2 + lh] = dqt[1, lh * DIM : (lh + 1) * DIM].astype(jnp.bfloat16)
            go("dq1")
            chain(-1, 3, 2)
            got("rA-10", "rA+10")
            a_send(1, 1, 0)

        p = 1 - n // 2
        lows, cats, d1, d2 = [], [], [], []
        for k in range(2):
            i = 2 * (n % 2) + k
            kl, kh = take(4 * i, 4, 0), take(4 * i, 4, 1)
            low, same = picks(4 * i, 4, p)
            lows.append(kl)
            cats.append(cat(kl, kh, low))
            d1.append(wt[i, p, 0])
            d2.append(wt[i, p, 1])
        one = tn(jnp.concatenate(lows, axis=0), jnp.concatenate(d1, axis=0))
        two = tn(jnp.concatenate(cats, axis=0), jnp.concatenate(d2, axis=0))
        dqt[p, 0:DIM] = dqt[p, 0:DIM] + two[0:DIM]
        dqt[p, high] = dqt[p, high] + (one + two[high])
        return carry

    lax.fori_loop(0, 4, queries_back, 0)

    for half, total in enumerate((a_total(0, 1, 2), b_total(0, 3, 6))):
        total = total + dg[half]
        for lh in range(2):
            rows = slice(lh * BLK + half * HALF, lh * BLK + (half + 1) * HALF)
            dk_ref[rows, :] = (total[lh] * SCALE).astype(jnp.bfloat16)
            dv_ref[rows, :] = total[2 + lh].astype(jnp.bfloat16)

    leave[2].start()
    leave[3].start()
    got("dq1", "dq20", "dq21")
    halves = []
    for lh in range(2):
        part = dqt[0, lh * DIM : (lh + 1) * DIM] + pd[2 + lh].astype(jnp.float32)
        halves.append(part + px[lh].astype(jnp.float32))
    store(dq_ref, (jnp.concatenate(halves, axis=0) * SCALE).T.astype(jnp.bfloat16))
    leave[1].start()
    for name, copy in msgs.items():
        if name not in early:
            copy.wait_send()
    for copy in leave:
        copy.wait()


def hand_out(*refs):
    sources, targets, held, sems = refs[:4], refs[4:8], refs[8:12], refs[12]
    come, leave = [], []
    for n in range(4):
        come.append(pltpu.make_async_copy(sources[n], held[n], sems.at[n]))
        leave.append(pltpu.make_async_copy(held[n], targets[n], sems.at[4 + n]))
    for copy in come:
        copy.start()
    for first, then in zip(come, leave):
        first.wait()
        then.start()
    for copy in leave:
        copy.wait()


def body(queries, keys, values, grad_out, block_pos):
    bf, f32 = jnp.bfloat16, jnp.float32
    window = (4, HALF, DIM)
    raw = (2 * BLK, HEADS * DIM)
    count = 108
    shapes = [
        jax.ShapeDtypeStruct(raw, bf),
        jax.ShapeDtypeStruct(raw, bf),
        jax.ShapeDtypeStruct((2 * BLK, DIM), bf),
        jax.ShapeDtypeStruct((2 * BLK, DIM), bf),
    ]
    outs = pl.pallas_call(
        kernel,
        out_shape=shapes,
        in_specs=[pl.BlockSpec(memory_space=pltpu.HBM)] * 5,
        out_specs=[pl.BlockSpec(memory_space=pltpu.HBM)] * 4,
        scratch_shapes=[
            pltpu.VMEM(raw, bf),
            pltpu.VMEM(raw, bf),
            pltpu.VMEM((2 * BLK, DIM), bf),
            pltpu.VMEM((2 * BLK, DIM), bf),
            pltpu.VMEM((CHUNKS, 4) + window, bf),
            pltpu.VMEM(raw, bf),
            pltpu.VMEM(raw, bf),
            pltpu.VMEM((3,) + raw, bf),
            pltpu.VMEM((3,) + raw, bf),
            pltpu.VMEM((4, ROWS, 2 * DIM), bf),
            pltpu.VMEM((4, ROWS, 2 * DIM), bf),
            pltpu.VMEM((4, 2 * DIM, ROWS), bf),
            pltpu.VMEM((4, 2 * DIM, ROWS), bf),
            pltpu.VMEM((4, 2 * DIM, ROWS), f32),
            pltpu.VMEM((4, 2 * DIM, ROWS), f32),
            pltpu.VMEM((24, ROWS), f32),
            pltpu.VMEM((8, 8, ROWS), f32),
            pltpu.VMEM((3, 24, ROWS), f32),
            pltpu.VMEM((24, ROWS), f32),
            pltpu.VMEM((STEPS, 8, ROWS), f32),
            pltpu.VMEM((STEPS, 4, 2, KEYS, ROWS), bf),
            pltpu.VMEM((3, 2 * DIM, ROWS), bf),
            pltpu.VMEM((3, 2 * DIM, ROWS), bf),
            pltpu.VMEM((4, DIM, ROWS), bf),
            pltpu.VMEM((4, DIM, ROWS), bf),
            pltpu.VMEM((2, DIM, ROWS), bf),
            pltpu.VMEM((2, DIM, ROWS), bf),
            pltpu.VMEM((CHUNKS, 4) + window, f32),
            pltpu.VMEM((CHUNKS, 4) + window, bf),
            pltpu.VMEM((CHUNKS, 4) + window, bf),
            pltpu.VMEM((3, 4) + window, bf),
            pltpu.VMEM((3,) + window, bf),
            pltpu.VMEM((3,) + window, bf),
            pltpu.VMEM((7,) + window, bf),
            pltpu.VMEM((7,) + window, bf),
            pltpu.VMEM((2,) + window, f32),
            pltpu.SMEM((4, 2 * BLK), jnp.int32),
            pltpu.SMEM((4 * CHUNKS + 4,), jnp.int32),
            pltpu.SemaphoreType.DMA((15,)),
            pltpu.SemaphoreType.DMA((count,)),
            pltpu.SemaphoreType.DMA((count,)),
        ],
        compiler_params=pltpu.CompilerParams(
            collective_id=0, has_side_effects=True, vmem_limit_bytes=54 * 1024 * 1024
        ),
        name="attention",
    )(block_pos, queries[0], keys[0], values[0], grad_out[0])
    outs = pl.pallas_call(
        hand_out,
        out_shape=shapes,
        in_specs=[pl.BlockSpec(memory_space=pltpu.HBM)] * 4,
        out_specs=[pl.BlockSpec(memory_space=pltpu.HBM)] * 4,
        scratch_shapes=[pltpu.VMEM(one.shape, bf) for one in shapes]
        + [pltpu.SemaphoreType.DMA((8,))],
        compiler_params=pltpu.CompilerParams(vmem_limit_bytes=54 * 1024 * 1024),
        name="hand_out",
    )(*outs)
    return tuple(out[None] for out in outs)


def solution(mesh):
    spec = P("inner", "outer", None)
    return jax.shard_map(
        body,
        mesh=mesh,
        in_specs=(spec, spec, spec, spec, P()),
        out_specs=(spec, spec, spec, spec),
        check_vma=False,
    )
```

```python
import jax
import jax.numpy as jnp
from jax import lax
from jax.experimental import pallas as pl
from jax.experimental.pallas import tpu as pltpu
from jax.sharding import PartitionSpec as P

MESH = pl.DeviceIdType.MESH
NEG = -1e30
BIG = 1e30
BLK = 64
HALF = 32
DIM = 128
HEADS = 8
ROWS = BLK * HEADS
CHUNKS = 16
STEPS = 4
BACK_STEPS = 8
KEYS = 16 * HALF
BACK_KEYS = 8 * HALF
SCALE = DIM**-0.5
C2 = SCALE * 1.4426950408889634

YORDER = (0, -1, 1, 2)
NEAR = (0, -1, 1, -2)
FAR = (2, -3, 3, 4)


def a_chunk(dz):
    return [(dy, dz) for dy in YORDER]


def b_chunk(dy, part):
    return [(dy, dz) for dz in part]


NAMES = (
    ("A0", a_chunk(0)),
    ("B0n", b_chunk(0, NEAR)),
    ("A-1", a_chunk(-1)),
    ("A+1", a_chunk(1)),
    ("B+1n", b_chunk(1, NEAR)),
    ("B0f", b_chunk(0, FAR)),
    ("A-2", a_chunk(-2)),
    ("A+2", a_chunk(2)),
    ("B-1n", b_chunk(-1, NEAR)),
    ("B+1f", b_chunk(1, FAR)),
    ("A-3", a_chunk(-3)),
    ("A+3", a_chunk(3)),
    ("B2f", b_chunk(2, FAR)),
    ("B-1f", b_chunk(-1, FAR)),
    ("B2n", b_chunk(2, NEAR)),
    ("A4", a_chunk(4)),
)
TABLE = [windows for _, windows in NAMES]
AT = {name: number for number, (name, _) in enumerate(NAMES)}


def nt(a, b):
    return lax.dot_general(a, b, (((1,), (0,)), ((), ())), preferred_element_type=jnp.float32)


def tn(a, b):
    return lax.dot_general(a, b, (((0,), (0,)), ((), ())), preferred_element_type=jnp.float32)


def fold(x, op):
    rows, lanes = x.shape
    return op(x.reshape(rows // 8, 8, lanes), axis=0)


def row_sum(x):
    return jnp.sum(x, axis=0, keepdims=True)


def row_max(x):
    return jnp.max(x, axis=0, keepdims=True)


def kernel(
    pos_ref,
    q_ref,
    k_ref,
    v_ref,
    g_ref,
    att_out,
    dq_out,
    dk_out,
    dv_out,
    att_ref,
    dq_ref,
    dk_ref,
    dv_ref,
    buf,
    mq,
    mg,
    pq,
    pg,
    qn,
    gn,
    qt,
    gt,
    ot,
    dqt,
    stat,
    ls,
    pstat,
    lse,
    mc,
    wt,
    mot,
    pot,
    sd,
    pd,
    xd,
    px,
    tf,
    snd,
    r1,
    r2,
    sy,
    ry,
    sz,
    rz,
    dg,
    pos,
    kt,
    lsem,
    ssem,
    rsem,
):
    outer = lax.axis_index("outer")
    inner = lax.axis_index("inner")
    yy = outer // 16
    xx = (outer // 8) % 2
    zz = outer % 8
    mate = inner + 1 - 2 * (inner % 2)

    def at(x, dy, dz):
        return (((yy + dy + 4) % 4) * 2 + x) * 8 + (zz + dz + 8) % 8

    beside = at(1 - xx, 0, 0)
    yp, ym = (at(xx, 1, 0), inner), (at(xx, -1, 0), inner)
    zp, zm = (at(xx, 0, 1), inner), (at(xx, 0, -1), inner)
    cp, xp, dp = (outer, mate), (beside, inner), (beside, mate)

    barrier = pltpu.get_barrier_semaphore()
    for dev in (yp, ym, zp, zm, cp, xp, dp):
        pl.semaphore_signal(barrier, inc=1, device_id=dev, device_id_type=MESH)

    fetch = [
        pltpu.make_async_copy(pos_ref, pos, lsem.at[0]),
        pltpu.make_async_copy(q_ref, mq, lsem.at[1]),
        pltpu.make_async_copy(g_ref, mg, lsem.at[2]),
    ]
    pieces = []
    for n, ref in enumerate((k_ref, v_ref)):
        for lh in range(2):
            for half in range(2):
                pieces.append(
                    pltpu.make_async_copy(
                        ref.at[pl.ds(lh * BLK + half * HALF, HALF)],
                        buf.at[half, 0, 2 * n + lh],
                        lsem.at[3 + len(pieces)],
                    )
                )
    for copy in pieces + fetch:
        copy.start()
    pl.semaphore_wait(barrier, 7)

    msgs = {}

    def msg(name, src, dst, dev):
        at_sem = len(msgs)
        msgs[name] = pltpu.make_async_remote_copy(
            src_ref=src,
            dst_ref=dst,
            send_sem=ssem.at[at_sem],
            recv_sem=rsem.at[at_sem],
            device_id=dev,
            device_id_type=MESH,
        )

    def go(*names):
        for name in names:
            msgs[name].start()

    def got(*names):
        for name in names:
            msgs[name].wait_recv()

    for name, src, dst in (("q", q_ref, pq), ("g", g_ref, pg)):
        msg(name + "1", src, dst.at[0], cp)
        for half in range(2):
            span = pl.ds(half * BLK, BLK)
            msg("%s2%d" % (name, half), src.at[span], dst.at[1, span], xp)
            msg("%s3%d" % (name, half), dst.at[1, span], dst.at[2, span], cp)
    msg("ay1", buf.at[0, 0], buf.at[0, 1], yp)
    msg("ay2", buf.at[0, 0], buf.at[0, 2], ym)
    msg("ay3", buf.at[0, 1], buf.at[0, 3], yp)
    for w in range(4):
        msg("azp%d" % w, buf.at[0, w], buf.at[AT["A-1"], w], zp)
        msg("azm%d" % w, buf.at[0, w], buf.at[AT["A+1"], w], zm)
        msg("byp%d" % w, buf.at[1, w], buf.at[AT["B-1n"], w], yp)
        msg("bym%d" % w, buf.at[1, w], buf.at[AT["B+1n"], w], ym)

    def block(name, source, target, first, count, dev):
        span = pl.ds(first, count)
        msg(name, buf.at[AT[source], span], buf.at[AT[target], span], dev)

    block("a7a", "A-1", "A-2", 0, 3, zp)
    block("a7b", "A-1", "A-2", 3, 1, zp)
    block("a8a", "A+1", "A+2", 0, 3, zm)
    block("a8b", "A+1", "A+2", 3, 1, zm)
    block("a11a", "A-2", "A-3", 0, 2, zp)
    block("a11b", "A-2", "A-3", 2, 2, zp)
    block("a12a", "A+2", "A+3", 2, 2, zm)
    block("a12b", "A+2", "A+3", 0, 2, zm)
    block("a15p", "A-3", "A4", 0, 2, zp)
    block("a15m", "A+3", "A4", 2, 2, zm)
    far = AT["B0f"]
    msg("bz1", buf.at[1, 0], buf.at[1, 1], zp)
    msg("bz2", buf.at[1, 0], buf.at[1, 2], zm)
    msg("bz3", buf.at[1, 1], buf.at[1, 3], zp)
    msg("bz4", buf.at[1, 2], buf.at[far, 0], zm)
    msg("bz5", buf.at[1, 3], buf.at[far, 1], zp)
    msg("bz6", buf.at[far, 0], buf.at[far, 2], zm)
    msg("bz7", buf.at[far, 1], buf.at[far, 3], zp)
    block("b9a", "B0f", "B-1f", 0, 3, yp)
    block("b9b", "B0f", "B-1f", 3, 1, yp)
    block("b10a", "B0f", "B+1f", 0, 3, ym)
    block("b10b", "B0f", "B+1f", 3, 1, ym)
    block("b13", "B-1n", "B2n", 0, 4, yp)
    block("b14a", "B+1f", "B2f", 0, 3, ym)
    block("b14b", "B+1f", "B2f", 3, 1, ym)
    for n, dev in enumerate((cp, xp, dp)):
        msg("stat%d" % n, stat, pstat.at[n], dev)
    for n, dev in enumerate((cp, xp, dp)):
        msg("ot%d" % n, mot.at[n], pot.at[n], dev)
    for lh in range(2):
        msg("dq3%d" % lh, sd.at[lh], pd.at[lh], cp)
        msg("dq2%d" % lh, xd.at[lh], px.at[lh], xp)
    msg("dq1", sd.at[pl.ds(2, 2)], pd.at[pl.ds(2, 2)], cp)
    def back(name, source, target, first, count, dev, into=None):
        span = pl.ds(first, count)
        into = r1.at[AT[target], span] if into is None else r2.at[into, span]
        msg(name, snd.at[AT[source], span], into, dev)

    back("rA4m", "A4", "A-3", 0, 2, zm)
    back("rA4p", "A4", "A+3", 2, 2, zp)
    for half in range(2):
        span = 2 * half, 2

        def both(source, target, dev, into=None):
            back("r%s%d" % (source, half), source, target, *span, dev, into)

        both("A-3", "A-2", zm)
        both("A+3", "A+2", zp)
        both("A-2", "A-1", zm)
        both("A+2", "A+1", zp)
        both("A-1", "A0", zm)
        both("A+1", "A0", zp, 0)
        both("B2n", "B-1n", ym)
        both("B2f", "B+1f", yp)
        both("B-1n", "B0n", ym)
        both("B-1f", "B0f", ym)
        both("B+1n", "B0n", yp, 1)
        both("B+1f", "B0f", yp, 2)
    for n, dev in enumerate((ym, ym, yp)):
        msg("ry%d" % n, sy.at[n], ry.at[n], dev)
    for n, dev in enumerate((zm, zm, zm, zm, zp, zp, zp)):
        msg("rz%d" % n, sz.at[n], rz.at[n], dev)

    go("q20", "q21", "q1")
    for copy in pieces:
        copy.wait()
    go("ay1", "ay2", "bz1", "bz2", "azp0", "azm0", "byp0", "bym0", "g1")
    fetch[0].wait()

    for p, (row, column) in enumerate(
        ((inner, outer), (mate, outer), (inner, beside), (mate, beside))
    ):
        kt[4 * CHUNKS + p] = pos[row, 2 * column]
    for c in range(CHUNKS):
        for w in range(4):
            dy, dz = TABLE[c][w]
            kt[4 * c + w] = pos[inner, 2 * at(xx, dy, dz)]

    def spread(p, src, rows, cols):
        for h in range(HEADS):
            lanes = slice(h * DIM, (h + 1) * DIM)
            rows[p, h * BLK : (h + 1) * BLK, 0:DIM] = src[0:BLK, lanes]
            rows[p, h * BLK : (h + 1) * BLK, DIM : 2 * DIM] = src[BLK : 2 * BLK, lanes]
        cols[p] = rows[p].T

    fetch[1].wait()
    spread(0, mq, qn, qt)
    got("ay1", "ay2", "bz1", "bz2")
    go("ay3", "bz3", "bz4", "azp1", "azm1", "azp2", "azm2", "byp1", "bym1", "byp2", "bym2")
    got("q1")
    spread(1, pq.at[0], qn, qt)

    tok_k = lax.broadcasted_iota(jnp.int32, (BLK, ROWS), 0)
    tok_q = lax.broadcasted_iota(jnp.int32, (BLK, ROWS), 1) % BLK
    diag = tok_k <= tok_q

    def own(kind):
        return jnp.concatenate([buf[0, 0, kind], buf[1, 0, kind]], axis=0)

    for lh in range(2):
        s = jnp.where(diag, nt(own(lh), qt[0, lh * DIM : (lh + 1) * DIM]), NEG)
        m = row_max(s)
        p = jnp.exp2((s - m) * C2)
        stat[lh : lh + 1] = m
        ls[lh] = fold(p, jnp.sum)
        ot[0, lh * DIM : (lh + 1) * DIM] = tn(own(2 + lh), p.astype(jnp.bfloat16))
    stat[2:8] = jnp.full((6, ROWS), NEG, jnp.float32)
    ls[2:8] = jnp.zeros((6, 8, ROWS), jnp.float32)

    got("ay3", "bz3", "bz4")
    go("azp3", "azm3", "bz5", "bz6", "byp3", "bym3")
    for w in range(3):
        got("azp%d" % w, "azm%d" % w)
    go("a7a", "a8a")
    for p in range(1, 4):
        ot[p] = jnp.zeros((2 * DIM, ROWS), jnp.float32)
    for name in ("B+1n", "B2n", "B-1f", "B2f", "A4"):
        r1[AT[name]] = jnp.zeros((4, 4, HALF, DIM), jnp.bfloat16)
    r1[AT["A-3"], 2:4] = jnp.zeros((2, 4, HALF, DIM), jnp.bfloat16)
    r1[AT["A+3"], 0:2] = jnp.zeros((2, 4, HALF, DIM), jnp.bfloat16)

    got("azp3", "azm3", "bz5", "bz6")
    go("a7b", "a8b", "bz7", "b9a", "b10a")
    got("byp0", "byp1", "byp2", "byp3")
    go("b13")
    got("q20")
    go("q30")
    fetch[2].wait()
    spread(0, mg, gn, gt)
    def take(first, count, kind):
        return buf[pl.ds(first, count), :, kind].reshape(count * 4 * HALF, DIM)

    def picks(first, count, p):
        number = [kt[4 * first + w] for w in range(4 * count)]
        mine = kt[4 * CHUNKS + p]
        return [n < mine for n in number], [n == mine for n in number]

    def windows(x):
        return [x[w * HALF : (w + 1) * HALF] for w in range(x.shape[0] // HALF)]

    def cat(low, high, chosen):
        zero = jnp.zeros((HALF, DIM), jnp.bfloat16)
        rows = []
        for a, b, pick in zip(windows(low), windows(high), chosen):
            rows.append(
                jnp.concatenate([lax.select(pick, a, zero), lax.select(pick, zero, b)], axis=1)
            )
        return jnp.concatenate(rows, axis=0)

    neg_rows = jnp.full((8, ROWS), NEG, jnp.float32)
    big_row = jnp.full((1, ROWS), BIG, jnp.float32)
    high = slice(DIM, 2 * DIM)

    def row(ref, r):
        return ref[pl.ds(r, 1)]

    def arrive(n):
        def do(at_step, *steps):
            @pl.when(n == at_step)
            def _():
                for step, names in steps:
                    step(*names)

        @pl.when(n == 1)
        def _():
            got("q21")
            go("q31", "g20", "g21")
            spread(2, pq.at[1], qn, qt)
            got("q30", "q31")
            spread(3, pq.at[2], qn, qt)
            got("a7a", "a8a", "bz7")
            go("b9b", "b10b")

        do(2, (got, ["a7b", "a8b"]), (go, ["a11a", "a12a", "a11b", "a12b"]))
        do(2, (got, ["bym%d" % w for w in range(4)] + ["b10a"]), (go, ["b14a"]))
        do(3, (got, ["b10b"]), (go, ["b14b"]))
        do(4, (got, ["a11a", "a12a"]), (go, ["a15p", "a15m"]))
        do(4, (got, ["g20", "g21"]), (go, ["g30", "g31"]), (got, ["a11b", "a12b"]))
        do(6, (got, ["b14a", "b14b", "b9a", "b9b", "b13", "a15p", "a15m"]))

        @pl.when(n == 5)
        def _():
            got("g1", "g30", "g31")
            for p in range(1, 4):
                spread(p, pg.at[p - 1], gn, gt)

    def forward(n, carry):
        i, pair = n // 2, n % 2
        arrive(n)
        kl, kh, vl, vh = [take(4 * i, 4, kind) for kind in range(4)]
        parts = []
        for p in (2 * pair, 2 * pair + 1):
            low, same = picks(4 * i, 4, p)
            kcat, vcat = cat(kl, kh, low), cat(vl, vh, low)
            olds = [row(stat, 2 * p + lh) for lh in range(2)]
            parts.append((p, low, same, kcat, vcat, olds))

        def scores(part):
            p, _, _, kcat, _, _ = part
            return nt(kl, qt[p, high]), windows(nt(kcat, qt[p]))

        def weigh(part, s1, s2):
            p, low, same, _, vcat, (ml, mh) = part
            rl, rh = 2 * p, 2 * p + 1
            tops_l, tops_h = neg_rows, fold(s1, jnp.max)
            for w in range(16):
                top = fold(s2[w], jnp.max)
                tops_l = jnp.maximum(tops_l, lax.select(low[w], top, neg_rows))
                tops_h = jnp.maximum(tops_h, lax.select(low[w] | same[w], neg_rows, top))
            nl, nh = jnp.maximum(ml, row_max(tops_l)), jnp.maximum(mh, row_max(tops_h))
            fl, fh = jnp.exp2((ml - nl) * C2), jnp.exp2((mh - nh) * C2)
            p1 = jnp.exp2((s1 - nh) * C2)
            tl, th = ls[rl] * fl, ls[rh] * fh + fold(p1, jnp.sum)
            pieces = []
            for w in range(16):
                ref = lax.select(same[w], big_row, lax.select(low[w], nl, nh))
                piece = jnp.exp2((s2[w] - ref) * C2)
                total = fold(piece, jnp.sum)
                zero = jnp.zeros_like(total)
                tl = tl + lax.select(low[w], total, zero)
                th = th + lax.select(low[w], zero, total)
                pieces.append(piece.astype(jnp.bfloat16))
            ls[rl], ls[rh] = tl, th
            stat[pl.ds(rl, 1)], stat[pl.ds(rh, 1)] = nl, nh
            mc[i, pl.ds(rl, 1)], mc[i, pl.ds(rh, 1)] = nl, nh
            w1, w2 = p1.astype(jnp.bfloat16), jnp.concatenate(pieces, axis=0)
            wt[i, p, 0], wt[i, p, 1] = w1, w2
            return p, fl, fh, w1, w2, vcat

        def update(p, fl, fh, w1, w2, vcat):
            o1, o2 = tn(vl, w1), tn(vcat, w2)
            ot[p, 0:DIM] = ot[p, 0:DIM] * fl + o2[0:DIM]
            ot[p, high] = ot[p, high] * fh + (o1 + o2[high])

        now, late = scores(parts[0]), None
        for k in range(2):
            later = scores(parts[k + 1]) if k < 1 else None
            done = weigh(parts[k], *now)
            if late is not None:
                update(*late)
            now, late = later, done
        update(*late)
        return carry

    lax.fori_loop(0, 2 * STEPS, forward, 0)

    for p in range(4):
        for lh in range(2):
            r = 2 * p + lh
            stat[8 + r : 9 + r] = row_sum(ls[r])
            rows = slice(lh * DIM, (lh + 1) * DIM)
            stat[16 + r : 17 + r] = row_sum(ot[p, rows] * gt[p, rows].astype(jnp.float32))
    go("stat2", "stat1", "stat0")
    for n in range(3):
        mot[n] = ot[n + 1].astype(jnp.bfloat16)
    go("ot0", "ot1", "ot2")

    dqt[1:4] = jnp.zeros((3, 2 * DIM, ROWS), jnp.float32)
    early = [name for name in msgs if name[0] in "qgab"]
    for name in early:
        msgs[name].wait_send()
    got("stat0", "stat1", "stat2")
    for p in range(4):
        for lh in range(2):
            r = 2 * p + lh
            held = [(stat, r)] + [(pstat.at[n - 1], 2 * (p ^ n) + lh) for n in range(1, 4)]
            tops = [row(ref, at_row) for ref, at_row in held]
            top = jnp.maximum(jnp.maximum(tops[0], tops[1]), jnp.maximum(tops[2], tops[3]))
            factors = [jnp.exp2((m - top) * C2) for m in tops]
            total, delta = 0.0, 0.0
            for factor, (ref, at_row) in zip(factors, held):
                total = total + factor * row(ref, 8 + at_row)
                delta = delta + factor * row(ref, 16 + at_row)
            lse[r : r + 1] = top + jnp.log(total) * (1.0 / SCALE)
            lse[8 + r : 9 + r] = delta / total
            if p == 0:
                for n in range(4):
                    lse[16 + 2 * n + lh : 17 + 2 * n + lh] = factors[n] / total

    for lh in range(2):
        rows = slice(lh * DIM, (lh + 1) * DIM)
        s = jnp.where(diag, nt(own(lh), qt[0, rows]), NEG)
        p = jnp.exp2((s - lse[lh : lh + 1]) * C2)
        ds = (p * (nt(own(2 + lh), gt[0, rows]) - lse[8 + lh : 9 + lh])).astype(jnp.bfloat16)
        dk = nt(ds, qn[0, :, rows])
        dv = nt(p.astype(jnp.bfloat16), gn[0, :, rows])
        for half in range(2):
            dg[half, lh] = dk[half * HALF : (half + 1) * HALF]
            dg[half, 2 + lh] = dv[half * HALF : (half + 1) * HALF]
        dqt[0, rows] = tn(own(lh), ds)

    def total_of(c, w, slot, ref, *arrived):
        total = tf[c, w] + r1[c, w].astype(jnp.float32) + r2[slot, w].astype(jnp.float32)
        for n in arrived:
            total = total + ref[n].astype(jnp.float32)
        return total

    def b_total(dz, *arrived):
        got(*["rz%d" % n for n in arrived])
        for slot, c in ((1, 1), (2, far)):
            for w in range(4):
                if TABLE[c][w][1] == dz:
                    return total_of(c, w, slot, rz, *arrived)

    def chain(dz, leaving, *arrived):
        sz[leaving] = b_total(dz, *arrived).astype(jnp.bfloat16)
        go("rz%d" % leaving)

    def a_total(w, *arrived):
        got(*["ry%d" % n for n in arrived])
        return total_of(0, w, 0, ry, *arrived)

    def a_send(w, leaving, *arrived):
        sy[leaving] = a_total(w, *arrived).astype(jnp.bfloat16)
        go("ry%d" % leaving)

    def sweep(i, group, more):
        step, rows = i // 2, pl.ds((i % 2) * BACK_KEYS, BACK_KEYS)
        kl, kh, vl, vh = [take(2 * i, 2, kind) for kind in range(4)]
        parts = []
        for p in group:
            low, same = picks(2 * i, 2, p)
            parts.append((p, low, cat(vl, vh, low)))

        def dots(part):
            p, low, vcat = part
            el, eh = lse[8 + 2 * p : 9 + 2 * p], lse[9 + 2 * p : 10 + 2 * p]
            first = (nt(vl, gt[p, high]) - eh).astype(jnp.bfloat16)
            second = [
                (dot - lax.select(pick, el, eh)).astype(jnp.bfloat16)
                for pick, dot in zip(low, windows(nt(vcat, gt[p])))
            ]
            return first, second

        def work(part, first, second):
            p, low, _ = part
            rl, rh = 2 * p, 2 * p + 1
            fl = jnp.exp2((mc[step, rl : rl + 1] - lse[rl : rl + 1]) * C2)
            fh = jnp.exp2((mc[step, rh : rh + 1] - lse[rh : rh + 1]) * C2)
            p1 = wt[step, p, 0, rows] * fh.astype(jnp.bfloat16)
            ds1 = p1 * first
            ps, ds = [], []
            for weight, dot, pick in zip(windows(wt[step, p, 1, rows]), second, low):
                piece = weight * lax.select(pick, fl, fh).astype(jnp.bfloat16)
                ps.append(piece)
                ds.append(piece * dot)
            p2, ds2 = jnp.concatenate(ps, axis=0), jnp.concatenate(ds, axis=0)
            if p < 2:
                wt[step, p, 0, rows], wt[step, p, 1, rows] = ds1, ds2
            if p >= 2:
                one, two = tn(kl, ds1), tn(cat(kl, kh, low), ds2)
                dqt[p, 0:DIM] = dqt[p, 0:DIM] + two[0:DIM]
                dqt[p, high] = dqt[p, high] + (one + two[high])
            return p, low, p1, ds1, p2, ds2

        def products(sums, p, low, p1, ds1, p2, ds2):
            new = []
            for one, two in (
                (nt(ds1, qn[p, :, high]), nt(ds2, qn[p])),
                (nt(p1, gn[p, :, high]), nt(p2, gn[p])),
            ):
                zero = jnp.zeros((HALF, DIM), jnp.float32)
                lows, highs = [], []
                for w in range(8):
                    here = slice(w * HALF, (w + 1) * HALF)
                    lows.append(one[here] + lax.select(low[w], two[here, 0:DIM], zero))
                    highs.append(lax.select(low[w], zero, two[here, high]))
                new += [lows, highs]
            if sums is None:
                return new
            return [[a + b for a, b in zip(x, y)] for x, y in zip(sums, new)]

        sums, late = None, None
        now = dots(parts[0])
        for k in range(len(parts)):
            later = dots(parts[k + 1]) if k < len(parts) - 1 else None
            done = work(parts[k], *now)
            if late is not None:
                sums = products(sums, *late)
            now, late = later, done
        sums = products(sums, *late)
        for kind in range(4):
            for w in range(8):
                c = 2 * i + w // 4
                term = sums[kind][w]
                tf[c, w % 4, kind] = tf[c, w % 4, kind] + term if more else term

    def backward(n, carry):
        i = BACK_STEPS - 1 - n
        sweep(i, range(4), False)

        def finish(at_step, *chunks):
            @pl.when(i == at_step)
            def _():
                for name, waits in chunks:
                    for half in (1, 0) if name in ("A-1", "A+1") else (0, 1):
                        c, span = AT[name], pl.ds(2 * half, 2)
                        if waits[half]:
                            got(waits[half])
                        total = tf[c, span] + r1[c, span].astype(jnp.float32)
                        snd[c, span] = total.astype(jnp.bfloat16)
                        go(("rA4m", "rA4p")[half] if name == "A4" else "r%s%d" % (name, half))

        def upstream(name):
            return ["r%s%d" % (name, half) for half in range(2)]

        none = [None, None]
        finish(7, ("A4", none), ("B2n", none))
        finish(6, ("B2f", none), ("B-1f", none))
        finish(5, ("A-3", ["rA4m", None]), ("A+3", [None, "rA4p"]))
        finish(4, ("B-1n", upstream("B2n")), ("B+1f", upstream("B2f")))
        finish(3, ("A-2", upstream("A-3")), ("A+2", upstream("A+3")))
        finish(2, ("B+1n", none))
        finish(1, ("A-1", upstream("A-2")), ("A+1", upstream("A+2")))

        @pl.when(i == 2)
        def _():
            got("rB-1f0", "rB-1f1", "rB+1f0", "rB+1f1")
            chain(4, 0)
            chain(3, 4)

        @pl.when(i == 1)
        def _():
            chain(-3, 1, 0)
            chain(2, 5, 4)

        return carry

    lax.fori_loop(0, BACK_STEPS - 1, backward, 0)

    sweep(0, (2, 3), False)
    for lh in range(2):
        sd[lh] = dqt[3, lh * DIM : (lh + 1) * DIM].astype(jnp.bfloat16)
        go("dq3%d" % lh)
    sweep(0, (0, 1), True)
    for lh in range(2):
        got("dq3%d" % lh)
        part = dqt[2, lh * DIM : (lh + 1) * DIM] + pd[lh].astype(jnp.float32)
        xd[lh] = part.astype(jnp.bfloat16)
        go("dq2%d" % lh)

    def store(ref, rows):
        for h in range(HEADS):
            lanes = slice(h * DIM, (h + 1) * DIM)
            ref[0:BLK, lanes] = rows[h * BLK : (h + 1) * BLK, 0:DIM]
            ref[BLK : 2 * BLK, lanes] = rows[h * BLK : (h + 1) * BLK, DIM : 2 * DIM]

    leave = [
        pltpu.make_async_copy(src, dst, lsem.at[11 + n])
        for n, (src, dst) in enumerate(
            ((att_ref, att_out), (dq_ref, dq_out), (dk_ref, dk_out), (dv_ref, dv_out))
        )
    ]

    def attend():
        got("ot0", "ot1", "ot2")
        halves = []
        for lh in range(2):
            rows = slice(lh * DIM, (lh + 1) * DIM)
            total = ot[0, rows] * lse[16 + lh : 17 + lh]
            for n in range(1, 4):
                total = total + pot[n - 1, rows].astype(jnp.float32) * lse[16 + 2 * n + lh : 17 + 2 * n + lh]
            halves.append(total)
        store(att_ref, jnp.concatenate(halves, axis=0).T.astype(jnp.bfloat16))

    got("rB-1n0", "rB-1n1", "rB+1n0", "rB+1n1")
    chain(-2, 2, 1)
    chain(1, 6, 5)
    attend()
    leave[0].start()

    def queries_back(n, carry):
        def stage(at_step):
            return pl.when(n == at_step)

        @stage(0)
        def _():
            got("rA-11", "rA+11")
            a_send(3, 0)
            a_send(2, 2)

        @stage(2)
        def _():
            for lh in range(2):
                sd[2 + lh] = dqt[1, lh * DIM : (lh + 1) * DIM].astype(jnp.bfloat16)
            go("dq1")
            chain(-1, 3, 2)
            got("rA-10", "rA+10")
            a_send(1, 1, 0)

        p = 1 - n // 2
        lows, cats, d1, d2 = [], [], [], []
        for k in range(2):
            i = 2 * (n % 2) + k
            kl, kh = take(4 * i, 4, 0), take(4 * i, 4, 1)
            low, same = picks(4 * i, 4, p)
            lows.append(kl)
            cats.append(cat(kl, kh, low))
            d1.append(wt[i, p, 0])
            d2.append(wt[i, p, 1])
        one = tn(jnp.concatenate(lows, axis=0), jnp.concatenate(d1, axis=0))
        two = tn(jnp.concatenate(cats, axis=0), jnp.concatenate(d2, axis=0))
        dqt[p, 0:DIM] = dqt[p, 0:DIM] + two[0:DIM]
        dqt[p, high] = dqt[p, high] + (one + two[high])
        return carry

    lax.fori_loop(0, 4, queries_back, 0)

    for half, total in enumerate((a_total(0, 1, 2), b_total(0, 3, 6))):
        total = total + dg[half]
        for lh in range(2):
            rows = slice(lh * BLK + half * HALF, lh * BLK + (half + 1) * HALF)
            dk_ref[rows, :] = (total[lh] * SCALE).astype(jnp.bfloat16)
            dv_ref[rows, :] = total[2 + lh].astype(jnp.bfloat16)

    leave[2].start()
    leave[3].start()
    got("dq1", "dq20", "dq21")
    halves = []
    for lh in range(2):
        part = dqt[0, lh * DIM : (lh + 1) * DIM] + pd[2 + lh].astype(jnp.float32)
        halves.append(part + px[lh].astype(jnp.float32))
    store(dq_ref, (jnp.concatenate(halves, axis=0) * SCALE).T.astype(jnp.bfloat16))
    leave[1].start()
    for name, copy in msgs.items():
        if name not in early:
            copy.wait_send()
    for copy in leave:
        copy.wait()


def hand_out(*refs):
    sources, targets, held, sems = refs[:4], refs[4:8], refs[8:12], refs[12]
    come, leave = [], []
    for n in range(4):
        come.append(pltpu.make_async_copy(sources[n], held[n], sems.at[n]))
        leave.append(pltpu.make_async_copy(held[n], targets[n], sems.at[4 + n]))
    for copy in come:
        copy.start()
    for first, then in zip(come, leave):
        first.wait()
        then.start()
    for copy in leave:
        copy.wait()


def body(queries, keys, values, grad_out, block_pos):
    bf, f32 = jnp.bfloat16, jnp.float32
    window = (4, HALF, DIM)
    raw = (2 * BLK, HEADS * DIM)
    count = 108
    shapes = [
        jax.ShapeDtypeStruct(raw, bf),
        jax.ShapeDtypeStruct(raw, bf),
        jax.ShapeDtypeStruct((2 * BLK, DIM), bf),
        jax.ShapeDtypeStruct((2 * BLK, DIM), bf),
    ]
    outs = pl.pallas_call(
        kernel,
        out_shape=shapes,
        in_specs=[pl.BlockSpec(memory_space=pltpu.HBM)] * 5,
        out_specs=[pl.BlockSpec(memory_space=pltpu.HBM)] * 4,
        scratch_shapes=[
            pltpu.VMEM(raw, bf),
            pltpu.VMEM(raw, bf),
            pltpu.VMEM((2 * BLK, DIM), bf),
            pltpu.VMEM((2 * BLK, DIM), bf),
            pltpu.VMEM((CHUNKS, 4) + window, bf),
            pltpu.VMEM(raw, bf),
            pltpu.VMEM(raw, bf),
            pltpu.VMEM((3,) + raw, bf),
            pltpu.VMEM((3,) + raw, bf),
            pltpu.VMEM((4, ROWS, 2 * DIM), bf),
            pltpu.VMEM((4, ROWS, 2 * DIM), bf),
            pltpu.VMEM((4, 2 * DIM, ROWS), bf),
            pltpu.VMEM((4, 2 * DIM, ROWS), bf),
            pltpu.VMEM((4, 2 * DIM, ROWS), f32),
            pltpu.VMEM((4, 2 * DIM, ROWS), f32),
            pltpu.VMEM((24, ROWS), f32),
            pltpu.VMEM((8, 8, ROWS), f32),
            pltpu.VMEM((3, 24, ROWS), f32),
            pltpu.VMEM((24, ROWS), f32),
            pltpu.VMEM((STEPS, 8, ROWS), f32),
            pltpu.VMEM((STEPS, 4, 2, KEYS, ROWS), bf),
            pltpu.VMEM((3, 2 * DIM, ROWS), bf),
            pltpu.VMEM((3, 2 * DIM, ROWS), bf),
            pltpu.VMEM((4, DIM, ROWS), bf),
            pltpu.VMEM((4, DIM, ROWS), bf),
            pltpu.VMEM((2, DIM, ROWS), bf),
            pltpu.VMEM((2, DIM, ROWS), bf),
            pltpu.VMEM((CHUNKS, 4) + window, f32),
            pltpu.VMEM((CHUNKS, 4) + window, bf),
            pltpu.VMEM((CHUNKS, 4) + window, bf),
            pltpu.VMEM((3, 4) + window, bf),
            pltpu.VMEM((3,) + window, bf),
            pltpu.VMEM((3,) + window, bf),
            pltpu.VMEM((7,) + window, bf),
            pltpu.VMEM((7,) + window, bf),
            pltpu.VMEM((2,) + window, f32),
            pltpu.SMEM((4, 2 * BLK), jnp.int32),
            pltpu.SMEM((4 * CHUNKS + 4,), jnp.int32),
            pltpu.SemaphoreType.DMA((15,)),
            pltpu.SemaphoreType.DMA((count,)),
            pltpu.SemaphoreType.DMA((count,)),
        ],
        compiler_params=pltpu.CompilerParams(
            collective_id=0, has_side_effects=True, vmem_limit_bytes=54 * 1024 * 1024
        ),
        name="attention",
    )(block_pos, queries[0], keys[0], values[0], grad_out[0])
    outs = pl.pallas_call(
        hand_out,
        out_shape=shapes,
        in_specs=[pl.BlockSpec(memory_space=pltpu.HBM)] * 4,
        out_specs=[pl.BlockSpec(memory_space=pltpu.HBM)] * 4,
        scratch_shapes=[pltpu.VMEM(one.shape, bf) for one in shapes]
        + [pltpu.SemaphoreType.DMA((8,))],
        compiler_params=pltpu.CompilerParams(vmem_limit_bytes=54 * 1024 * 1024),
        name="hand_out",
    )(*outs)
    return tuple(out[None] for out in outs)


def solution(mesh):
    spec = P("inner", "outer", None)
    return jax.shard_map(
        body,
        mesh=mesh,
        in_specs=(spec, spec, spec, spec, P()),
        out_specs=(spec, spec, spec, spec),
        check_vma=False,
    )
```
